32 devices in a mesh: dp: 4 (over y, x), seq: 8 (over z, core).
Axes of the slice: x: 2, y: 2, z: 4, core: 2. Of those that a mesh axis runs over, the one named last changes fastest.
Arguments:
- layer_input: bfloat16 [8192, 2048], P(('dp', 'seq')), may hold values from -6 to 6
- attn_gain: bfloat16 [2048], P(('dp', 'seq')), may hold values from 0.5 to 1.5
- w_query: bfloat16 [2048, 4096], P('dp', 'seq'), may hold values from -0.125 to 0.125
- key_matrix: bfloat16 [2048, 512], P(('dp', 'seq')), may hold values from -0.125 to 0.125
- value_matrix: bfloat16 [2048, 512], P(('dp', 'seq')), may hold values from -0.125 to 0.125
- query_gain: bfloat16 [128], replicated, may hold values from 0.5 to 1.5
- key_gain: bfloat16 [128], replicated, may hold values from 0.5 to 1.5
- w_out: bfloat16 [4096, 2048], P(('dp', 'seq')), may hold values from -1.5 to 1.5
- moe_gain: bfloat16 [2048], P(('dp', 'seq')), may hold values from 0.5 to 1.5
- router: bfloat16 [2048, 32], P(('dp', 'seq')), may hold values from -0.06591797 to 0.06591797
- expert_gate: bfloat16 [32, 2048, 768], P(('dp', 'seq')), may hold values from -0.125 to 0.125
- expert_up: bfloat16 [32, 2048, 768], P(('dp', 'seq')), may hold values from -0.125 to 0.125
- expert_down: bfloat16 [32, 768, 2048], P(('dp', 'seq')), may hold values from -0.625 to 0.625
- expert_ids: int32 [8192, 8], P(('dp', 'seq')), may hold values from 0 to 31, all different within a row
- cont_segment: int32 [4, 1024], P('dp'), may hold values from 0 to 3, never falling along the last dimension, each value on 1 to 512 neighbouring positions
- out_grad: bfloat16 [8192, 2048], P(('dp', 'seq')), may hold values from -6 to 6
Outputs:
- layer_output: bfloat16 [8192, 2048], P(('dp', 'seq'))
- x_grad: float32 [8192, 2048], P(('dp', 'seq'))
- attn_gain_grad: float32 [2048], P(('dp', 'seq'))
- w_query_grad: float32 [2048, 4096], P('dp', 'seq')
- w_key_grad: float32 [2048, 512], P(('dp', 'seq'))
- w_value_grad: float32 [2048, 512], P(('dp', 'seq'))
- query_gain_grad: float32 [128], replicated
- key_gain_grad: float32 [128], replicated
- w_out_grad: float32 [4096, 2048], P(('dp', 'seq'))
- moe_gain_grad: float32 [2048], P(('dp', 'seq'))
- router_grad: float32 [2048, 32], P(('dp', 'seq'))
- expert_gate_grad: float32 [32, 2048, 768], P(('dp', 'seq'))
- expert_up_grad: float32 [32, 2048, 768], P(('dp', 'seq'))
- expert_down_grad: float32 [32, 768, 2048], P(('dp', 'seq'))
The draws below stay inside these ranges and needn't reach their ends.
Inputs may be any that keep to these rules, and one draw needn't show every extreme that they name: `expert_ids`: each token names 8 different experts. `cont_segment`: continuation numbers never fall along a group; each continuation holds 1 to 512 tokens and one holds exactly that many.
All inputs are finite; a program needn't handle non-finite values.
Results may differ from the reference program's by a relative error of at most 0.022.
Values may be sent and summed in bfloat16 or wider, within the bound.
No kernel may reach another device: no remote copies, remote signals or barrier semaphores. Data moves between devices by JAX's collectives and lax.ppermute only.
A program may use at most 320 MiB of HBM per device.

```python
import math
import jax
import jax.numpy as jnp
import numpy as np
from jax import lax

MODEL_WIDTH = 2048
HQ = 32
KEY_VALUE_HEADS = 4
HEAD_SIZE = 128
FF = 768
TOP = 8
EXPERTS = 32
PROMPT = 1024
CONT = 256
NCONT = 4
QBLK = 512
GROUPS = 4
CTOK = 1024
GROUP_TOK = 2048
TOKENS = 8192
TOK_DEV = 256
CAP = 64
N_SEQ = 8


def shard_levels(rng, dims, cuts, smallest, high):
    def one(position, parts):
        heights = jax.random.uniform(jax.random.fold_in(jax.random.fold_in(rng, 6), position), (parts,), jnp.float32, smallest / len(cuts), high / len(cuts))
        return jnp.repeat(jnp.exp(heights), dims[position] // parts).reshape((-1,) + (1,) * (len(dims) - position - 1))

    level = one(*cuts[0])
    for cut in cuts[1:]:
        level = level * one(*cut)
    return level


def different_ones(own_key, rows, count, top, lift):
    order = jax.random.permutation(jax.random.fold_in(own_key, 1), count)
    favour = order
    for power in range(3):
        favour = favour * favour // count
    favour = favour * lift // count
    chance = jax.random.randint(jax.random.fold_in(own_key, 2), (rows, count), 0, 4096) + favour
    fixed_rows = jax.random.permutation(jax.random.fold_in(own_key, 3), rows)[jnp.arange(count) % rows]
    chance = jnp.where(jnp.arange(rows)[:, None] == fixed_rows[None, :], 1 << 14, chance)
    priority = chance * count + jnp.arange(count)
    return lax.top_k(priority.astype(jnp.int32), top)[1].astype(jnp.int32)


def split_up(number_of, total, limit, slope):
    weights = [(1 << 20) // math.isqrt(rank ** slope) + 1 for rank in range(2, number_of + 1)]
    spare, holding = total - limit - (number_of - 1), [1] * (number_of - 1)
    while spare > 0:
        free = [i for i in range(number_of - 1) if holding[i] < limit]
        whole, budget = sum([weights[i] for i in free]), spare
        for i in free:
            more = min(limit - holding[i], max(1, budget * weights[i] // whole), spare)
            holding[i] = holding[i] + more
            spare = spare - more
    return np.array([limit] + holding)


def uneven_parts(rng, count, total, most, slope):
    if count == 2:
        one = jax.random.randint(rng, (), max(1, total - most), min(most, total - 1) + 1)
        return jnp.stack([one, total - one])
    tallies = jnp.asarray(split_up(count, total, most, slope), jnp.int32)
    pairs = (count - 1) // 2
    donor, sink = tallies[1:1 + 2 * pairs:2], tallies[2:2 + 2 * pairs:2]
    margin = jnp.minimum(donor - 1, most - sink)
    passed = jax.random.randint(jax.random.fold_in(rng, 1), (pairs,), 0, 1 << 20) % (margin + 1)
    tallies = tallies.at[1:1 + 2 * pairs:2].set(donor - passed).at[2:2 + 2 * pairs:2].set(sink + passed)
    return tallies[jax.random.permutation(jax.random.fold_in(rng, 2), count)]


def centred(own_key, dims, spread, reach, cuts=(), kind=jnp.bfloat16):
    entries = jax.random.normal(own_key, dims, jnp.float32) * spread
    if len(cuts) > 0:
        entries = shard_levels(own_key, dims, cuts, -0.22, 0.18) * entries
    return jnp.clip(entries, min=-reach, max=reach).astype(kind)


def setup_inputs(seed: int = 0) -> dict:
    key_list = jax.random.split(jax.random.key(seed), 17)
    return {
        "layer_input": centred(key_list[0], (TOKENS, MODEL_WIDTH), 1.0, 6.0, ((0, 32),)),
        "attn_gain": jnp.clip(1.0 + 0.1 * jax.random.normal(key_list[1], (MODEL_WIDTH,), jnp.float32), 0.5, 1.5).astype(jnp.bfloat16),
        "w_query": centred(key_list[2], (MODEL_WIDTH, HQ * HEAD_SIZE), MODEL_WIDTH ** -0.5, 0.125, ((0, 4), (1, 8))),
        "key_matrix": centred(key_list[3], (MODEL_WIDTH, KEY_VALUE_HEADS * HEAD_SIZE), MODEL_WIDTH ** -0.5, 0.125, ((0, 32),)),
        "value_matrix": centred(key_list[4], (MODEL_WIDTH, KEY_VALUE_HEADS * HEAD_SIZE), MODEL_WIDTH ** -0.5, 0.125, ((0, 32),)),
        "query_gain": jnp.clip(1.0 + 0.1 * jax.random.normal(key_list[5], (HEAD_SIZE,), jnp.float32), 0.5, 1.5).astype(jnp.bfloat16),
        "key_gain": jnp.clip(1.0 + 0.1 * jax.random.normal(key_list[6], (HEAD_SIZE,), jnp.float32), 0.5, 1.5).astype(jnp.bfloat16),
        "w_out": centred(key_list[7], (HQ * HEAD_SIZE, MODEL_WIDTH), (HQ * HEAD_SIZE // 256) ** -0.5, 1.5, ((0, 32),)),
        "moe_gain": jnp.clip(1.0 + 0.1 * jax.random.normal(key_list[8], (MODEL_WIDTH,), jnp.float32), 0.5, 1.5).astype(jnp.bfloat16),
        "router": centred(key_list[9], (MODEL_WIDTH, EXPERTS), 0.011, 0.06591797, ((0, 32),)),
        "expert_gate": centred(key_list[10], (EXPERTS, MODEL_WIDTH, FF), MODEL_WIDTH ** -0.5, 0.125, ((0, 32),)),
        "expert_up": centred(key_list[11], (EXPERTS, MODEL_WIDTH, FF), MODEL_WIDTH ** -0.5, 0.125, ((0, 32),)),
        "expert_down": centred(key_list[12], (EXPERTS, FF, MODEL_WIDTH), (FF // 8) ** -0.5, 0.625, ((0, 32),)),
        "expert_ids": different_ones(key_list[13], TOKENS, EXPERTS, TOP, 0),
        "cont_segment": jax.vmap(lambda own: jnp.searchsorted(jnp.cumsum(uneven_parts(own, NCONT, CTOK, 2 * CONT, 0)), jnp.arange(CTOK), side="right"))(jax.random.split(key_list[14], GROUPS)).reshape((GROUPS, CTOK)).astype(jnp.int32),
        "out_grad": centred(key_list[15], (TOKENS, MODEL_WIDTH), 1.0, 6.0, ((0, 32),)),
    }


EPS = 1e-06
THETA = 1000000.0
HIGH_PRECISION = lax.Precision.HIGHEST

@jax.custom_vjp
def low(v):
    return lax.optimization_barrier(v.astype(jnp.bfloat16)).astype(jnp.float32)

@jax.custom_vjp
def reduced_backward(v):
    return v

def low_keep(v):
    return (low(v), None)

def low_pass(kept, grad):
    return (grad,)

def back_keep(v):
    return (v, None)

def back_low(kept, grad):
    return (low(grad),)
low.defvjp(low_keep, low_pass)
reduced_backward.defvjp(back_keep, back_low)

def norm_rows(value, gain):
    factor = lax.rsqrt(lax.optimization_barrier(jnp.mean(value * value, axis=-1, keepdims=True)) + EPS)
    return value * factor * gain

def rotate(value, cosine, sine):
    middle = value.shape[-1] // 2
    turned = jnp.concatenate([-value[..., middle:], value[..., :middle]], axis=-1)
    return value * cosine + turned * sine

def angle_tables(where_at, head_width):
    ranks = jnp.arange(head_width // 2, dtype=jnp.float32) * (2.0 / head_width)
    inverse = jnp.exp(-ranks * math.log(THETA))
    angles = where_at.astype(jnp.float32)[:, None] * inverse[None, :]
    angles = jnp.concatenate([angles, angles], axis=-1)
    return (jnp.cos(angles)[:, None, :], jnp.sin(angles)[:, None, :])

def group_layout(segment):
    length = segment.shape[0]
    one_hot = (segment[:, None] == jnp.arange(NCONT, dtype=jnp.int32)[None, :]).astype(jnp.int32)
    counted = lax.optimization_barrier(jnp.sum(one_hot, axis=0))
    starts = jnp.cumsum(counted) - counted
    begins = lax.optimization_barrier(jnp.sum(one_hot * starts[None, :], axis=1))
    within = jnp.arange(length, dtype=jnp.int32) - begins
    where_at = jnp.concatenate([jnp.arange(PROMPT, dtype=jnp.int32), PROMPT + within])
    labels = jnp.concatenate([jnp.zeros((PROMPT,), jnp.int32), segment + 1])
    return (where_at, labels)

def block_mask(labels, start, rows):
    query_at = start + jnp.arange(rows, dtype=jnp.int32)
    key_at = jnp.arange(labels.shape[0], dtype=jnp.int32)
    query_label = lax.dynamic_slice_in_dim(labels, start, rows, 0)
    causal = key_at[None, :] <= query_at[:, None]
    same = (labels[None, :] == 0) | (labels[None, :] == query_label[:, None])
    return causal & same

def slot_plan(ids, experts, capacity):
    flat = ids.reshape(-1)
    one_hot = (flat[:, None] == jnp.arange(experts, dtype=jnp.int32)[None, :]).astype(jnp.int32)
    earlier = jnp.cumsum(one_hot, axis=0) - one_hot
    slots = lax.optimization_barrier(jnp.sum(earlier * one_hot, axis=1))
    kept = slots < capacity
    target = jnp.where(kept, flat * capacity + slots, experts * capacity)
    return (target, kept.astype(jnp.float32))

def attention_branch(rows, where_at, labels, attn_gain, w_query, key_matrix, value_matrix, query_gain, key_gain, w_out):
    group_length = rows.shape[0]
    normalized_input = low(norm_rows(rows, attn_gain))
    query_raw = reduced_backward(jnp.dot(normalized_input, w_query, precision=HIGH_PRECISION)).reshape(group_length, HQ, HEAD_SIZE)
    key_unrotated = reduced_backward(jnp.dot(normalized_input, key_matrix, precision=HIGH_PRECISION)).reshape(group_length, KEY_VALUE_HEADS, HEAD_SIZE)
    value_unprojected = reduced_backward(jnp.dot(normalized_input, value_matrix, precision=HIGH_PRECISION)).reshape(group_length, KEY_VALUE_HEADS, HEAD_SIZE)
    cosine, sine = angle_tables(where_at, HEAD_SIZE)
    replica_count = N_SEQ // KEY_VALUE_HEADS
    queries = low(reduced_backward(rotate(norm_rows(query_raw, query_gain), cosine, sine)))
    queries = queries.reshape(group_length, N_SEQ, HQ // N_SEQ, HEAD_SIZE)
    keys = low(reduced_backward(jnp.repeat(rotate(norm_rows(key_unrotated, key_gain), cosine, sine), replica_count, axis=1)))
    values = low(reduced_backward(jnp.repeat(value_unprojected, replica_count, axis=1)))
    factor = 1.0 / math.sqrt(HEAD_SIZE)

    def block(index):
        start = index * QBLK
        query_block = lax.dynamic_slice_in_dim(queries, start, QBLK, 0)
        scores = reduced_backward(jnp.einsum('qjhd,kjd->jhqk', query_block, keys, precision=HIGH_PRECISION) * factor)
        allowed = block_mask(labels, start, QBLK)
        probs = jax.nn.softmax(jnp.where(allowed[None, None], scores, -jnp.inf), axis=-1)
        mixed = jnp.einsum('jhqk,kjd->qjhd', low(probs), values, precision=HIGH_PRECISION)
        return mixed.reshape(QBLK, HQ * HEAD_SIZE)
    mixed = lax.map(jax.checkpoint(block), jnp.arange(group_length // QBLK, dtype=jnp.int32))
    mixed = low(reduced_backward(mixed.reshape(group_length, HQ * HEAD_SIZE)))
    return reduced_backward(jnp.dot(mixed, w_out, precision=HIGH_PRECISION))

def expert_block(rows, ids, moe_gain, router, expert_gate, expert_up, expert_down):
    moe_normed = low(norm_rows(rows, moe_gain))
    logits = reduced_backward(jnp.dot(moe_normed, router, precision=HIGH_PRECISION))
    gates = jax.nn.softmax(jnp.take_along_axis(logits, ids, axis=1), axis=-1)
    target, kept = slot_plan(ids, EXPERTS, CAP)
    slot_count = EXPERTS * CAP
    filled = jnp.zeros((slot_count + 1, MODEL_WIDTH), jnp.float32).at[target].set(jnp.repeat(moe_normed, TOP, axis=0))
    slots = reduced_backward(filled[:slot_count]).reshape(EXPERTS, CAP, MODEL_WIDTH)
    gate = reduced_backward(jnp.einsum('ecd,edf->ecf', slots, expert_gate, precision=HIGH_PRECISION))
    up_pre = reduced_backward(jnp.einsum('ecd,edf->ecf', slots, expert_up, precision=HIGH_PRECISION))
    hidden = low(jax.nn.silu(gate) * up_pre)
    produced = low(reduced_backward(jnp.einsum('ecf,efd->ecd', hidden, expert_down, precision=HIGH_PRECISION)))
    padded = jnp.concatenate([produced.reshape(slot_count, MODEL_WIDTH), jnp.zeros((1, MODEL_WIDTH), jnp.float32)], axis=0)
    pair_out = padded[target]
    weight = gates.reshape(-1) * kept
    return lax.optimization_barrier(jnp.sum((weight[:, None] * pair_out).reshape(rows.shape[0], TOP, MODEL_WIDTH), axis=1))

def reference(layer_input, attn_gain, w_query, key_matrix, value_matrix, query_gain, key_gain, w_out, moe_gain, router, expert_gate, expert_up, expert_down, expert_ids, cont_segment, out_grad):
    where_at, labels = lax.map(group_layout, cont_segment)
    floats = tuple((a.astype(jnp.float32) for a in (layer_input, attn_gain, w_query, key_matrix, value_matrix, query_gain, key_gain, w_out, moe_gain, router, expert_gate, expert_up, expert_down)))

    def forward(inputs, a_gain, wq_full, wk_full, wv_full, q_gain, k_gain, wo_full, m_gain, route_w, gate_w, up_w, down_w):
        grouped = inputs.reshape(GROUPS, GROUP_TOK, MODEL_WIDTH)

        def branch(pack):
            return attention_branch(pack[0], pack[1], pack[2], a_gain, wq_full, wk_full, wv_full, q_gain, k_gain, wo_full)
        attended = lax.map(jax.checkpoint(branch), (grouped, where_at, labels)).reshape(TOKENS, MODEL_WIDTH)
        resid = inputs + attended

        def moe_part(pack):
            return expert_block(pack[0], pack[1], m_gain, route_w, gate_w, up_w, down_w)
        moe_out = lax.map(jax.checkpoint(moe_part), (resid.reshape(TOKENS // TOK_DEV, TOK_DEV, MODEL_WIDTH), expert_ids.reshape(TOKENS // TOK_DEV, TOK_DEV, TOP)))
        return resid + moe_out.reshape(TOKENS, MODEL_WIDTH)
    result, pull = jax.vjp(forward, *floats)
    grads = pull(out_grad.astype(jnp.float32))
    return (result.astype(jnp.bfloat16), grads[0], grads[1], grads[2], grads[3], grads[4], grads[5], grads[6], grads[7], grads[8], grads[9], grads[10], grads[11], grads[12])
```

```python
from functools import partial
import math

import jax
import jax.numpy as jnp
from jax import lax
from jax.experimental import pallas as pl
from jax.experimental.pallas import tpu as pltpu
from jax.sharding import Mesh, PartitionSpec as P

HQ = 32
KEY_VALUE_HEADS = 4
TOP = 8
PROMPT = 1024
NCONT = 4
HEAD = 128

EPS = 1e-06
THETA = 1000000.0
LOG2E = 1.4426950408889634
BF = jnp.bfloat16
F32 = jnp.float32

STEPS = 4
ORDER = ((0, 1, 2, 3), (1, 0, 2, 3), (2, 3, 1, 0), (3, 2, 1, 0))
PLANE = ("dp", "core")
ALL = ("dp", "z", "core")


def norm_rows(value, gain):
    factor = lax.rsqrt(jnp.mean(value * value, axis=-1, keepdims=True) + EPS)
    return value * factor * gain


def rotate(value, cosine, sine):
    middle = value.shape[-1] // 2
    turned = jnp.concatenate([-value[..., middle:], value[..., :middle]], axis=-1)
    return value * cosine + turned * sine


def angle_tables(where_at, head_width):
    ranks = jnp.arange(head_width // 2, dtype=F32) * (2.0 / head_width)
    inverse = jnp.exp(-ranks * math.log(THETA))
    angles = where_at.astype(F32)[:, None] * inverse[None, :]
    angles = jnp.concatenate([angles, angles], axis=-1)
    return (jnp.cos(angles)[:, None, :], jnp.sin(angles)[:, None, :])


def group_layout(segment):
    length = segment.shape[0]
    one_hot = (segment[:, None] == jnp.arange(NCONT, dtype=jnp.int32)[None, :]).astype(jnp.int32)
    counted = jnp.sum(one_hot, axis=0)
    before = jnp.arange(NCONT)[:, None] > jnp.arange(NCONT)[None, :]
    starts = jnp.sum(jnp.where(before, counted[None, :], 0), axis=1)
    begins = jnp.sum(one_hot * starts[None, :], axis=1)
    within = jnp.arange(length, dtype=jnp.int32) - begins
    where_at = jnp.concatenate([jnp.arange(PROMPT, dtype=jnp.int32), PROMPT + within])
    opens = jnp.concatenate([jnp.full((PROMPT,), PROMPT, jnp.int32), PROMPT + begins])
    return (where_at, opens)


def prep_heads(cosine, sine, raw, gain):
    return rotate(norm_rows(raw, gain), cosine, sine)


def contract_rows(left, right):
    return lax.dot_general(left, right, (((0,), (0,)), ((), ())), preferred_element_type=F32)


def times_transposed(left, right):
    return lax.dot_general(left, right, (((1,), (1,)), ((), ())), preferred_element_type=F32)


def line_gather(block, z):
    up = lax.ppermute(block, "z", [(0, 1), (1, 2), (2, 3)])
    down = lax.ppermute(block, "z", [(1, 0), (2, 1), (3, 2)])
    up2 = lax.ppermute(up, "z", [(1, 2), (2, 3)])
    down2 = lax.ppermute(down, "z", [(1, 0), (2, 1)])
    last = lax.ppermute(jnp.where(z == 2, up2, down2), "z", [(2, 3), (1, 0)])
    first = jnp.where(z % 2 == 0, down, up)
    second = jnp.where(z == 0, down2, jnp.where(z == 1, down, jnp.where(z == 2, up, up2)))
    third = jnp.where(z == 1, down2, jnp.where(z == 2, up2, last))
    return [block, first, second, third]


def line_scatter(parts, z):
    def added(part, got):
        return (part.astype(F32) + got.astype(F32)).astype(BF)

    own, first, second, third = parts
    got = lax.ppermute(third, "z", [(0, 1), (3, 2)])
    middle = added(jnp.where((z == 0) | (z == 3), second, third), got)
    up = lax.ppermute(middle, "z", [(0, 1), (1, 2)])
    down = lax.ppermute(middle, "z", [(3, 2), (2, 1)])
    up = lax.ppermute(added(jnp.where(z == 1, second, first), up), "z", [(0, 1), (1, 2), (2, 3)])
    down = lax.ppermute(added(jnp.where(z == 2, second, first), down), "z", [(3, 2), (2, 1), (1, 0)])
    return own.astype(F32) + up.astype(F32) + down.astype(F32)


def other_cores(value):
    cores = lax.axis_size("core")
    return [
        lax.ppermute(value, "core", [((i + k) % cores, i) for i in range(cores)])
        for k in range(1, cores)
    ]


def cores_in_order(value, c):
    cores = lax.axis_size("core")
    pieces = jnp.stack([value, *other_cores(value)])
    return jnp.concatenate(
        [
            lax.dynamic_index_in_dim(pieces, (n - c) % cores, 0, keepdims=True)
            for n in range(cores)
        ]
    )


def sum_over_cores(pieces):
    cores = lax.axis_size("core")
    total = pieces[0].astype(F32)
    for k in range(1, cores):
        got = lax.ppermute(pieces[k], "core", [(i, (i + k) % cores) for i in range(cores)])
        total = total + got.astype(F32)
    return total


def _mask_bias(at_ref, opens_ref, bias_ref, low, high):
    rows = bias_ref.shape[0]
    key_at = low + lax.broadcasted_iota(jnp.int32, (rows, high - low), 1)
    query_at = at_ref[...]
    allowed = (key_at <= query_at) & ((key_at < PROMPT) | (key_at >= opens_ref[...]))
    bias_ref[:, low:high] = jnp.where(allowed, 0.0, -1e30).astype(F32)


def _spans(number, chunk):
    low = min(number * chunk, PROMPT)
    return (number + 1) * chunk, low


def _attend_kernel(order, q_ref, k_ref, v_ref, at_ref, opens_ref, o_ref, l_ref, bias_ref, *, chunk):
    number = order[pl.program_id(0)]
    for n in range(STEPS):

        @pl.when(number == n)
        def _(n=n):
            keys, masked = _spans(n, chunk)

            @pl.when(pl.program_id(1) == 0)
            def _():
                _mask_bias(at_ref, opens_ref, bias_ref, masked, keys)

            query = q_ref[...]
            scores = []
            for low in range(0, keys, chunk):
                s = times_transposed(query, k_ref[low : low + chunk, :])
                if low >= masked:
                    s = s + bias_ref[:, low : low + chunk]
                scores.append(s)
            peak = scores[0].max(axis=-1, keepdims=True)
            for s in scores[1:]:
                peak = jnp.maximum(peak, s.max(axis=-1, keepdims=True))
            total, out = None, None
            for j, s in enumerate(scores):
                p = jnp.exp2(s - peak)
                t = jnp.sum(p, axis=-1, keepdims=True)
                o = jnp.dot(
                    p.astype(BF), v_ref[j * chunk : (j + 1) * chunk, :], preferred_element_type=F32
                )
                total = t if total is None else total + t
                out = o if out is None else out + o
            o_ref[...] = (out / total).astype(BF)
            l_ref[0] = jnp.broadcast_to(peak + jnp.log2(total), l_ref.shape[1:])


def attend(order, queries, keys, values, query_at, opens, rows):
    tokens, width = queries.shape
    heads = width // HEAD
    group = keys.shape[0]
    chunk = group // STEPS
    full = pl.BlockSpec((group, HEAD), lambda i, h, o: (0, 0))
    column = pl.BlockSpec((rows, 1), lambda i, h, o: (i, 0))
    tile = pl.BlockSpec((rows, HEAD), lambda i, h, o: (i, h))
    scores = heads * rows * group * STEPS * 5 // 8
    return pl.pallas_call(
        partial(_attend_kernel, chunk=chunk),
        grid_spec=pltpu.PrefetchScalarGridSpec(
            num_scalar_prefetch=1,
            grid=(STEPS, heads),
            in_specs=[tile, full, full, column, column],
            out_specs=[tile, pl.BlockSpec((1, rows, HEAD), lambda i, h, o: (h, i, 0))],
            scratch_shapes=[pltpu.VMEM((rows, group), F32)],
        ),
        out_shape=[
            jax.ShapeDtypeStruct((tokens, width), BF),
            jax.ShapeDtypeStruct((heads, tokens, HEAD), F32),
        ],
        compiler_params=pltpu.CompilerParams(vmem_limit_bytes=40 * 1024 * 1024),
        cost_estimate=pl.CostEstimate(
            flops=4 * scores * HEAD, bytes_accessed=12 * tokens * width, transcendentals=scores
        ),
        name="attend",
    )(order, queries, keys, values, query_at, opens)


def _attend_back_kernel(
    order, q_ref, do_ref, o_ref, l_ref, k_ref, v_ref, at_ref, opens_ref,
    dq_ref, dk_ref, dv_ref, bias_ref, *, chunk,
):
    number = order[pl.program_id(0)]

    @pl.when((pl.program_id(0) == 0) & (pl.program_id(1) == 0))
    def _():
        dk_ref[...] = jnp.zeros_like(dk_ref)
        dv_ref[...] = jnp.zeros_like(dv_ref)

    for n in range(STEPS):

        @pl.when(number == n)
        def _(n=n):
            keys, masked = _spans(n, chunk)

            @pl.when(pl.program_id(1) == 0)
            def _():
                _mask_bias(at_ref, opens_ref, bias_ref, masked, keys)

            query, grad = q_ref[...], do_ref[...]
            centre = jnp.sum(
                grad.astype(F32) * o_ref[...].astype(F32), axis=-1, keepdims=True
            )
            log_total = l_ref[0][:, :1]
            dq = None
            for low in range(0, keys, chunk):
                span = slice(low, low + chunk)
                key = k_ref[span, :]
                s = times_transposed(query, key)
                if low >= masked:
                    s = s + bias_ref[:, span]
                p = jnp.exp2(s - log_total)
                dp = times_transposed(grad, v_ref[span, :])
                ds = (p * (dp - centre)).astype(BF)
                dv_ref[span, :] += contract_rows(p.astype(BF), grad)
                dk_ref[span, :] += contract_rows(ds, query)
                part = jnp.dot(ds, key, preferred_element_type=F32)
                dq = part if dq is None else dq + part
            dq_ref[...] = dq.astype(dq_ref.dtype)


def attend_back(order, queries, grads, mixed, log_totals, keys, values, query_at, opens, rows):
    tokens, width = queries.shape
    heads = width // HEAD
    group = keys.shape[0]
    chunk = group // STEPS
    full = pl.BlockSpec((group, HEAD), lambda i, h, o: (0, 0))
    column = pl.BlockSpec((rows, 1), lambda i, h, o: (i, 0))
    tile = pl.BlockSpec((rows, HEAD), lambda i, h, o: (i, h))
    scores = heads * rows * group * STEPS * 5 // 8
    return pl.pallas_call(
        partial(_attend_back_kernel, chunk=chunk),
        grid_spec=pltpu.PrefetchScalarGridSpec(
            num_scalar_prefetch=1,
            grid=(STEPS, heads),
            in_specs=[
                tile,
                tile,
                tile,
                pl.BlockSpec((1, rows, HEAD), lambda i, h, o: (h, i, 0)),
                full,
                full,
                column,
                column,
            ],
            out_specs=[tile, full, full],
            scratch_shapes=[pltpu.VMEM((rows, group), F32)],
        ),
        out_shape=[
            jax.ShapeDtypeStruct((tokens, width), F32),
            jax.ShapeDtypeStruct((group, HEAD), F32),
            jax.ShapeDtypeStruct((group, HEAD), F32),
        ],
        compiler_params=pltpu.CompilerParams(vmem_limit_bytes=40 * 1024 * 1024),
        cost_estimate=pl.CostEstimate(
            flops=10 * scores * HEAD, bytes_accessed=18 * tokens * width, transcendentals=scores
        ),
        name="attend_back",
    )(order, queries, grads, mixed, log_totals, keys, values, query_at, opens)


def _expert_kernel(x_ref, pulled_ref, weight_ref, gate_ref, up_ref, dx_ref, dg_ref, du_ref, h_ref, c_ref):
    rows = x_ref[...]
    gate = jnp.dot(rows, gate_ref[...], preferred_element_type=F32)
    up = jnp.dot(rows, up_ref[...], preferred_element_type=F32)
    weight = weight_ref[...]
    sigma = jax.nn.sigmoid(gate)
    swish = gate * sigma
    hidden = swish * up
    pulled = pulled_ref[...].astype(F32)
    c_ref[...] = jnp.sum(hidden * pulled, axis=-1, keepdims=True)
    h_ref[...] = (weight * hidden).astype(BF)
    pulled = weight * pulled
    gate_grad = (pulled * up * sigma * (1.0 + gate * (1.0 - sigma))).astype(BF)
    up_grad = (pulled * swish).astype(BF)
    dg_ref[...] = gate_grad
    du_ref[...] = up_grad
    dx = times_transposed(gate_grad, gate_ref[...]) + times_transposed(up_grad, up_ref[...])
    dx_ref[...] = dx.astype(BF)


def expert(rows, pulled, weight, gate, up):
    count, width = rows.shape
    hidden = gate.shape[1]
    step = min(count, 256)
    across = pl.BlockSpec((step, width), lambda i: (i, 0))
    thin = pl.BlockSpec((step, hidden), lambda i: (i, 0))
    column = pl.BlockSpec((step, 1), lambda i: (i, 0))
    full = pl.BlockSpec((width, hidden), lambda i: (0, 0))
    return pl.pallas_call(
        _expert_kernel,
        grid=(count // step,),
        in_specs=[across, thin, column, full, full],
        out_specs=[across, thin, thin, thin, column],
        out_shape=[
            jax.ShapeDtypeStruct((count, width), BF),
            jax.ShapeDtypeStruct((count, hidden), BF),
            jax.ShapeDtypeStruct((count, hidden), BF),
            jax.ShapeDtypeStruct((count, hidden), BF),
            jax.ShapeDtypeStruct((count, 1), F32),
        ],
        compiler_params=pltpu.CompilerParams(vmem_limit_bytes=48 * 1024 * 1024),
        cost_estimate=pl.CostEstimate(
            flops=8 * count * width * hidden,
            bytes_accessed=4 * count * width + 8 * count * hidden + 4 * width * hidden,
            transcendentals=count * hidden,
        ),
        name="expert",
    )(rows, pulled, weight, gate, up)


def _rows_kernel(*refs):
    count = (len(refs) - 1) // 2
    total = None
    for left, right in zip(refs[:count], refs[count:-1]):
        part = contract_rows(left[...], right[...])
        total = part if total is None else total + part
    refs[-1][...] = total


def contract_chunks(lefts, rights):
    count, tall = lefts[0].shape
    wide = rights[0].shape[1]
    step = min(tall, 256)
    return pl.pallas_call(
        _rows_kernel,
        grid=(tall // step,),
        in_specs=[pl.BlockSpec((count, step), lambda i: (0, i))] * len(lefts)
        + [pl.BlockSpec((count, wide), lambda i: (0, 0))] * len(rights),
        out_specs=pl.BlockSpec((step, wide), lambda i: (i, 0)),
        out_shape=jax.ShapeDtypeStruct((tall, wide), F32),
        compiler_params=pltpu.CompilerParams(vmem_limit_bytes=48 * 1024 * 1024),
        cost_estimate=pl.CostEstimate(
            flops=2 * len(lefts) * count * tall * wide,
            bytes_accessed=2 * len(lefts) * count * (tall + wide) + 4 * tall * wide,
            transcendentals=0,
        ),
        name="contract_chunks",
    )(*lefts, *rights)


def body(
    layer_input,
    attn_gain,
    w_query,
    key_matrix,
    value_matrix,
    query_gain,
    key_gain,
    w_out,
    moe_gain,
    router,
    expert_gate,
    expert_up,
    expert_down,
    expert_ids,
    cont_segment,
    out_grad,
):
    tokens, width = layer_input.shape
    sizes = [lax.axis_size(a) for a in ALL]
    dps, _, cores = sizes
    devices = math.prod(sizes)
    dp, z, c = [lax.axis_index(a) for a in ALL]
    experts = router.shape[1]
    capacity = tokens * TOP // experts
    plane = dps * cores
    slots = plane * capacity
    order = jnp.array(ORDER, jnp.int32)[z]
    where_block = jnp.array([[o.index(b) for b in range(STEPS)] for o in ORDER], jnp.int32)[z]
    own_heads = HQ // (STEPS * cores)
    heads = HQ // STEPS
    head_cols = heads * HEAD

    router_pad = -(experts + 2) % 128
    small = jnp.concatenate(
        [router, attn_gain[:, None], moe_gain[:, None], jnp.zeros((router.shape[0], router_pad), BF)],
        axis=1,
    )
    rows_dev = small.shape[0]
    packed = jnp.concatenate(
        [
            key_matrix.reshape(rows_dev, STEPS, HEAD).transpose(1, 0, 2),
            value_matrix.reshape(rows_dev, STEPS, HEAD).transpose(1, 0, 2),
            jnp.broadcast_to(small[None], (STEPS, *small.shape)),
        ],
        axis=2,
    )
    packed = lax.all_to_all(packed, "z", split_axis=0, concat_axis=0, tiled=True)
    packed = cores_in_order(packed, c).transpose(1, 0, 2, 3).reshape(w_query.shape[0], -1)
    gathered = lax.all_gather(jnp.concatenate([w_query, packed], axis=1), "dp", axis=0, tiled=True)
    own_cols = own_heads * HEAD
    query_own = gathered[:, :own_cols]
    key_value = gathered[:, own_cols : own_cols + 2 * HEAD]
    rest = gathered[:, own_cols + 2 * HEAD :]
    router_all = rest[:, :experts]
    attn_gain_all = rest[:, experts].astype(F32)
    moe_gain_all = rest[:, experts + 1].astype(F32)
    w_in = jnp.concatenate([query_own, *other_cores(query_own), key_value], axis=1)

    flat = [(b, (b % dps) * (devices // dps) + b // dps) for b in range(devices)]
    out_own = lax.all_gather(lax.ppermute(w_out, ALL, flat), "dp", axis=0, tiled=True)
    w_back = jnp.concatenate([out_own, *other_cores(out_own)], axis=0)

    where_at, opens = group_layout(cont_segment[0])
    group = where_at.shape[0]

    def own_rows(table):
        mine = lax.dynamic_index_in_dim(table.reshape(STEPS, cores, tokens), c, 1, keepdims=False)
        return jnp.concatenate(
            [lax.dynamic_index_in_dim(mine, order[i], 0, keepdims=False) for i in range(STEPS)]
        )

    cosine, sine = angle_tables(own_rows(where_at), HEAD)
    query_at = own_rows(jnp.arange(group, dtype=jnp.int32))[:, None]
    opens = own_rows(opens)[:, None]

    ids = lax.all_gather(expert_ids, "z", axis=0)
    ids = jnp.concatenate(
        [lax.dynamic_index_in_dim(ids, order[i], 0, keepdims=True) for i in range(STEPS)]
    )
    chosen = jnp.any(
        ids[:, :, :, None] == jnp.arange(experts, dtype=jnp.int32)[None, None, None, :], axis=2
    )
    earlier = jnp.arange(tokens)[:, None] > jnp.arange(tokens)[None, :]
    ranks = jnp.einsum(
        "ij,bje->bie", earlier.astype(BF), chosen.astype(BF), preferred_element_type=F32
    ).astype(jnp.int32)
    ranks = jnp.where(chosen & (ranks < capacity), ranks, -1)
    in_plane = lax.dynamic_index_in_dim(
        ranks.reshape(STEPS, tokens, dps, STEPS, cores), z, 3, keepdims=False
    ).reshape(STEPS, tokens, plane)
    at_slot = jnp.arange(capacity, dtype=jnp.int32)
    pick = (in_plane[:, :, :, None] == at_slot).reshape(STEPS, tokens, slots).astype(BF)
    own_chosen = chosen[0]
    own_ranks = ranks[0]
    own_pick = own_ranks[:, :, None] == at_slot

    def to_plane(rows):
        return lax.all_to_all(rows, PLANE, split_axis=0, concat_axis=0, tiled=True)

    def dispatch(i, rows):
        return to_plane(contract_rows(pick[i], rows).astype(BF))

    def combine(i, rows):
        return jnp.dot(pick[i], to_plane(rows), preferred_element_type=F32).astype(BF)

    arrived = jnp.concatenate(line_gather(layer_input, z))
    upstream_slots = [dispatch(i, g) for i, g in enumerate(line_gather(out_grad, z))]
    inputs = arrived.astype(F32)
    input_factor = lax.rsqrt(jnp.mean(inputs * inputs, axis=-1, keepdims=True) + EPS)
    normed = (inputs * input_factor * attn_gain_all).astype(BF)
    raw = jnp.dot(normed, w_in, preferred_element_type=F32)
    query_gain_f = query_gain.astype(F32)
    key_gain_f = key_gain.astype(F32)
    scale = LOG2E / math.sqrt(HEAD)
    query_rot, query_pull = jax.vjp(
        partial(prep_heads, cosine, sine), raw[:, :head_cols].reshape(-1, heads, HEAD), query_gain_f
    )
    key_rot, key_pull = jax.vjp(
        partial(prep_heads, cosine, sine),
        raw[:, head_cols : head_cols + HEAD].reshape(-1, 1, HEAD),
        key_gain_f,
    )
    queries = (query_rot * scale).astype(BF).reshape(-1, head_cols)
    key_value_rows = jnp.concatenate([key_rot[:, 0], raw[:, head_cols + HEAD :]], axis=1).astype(BF)
    spread = cores_in_order(key_value_rows, c).reshape(cores, STEPS, tokens, 2 * HEAD)
    spread = jnp.concatenate(
        [
            lax.dynamic_index_in_dim(spread, where_block[b], 1, keepdims=False).reshape(-1, 2 * HEAD)
            for b in range(STEPS)
        ]
    )
    keys, values = spread[:, :HEAD], spread[:, HEAD:]
    mixed, log_totals = attend(order, queries, keys, values, query_at, opens, tokens)
    attended = jnp.dot(mixed, w_back, preferred_element_type=F32).astype(BF)
    own_input = layer_input.astype(F32)
    resid = own_input + line_scatter(
        [attended[i * tokens : (i + 1) * tokens] for i in range(STEPS)], z
    )

    moe_normed, moe_norm_pull = jax.vjp(norm_rows, resid, moe_gain_all)
    moe_low = moe_normed.astype(BF)
    logits = jnp.dot(moe_low, router_all, preferred_element_type=F32)
    logits = jnp.where(own_chosen, logits, -jnp.inf)
    raised = jnp.exp(logits - jnp.max(logits, axis=-1, keepdims=True))
    gates = raised / jnp.sum(raised, axis=-1, keepdims=True)
    slot_gates = jnp.sum(jnp.where(own_pick, gates[:, :, None], 0.0), axis=0)
    slot_gates = lax.all_to_all(slot_gates, ALL, split_axis=0, concat_axis=0, tiled=True)
    slot_gates = slot_gates.reshape(dps, STEPS, cores, capacity)

    gate_w, up_w, down_w = expert_gate[0], expert_up[0], expert_down[0]
    pulled = [times_transposed(g, down_w) for g in upstream_slots]
    rows, outs = [], []
    for i, block in enumerate(line_gather(moe_low, z)):
        rows.append(dispatch(i, block))
        weight = lax.dynamic_index_in_dim(slot_gates, order[i], 1, keepdims=False).reshape(slots, 1)
        outs.append(expert(rows[i], pulled[i], weight, gate_w, up_w))
    slot_grads, gate_grads, up_grads, hiddens, centres = zip(*outs)

    stacked = jnp.stack([v.reshape(dps, cores, capacity) for v in centres])
    centre_back = jnp.stack(
        [
            lax.dynamic_index_in_dim(stacked, where_block[b], 0, keepdims=False)
            for b in range(STEPS)
        ],
        axis=1,
    ).reshape(experts, capacity)
    centre_back = lax.all_to_all(centre_back, ALL, split_axis=0, concat_axis=0, tiled=True)
    weight_grad = jnp.sum(jnp.where(own_pick, centre_back[None], 0.0), axis=2)
    slot_sum = line_scatter([combine(i, slot_grads[i]) for i in range(STEPS)], z)
    logit_grad = (
        gates * (weight_grad - jnp.sum(gates * weight_grad, axis=-1, keepdims=True))
    ).astype(BF)
    moe_low_grad = slot_sum + times_transposed(logit_grad, router_all)
    router_grad = contract_rows(moe_low, logit_grad)
    upstream = out_grad.astype(F32)
    resid_part, moe_gain_grad = moe_norm_pull(moe_low_grad)
    resid_grad = upstream + resid_part
    resid_low = resid_grad.astype(BF)

    down_weight_grad = contract_chunks(hiddens, upstream_slots)
    gate_weight_grad = contract_chunks(rows, gate_grads)
    up_weight_grad = contract_chunks(rows, up_grads)
    produced = [
        combine(i, jnp.dot(h, down_w, preferred_element_type=F32).astype(BF))
        for i, h in enumerate(hiddens)
    ]
    output = (resid + line_scatter(produced, z)).astype(BF)

    resid_all = jnp.concatenate(line_gather(resid_low, z))
    out_weight_grad = contract_rows(mixed, resid_all).astype(BF)
    rows_own = own_heads * HEAD
    out_weight_grad = sum_over_cores(
        [out_weight_grad[k * rows_own : (k + 1) * rows_own] for k in range(cores)]
    ).astype(BF)
    out_weight_grad = lax.psum_scatter(out_weight_grad, "dp", scatter_dimension=0, tiled=True)
    out_weight_grad = lax.ppermute(out_weight_grad, ALL, [(b, a) for a, b in flat]).astype(F32)
    mixed_grad = times_transposed(resid_all, w_back).astype(BF)
    query_grads, key_sum, value_sum = attend_back(
        order, queries, mixed_grad, mixed, log_totals, keys, values, query_at, opens, tokens
    )
    both = jnp.concatenate([key_sum * (1.0 / LOG2E), value_sum], axis=1)
    both = both.reshape(STEPS, cores, tokens, 2 * HEAD)
    both = jnp.stack(
        [lax.dynamic_index_in_dim(both, order[i], 0, keepdims=False) for i in range(STEPS)], axis=1
    )
    both = sum_over_cores(
        [
            lax.dynamic_index_in_dim(both, (c + k) % cores, 0, keepdims=False)
            for k in range(cores)
        ]
    ).reshape(-1, 2 * HEAD)
    query_raw_grad, query_gain_grad = query_pull(
        query_grads.reshape(-1, heads, HEAD) * (1.0 / math.sqrt(HEAD))
    )
    key_raw_grad, key_gain_grad = key_pull(both[:, None, :HEAD])
    raw_grad = jnp.concatenate(
        [query_raw_grad.reshape(-1, head_cols), key_raw_grad[:, 0], both[:, HEAD:]], axis=1
    ).astype(BF)
    normed_grad = times_transposed(raw_grad, w_in)
    attn_gain_grad = jnp.sum(normed_grad * inputs * input_factor, axis=0)
    normed_grad = normed_grad.astype(BF)
    normed_grad = line_scatter(
        [normed_grad[i * tokens : (i + 1) * tokens] for i in range(STEPS)], z
    )
    _, attn_norm_pull = jax.vjp(lambda v: norm_rows(v, attn_gain_all), own_input)
    input_grad = resid_grad + attn_norm_pull(normed_grad)[0]

    in_grad = contract_rows(normed, raw_grad).astype(BF)
    query_share = sum_over_cores(
        [in_grad[:, k * own_cols : (k + 1) * own_cols] for k in range(cores)]
    ).astype(BF)
    key_value_grad = in_grad[:, head_cols:].reshape(dps, STEPS, cores, rows_dev, 2 * HEAD)
    key_value_grad = sum_over_cores(
        [
            lax.dynamic_index_in_dim(key_value_grad, (c + k) % cores, 2, keepdims=False)
            for k in range(cores)
        ]
    )
    key_value_grad = key_value_grad.astype(BF).reshape(dps, -1, own_cols)
    share = jnp.concatenate(
        [query_share.reshape(dps, -1, own_cols), key_value_grad], axis=1
    ).reshape(-1, own_cols)
    share = lax.psum_scatter(share, "dp", scatter_dimension=0, tiled=True)
    query_rows = w_query.shape[0]
    query_weight_grad = share[:query_rows].astype(F32)
    key_value_grad = share[query_rows:].reshape(STEPS, rows_dev, 2 * HEAD)
    key_value_grad = lax.all_to_all(key_value_grad, "z", split_axis=0, concat_axis=0, tiled=True)
    key_value_grad = key_value_grad.transpose(1, 0, 2).astype(F32)
    key_weight_grad = key_value_grad[:, :, :HEAD].reshape(rows_dev, -1)
    value_weight_grad = key_value_grad[:, :, HEAD:].reshape(rows_dev, -1)

    small_grads = jnp.concatenate(
        [
            router_grad,
            attn_gain_grad[:, None],
            moe_gain_grad[:, None],
            jnp.zeros((width, router_pad), F32),
        ],
        axis=1,
    )
    small_grads = lax.psum_scatter(small_grads, ALL, scatter_dimension=0, tiled=True)
    gain_sums = lax.psum(jnp.stack([query_gain_grad, key_gain_grad]), ALL)
    return (
        output,
        input_grad,
        small_grads[:, experts],
        query_weight_grad,
        key_weight_grad,
        value_weight_grad,
        gain_sums[0],
        gain_sums[1],
        out_weight_grad,
        small_grads[:, experts + 1],
        small_grads[:, :experts],
        gate_weight_grad[None],
        up_weight_grad[None],
        down_weight_grad[None],
    )


def solution(mesh):
    dps, sequence = mesh.devices.shape
    inner = Mesh(mesh.devices.reshape(dps, STEPS, sequence // STEPS), ALL)
    rows = P(ALL, None)
    placed = (
        rows,
        P(ALL),
        P("dp", ("z", "core")),
        rows,
        rows,
        P(),
        P(),
        rows,
        P(ALL),
        rows,
        P(ALL, None, None),
        P(ALL, None, None),
        P(ALL, None, None),
        rows,
        P("dp", None),
        rows,
    )
    return jax.shard_map(
        body,
        mesh=inner,
        in_specs=placed,
        out_specs=(
            rows,
            rows,
            P(ALL),
            P("dp", ("z", "core")),
            rows,
            rows,
            P(),
            P(),
            rows,
            P(ALL),
            rows,
            P(ALL, None, None),
            P(ALL, None, None),
            P(ALL, None, None),
        ),
        check_vma=False,
    )
```

```python
from functools import partial
import math

import jax
import jax.numpy as jnp
from jax import lax
from jax.experimental import pallas as pl
from jax.experimental.pallas import tpu as pltpu
from jax.sharding import Mesh, PartitionSpec as P

HQ = 32
KEY_VALUE_HEADS = 4
TOP = 8
PROMPT = 1024
NCONT = 4
HEAD = 128

EPS = 1e-06
THETA = 1000000.0
LOG2E = 1.4426950408889634
BF = jnp.bfloat16
F32 = jnp.float32

STEPS = 4
ORDER = ((0, 1, 2, 3), (1, 0, 2, 3), (2, 3, 1, 0), (3, 2, 1, 0))
PLANE = ("dp", "core")
ALL = ("dp", "z", "core")


def angle_tables(where_at, head_width):
    ranks = jnp.arange(head_width // 2, dtype=F32) * (2.0 / head_width)
    inverse = jnp.exp(-ranks * math.log(THETA))
    angles = where_at.astype(F32)[:, None] * inverse[None, :]
    cosine, sine = jnp.cos(angles), jnp.sin(angles)
    return (
        jnp.concatenate([cosine, cosine], axis=-1),
        jnp.concatenate([-sine, sine], axis=-1),
    )


def group_layout(segment):
    length = segment.shape[0]
    one_hot = (segment[:, None] == jnp.arange(NCONT, dtype=jnp.int32)[None, :]).astype(jnp.int32)
    counted = jnp.sum(one_hot, axis=0)
    before = jnp.arange(NCONT)[:, None] > jnp.arange(NCONT)[None, :]
    starts = jnp.sum(jnp.where(before, counted[None, :], 0), axis=1)
    begins = jnp.sum(one_hot * starts[None, :], axis=1)
    within = jnp.arange(length, dtype=jnp.int32) - begins
    where_at = jnp.concatenate([jnp.arange(PROMPT, dtype=jnp.int32), PROMPT + within])
    opens = jnp.concatenate([jnp.full((PROMPT,), PROMPT, jnp.int32), PROMPT + begins])
    return (where_at, opens)


def contract_rows(left, right):
    return lax.dot_general(left, right, (((0,), (0,)), ((), ())), preferred_element_type=F32)


def times_transposed(left, right):
    return lax.dot_general(left, right, (((1,), (1,)), ((), ())), preferred_element_type=F32)


def hold(*values):
    return lax.optimization_barrier(values)


def spread_first(block):
    return (
        lax.ppermute(block, "z", [(0, 1), (1, 2), (2, 3)]),
        lax.ppermute(block, "z", [(1, 0), (2, 1), (3, 2)]),
    )


def spread_second(up, down):
    return (
        lax.ppermute(up, "z", [(1, 2), (2, 3)]),
        lax.ppermute(down, "z", [(2, 1), (1, 0)]),
    )


def spread_third(up2, down2, z):
    return lax.ppermute(jnp.where(z == 2, up2, down2), "z", [(2, 3), (1, 0)])


FIRST = (1, 0, 1, 0)
SECOND = (3, 1, 0, 2)
THIRD = (2, 1, 0, 2)


def sum_first(third):
    return lax.ppermute(third, "z", [(0, 1), (3, 2)])


def sum_second(middle):
    return (
        lax.ppermute(middle, "z", [(0, 1), (1, 2)]),
        lax.ppermute(middle, "z", [(3, 2), (2, 1)]),
    )


def sum_third(up, down):
    return (
        lax.ppermute(up, "z", [(0, 1), (1, 2), (2, 3)]),
        lax.ppermute(down, "z", [(3, 2), (2, 1), (1, 0)]),
    )


def over_dps(value, dp):
    dps = value.shape[0]
    total = lax.dynamic_index_in_dim(value, dp, 0, keepdims=False).astype(F32)
    for k in range(1, dps):
        piece = lax.dynamic_index_in_dim(value, dp ^ k, 0, keepdims=False)
        total = total + lax.ppermute(piece, "dp", [(i, i ^ k) for i in range(dps)]).astype(F32)
    return total


def from_dps(value, dp):
    dps = lax.axis_size("dp")
    whole = jnp.zeros((dps, *value.shape), value.dtype)
    whole = lax.dynamic_update_index_in_dim(whole, value, dp, 0)
    for k in range(1, dps):
        got = lax.ppermute(value, "dp", [(i, i ^ k) for i in range(dps)])
        whole = lax.dynamic_update_index_in_dim(whole, got, dp ^ k, 0)
    return whole


def other_cores(value):
    cores = lax.axis_size("core")
    return [
        lax.ppermute(value, "core", [((i + k) % cores, i) for i in range(cores)])
        for k in range(1, cores)
    ]


def cores_in_order(value, c):
    cores = lax.axis_size("core")
    pieces = [value, *other_cores(value)]
    ordered = []
    for n in range(cores):
        piece = pieces[0]
        for k in range(1, cores):
            piece = jnp.where((n - c) % cores == k, pieces[k], piece)
        ordered.append(piece)
    return ordered


def sum_over_cores(pieces):
    cores = lax.axis_size("core")
    total = pieces[0].astype(F32)
    for k in range(1, cores):
        got = lax.ppermute(pieces[k], "core", [(i, (i + k) % cores) for i in range(cores)])
        total = total + got.astype(F32)
    return total


CHEAP = pl.CostEstimate(flops=1, bytes_accessed=1, transcendentals=0)


def run(kernel, name, grid, operands, in_specs, outs, out_specs, scalars=None, scratch=(), aliases=None):
    prefetch = () if scalars is None else (scalars,)
    aliases = {i + len(prefetch): o for i, o in (aliases or {}).items()}
    got = pl.pallas_call(
        kernel,
        grid_spec=pltpu.PrefetchScalarGridSpec(
            num_scalar_prefetch=len(prefetch),
            grid=grid,
            in_specs=in_specs,
            out_specs=out_specs,
            scratch_shapes=scratch,
        ),
        out_shape=[pltpu.HBM(shape, kind) for shape, kind in outs],
        input_output_aliases=aliases,
        compiler_params=pltpu.CompilerParams(vmem_limit_bytes=52 * 1024 * 1024),
        cost_estimate=CHEAP,
        name=name,
    )(*prefetch, *[pltpu.with_memory_space_constraint(v, pltpu.HBM) for v in operands])
    return got


def full(*shape):
    return pl.BlockSpec(shape, lambda *_: (0,) * len(shape))


def _matmul_kernel(a_ref, b_ref, o_ref, *, dims):
    part = lax.dot_general(a_ref[...], b_ref[...], (dims, ((), ())), preferred_element_type=F32)
    o_ref[...] = part.astype(o_ref.dtype)


def matmul(a, b, kind, steps, by, out=BF):
    dims = {"nn": ((1,), (0,)), "nt": ((1,), (1,)), "tn": ((0,), (0,))}[kind]
    rows = a.shape[1 - dims[0][0]]
    columns = b.shape[1 - dims[1][0]]
    a_spec, b_spec = full(*a.shape), full(*b.shape)
    if by == "rows":
        size = rows // steps
        if kind == "tn":
            a_spec = pl.BlockSpec((a.shape[0], size), lambda i: (0, i))
        else:
            a_spec = pl.BlockSpec((size, a.shape[1]), lambda i: (i, 0))
        o_spec = pl.BlockSpec((size, columns), lambda i: (i, 0))
    else:
        size = columns // steps
        if kind == "nt":
            b_spec = pl.BlockSpec((size, b.shape[1]), lambda i: (i, 0))
        else:
            b_spec = pl.BlockSpec((b.shape[0], size), lambda i: (0, i))
        o_spec = pl.BlockSpec((rows, size), lambda i: (0, i))
    return run(
        partial(_matmul_kernel, dims=dims),
        "matmul_" + kind,
        (steps,),
        (a, b),
        [a_spec, b_spec],
        [((rows, columns), out)],
        [o_spec],
    )[0]


def _dispatch_kernel(s_ref, pick_ref, *refs, sources):
    z, rows = s_ref[0], refs[0][...]
    for n in range(1, len(refs) - 1):
        here = False
        for at, source in enumerate(sources):
            if source == n:
                here = here | (z == at)
        rows = jnp.where(here, refs[n][...], rows)
    refs[-1][...] = jnp.dot(pick_ref[...], rows, preferred_element_type=F32).astype(BF)


def dispatch(scalars, pick, blocks, sources):
    slots, tokens = pick.shape
    width = blocks[0].shape[1]
    tile = pl.BlockSpec((tokens, 1024), lambda j, s: (0, j))
    return run(
        partial(_dispatch_kernel, sources=sources),
        "dispatch",
        (width // 1024,),
        (pick, *blocks),
        [full(slots, tokens)] + [tile] * len(blocks),
        [((slots, width), BF)],
        [pl.BlockSpec((slots, 1024), lambda j, s: (0, j))],
        scalars=scalars,
    )[0]


def _part_kernel(s_ref, a_ref, b_ref, *refs, step):
    z = s_ref[0]
    part = jnp.dot(a_ref[...], b_ref[...], preferred_element_type=F32)
    if step == 0:
        refs[0][...] = part.astype(BF)
    elif step == 1:
        third, got, part_ref, middle_ref = refs
        part_ref[...] = part.astype(BF)
        middle = jnp.where((z == 0) | (z == 3), part, third[...].astype(F32))
        middle_ref[...] = (middle + got[...].astype(F32)).astype(BF)
    else:
        second, up, down, up_ref, down_ref = refs
        other = second[...].astype(F32)
        up_ref[...] = (jnp.where(z == 1, other, part) + up[...].astype(F32)).astype(BF)
        down_ref[...] = (jnp.where(z == 2, other, part) + down[...].astype(F32)).astype(BF)


def line_part(scalars, a, b, tokens, step=0, more=()):
    width = b.shape[1]
    tile = pl.BlockSpec((tokens, 1024), lambda j, s: (0, j))
    return run(
        partial(_part_kernel, step=step),
        "line_part",
        (width // 1024,),
        (a, b, *more),
        [
            pl.BlockSpec((tokens, a.shape[1]), lambda j, s: (s[1], 0)),
            pl.BlockSpec((b.shape[0], 1024), lambda j, s: (0, j)),
        ]
        + [tile] * len(more),
        [((tokens, width), BF)] * (1 if step == 0 else 2),
        [tile] * (1 if step == 0 else 2),
        scalars=scalars,
    )


def _norm_kernel(x_ref, gain_ref, *refs):
    terms, (resid_ref, low_ref) = refs[:-2], refs[-2:]
    value = x_ref[...].astype(F32)
    for term in terms:
        value = value + term[...].astype(F32)
    resid_ref[...] = value
    factor = lax.rsqrt(jnp.mean(value * value, axis=-1, keepdims=True) + EPS)
    low_ref[...] = (value * factor * gain_ref[...]).astype(BF)


def add_and_norm(x, gain, terms):
    tokens, width = x.shape
    step = min(tokens, 64)
    tile = pl.BlockSpec((step, width), lambda i: (i, 0))
    return run(
        _norm_kernel,
        "add_and_norm",
        (tokens // step,),
        (x, gain, *terms),
        [tile, full(1, width)] + [tile] * len(terms),
        [((tokens, width), F32), ((tokens, width), BF)],
        [tile, tile],
    )


def _norm_back_kernel(v_ref, gain_ref, above_ref, *refs, logits):
    if logits:
        logit_ref, router_ref, *terms, total_ref, low_ref, gain_grad_ref = refs
    else:
        *terms, total_ref = refs
    grad = sum([term[...].astype(F32) for term in terms])
    if logits:
        grad = grad + times_transposed(logit_ref[...], router_ref[...])
    value = v_ref[...].astype(F32)
    factor = lax.rsqrt(jnp.mean(value * value, axis=-1, keepdims=True) + EPS)
    unit = value * factor
    if logits:

        @pl.when(pl.program_id(0) == 0)
        def _():
            gain_grad_ref[...] = jnp.zeros_like(gain_grad_ref)

        gain_grad_ref[...] += jnp.sum(grad * unit, axis=0, keepdims=True)
    grad = grad * gain_ref[...]
    shift = jnp.mean(grad * unit, axis=-1, keepdims=True)
    total = above_ref[...].astype(F32) + factor * (grad - unit * shift)
    total_ref[...] = total
    if logits:
        low_ref[...] = total.astype(BF)


def norm_back(value, gain, above, terms, logit_grad=None, router=None):
    tokens, width = value.shape
    step = min(tokens, 64)
    tile = pl.BlockSpec((step, width), lambda i: (i, 0))
    operands, specs = [value, gain, above], [tile, full(1, width), tile]
    outs, out_specs = [((tokens, width), F32)], [tile]
    if logit_grad is not None:
        lanes = logit_grad.shape[1]
        operands += [logit_grad, router]
        specs += [pl.BlockSpec((step, lanes), lambda i: (i, 0)), full(width, lanes)]
        outs += [((tokens, width), BF), ((1, width), F32)]
        out_specs += [tile, full(1, width)]
    return run(
        partial(_norm_back_kernel, logits=logit_grad is not None),
        "norm_back",
        (tokens // step,),
        (*operands, *terms),
        specs + [tile] * len(terms),
        outs,
        out_specs,
    )


def _project_kernel(
    x_ref, gain_ref, w_ref, cos_ref, sin_ref, qg_ref, kg_ref, n_ref, raw_ref, q_ref, kv_ref
):
    x = x_ref[...].astype(F32)
    factor = lax.rsqrt(jnp.mean(x * x, axis=-1, keepdims=True) + EPS)
    normed = (x * factor * gain_ref[...]).astype(BF)
    n_ref[...] = normed
    raw_ref[...] = jnp.dot(normed, w_ref[...], preferred_element_type=F32)
    cosine, sine = cos_ref[...], sin_ref[...]
    heads = q_ref.shape[1] // HEAD
    for h in range(heads + 1):
        cols = slice(h * HEAD, (h + 1) * HEAD)
        value = raw_ref[:, cols]
        factor = lax.rsqrt(jnp.mean(value * value, axis=-1, keepdims=True) + EPS)
        value = value * factor * (qg_ref[...] if h < heads else kg_ref[...])
        value = (value * cosine + pltpu.roll(value, HEAD // 2, 1) * sine).astype(BF)
        if h < heads:
            q_ref[:, cols] = value
        else:
            kv_ref[:, :HEAD] = value
    kv_ref[:, HEAD:] = raw_ref[:, (heads + 1) * HEAD :].astype(BF)


def project(x, gain, w_in, cosine, sine, query_gain, key_gain, rows):
    tokens, width = x.shape
    columns = w_in.shape[1]

    def tile(size):
        return pl.BlockSpec((rows, size), lambda i: (i, 0))

    return run(
        _project_kernel,
        "project",
        (tokens // rows,),
        (x, gain, w_in, cosine, sine, query_gain, key_gain),
        [tile(width), full(1, width), full(width, columns), tile(HEAD), tile(HEAD)]
        + [full(1, HEAD)] * 2,
        [
            ((tokens, width), BF),
            ((tokens, columns), F32),
            ((tokens, columns - 2 * HEAD), BF),
            ((tokens, 2 * HEAD), BF),
        ],
        [tile(width), tile(columns), tile(columns - 2 * HEAD), tile(2 * HEAD)],
    )


def _project_back_kernel(
    raw_ref, dq_ref, dkv_ref, w_ref, cos_ref, sin_ref, qg_ref, kg_ref, ng_ref, rg_ref, dqg_ref, dkg_ref
):
    @pl.when(pl.program_id(0) == 0)
    def _():
        dqg_ref[...] = jnp.zeros_like(dqg_ref)
        dkg_ref[...] = jnp.zeros_like(dkg_ref)

    cosine, sine = cos_ref[...], sin_ref[...]
    heads = dq_ref.shape[1] // HEAD
    for h in range(heads + 1):
        cols = slice(h * HEAD, (h + 1) * HEAD)
        value = raw_ref[:, cols]
        factor = lax.rsqrt(jnp.mean(value * value, axis=-1, keepdims=True) + EPS)
        unit = value * factor
        if h < heads:
            grad = dq_ref[:, cols].astype(F32) * (1.0 / math.sqrt(HEAD))
        else:
            grad = dkv_ref[:, :HEAD]
        grad = grad * cosine + pltpu.roll(grad * sine, HEAD // 2, 1)
        gain_grad = jnp.sum(grad * unit, axis=0, keepdims=True)
        if h < heads:
            dqg_ref[...] += gain_grad
            grad = grad * qg_ref[...]
        else:
            dkg_ref[...] += gain_grad
            grad = grad * kg_ref[...]
        shift = jnp.mean(grad * unit, axis=-1, keepdims=True)
        rg_ref[:, cols] = (factor * (grad - unit * shift)).astype(BF)
    rg_ref[:, (heads + 1) * HEAD :] = dkv_ref[:, HEAD:].astype(BF)
    ng_ref[...] = times_transposed(rg_ref[...], w_ref[...]).astype(BF)


def project_back(raw, query_grads, key_value_grads, w_in, cosine, sine, query_gain, key_gain, rows):
    tokens, columns = raw.shape
    width = w_in.shape[0]

    def tile(size):
        return pl.BlockSpec((rows, size), lambda i: (i, 0))

    return run(
        _project_back_kernel,
        "project_back",
        (tokens // rows,),
        (raw, query_grads, key_value_grads, w_in, cosine, sine, query_gain, key_gain),
        [
            tile(columns),
            tile(columns - 2 * HEAD),
            tile(2 * HEAD),
            full(width, columns),
            tile(HEAD),
            tile(HEAD),
            full(1, HEAD),
            full(1, HEAD),
        ],
        [((tokens, width), BF), ((tokens, columns), BF), ((1, HEAD), F32), ((1, HEAD), F32)],
        [tile(width), tile(columns), full(1, HEAD), full(1, HEAD)],
    )


def _mask_bias(at_ref, opens_ref, bias_ref, low, high):
    rows = at_ref.shape[0]
    key_at = low + lax.broadcasted_iota(jnp.int32, (rows, high - low), 1)
    query_at = at_ref[...]
    allowed = (key_at <= query_at) & ((key_at < PROMPT) | (key_at >= opens_ref[...]))
    bias = jnp.where(allowed, 0.0, -1e30).astype(F32)
    bias_ref[:rows, low:high] = bias
    bias_ref[rows:, low:high] = bias


def _spans(number, chunk):
    return (number + 1) * chunk, min(number * chunk, PROMPT)


def _place_keys(table, pieces, k_ref, v_ref, rows):
    for k, piece in enumerate(pieces):
        for i in range(STEPS):
            place = pl.ds(pl.multiple_of(table[k * STEPS + i], rows), rows)
            k_ref[place, :HEAD] = piece[i * rows : (i + 1) * rows, :HEAD]
            v_ref[place, :HEAD] = piece[i * rows : (i + 1) * rows, HEAD:]


def _two_heads(ref, pair):
    first = pl.multiple_of(pair * 2 * HEAD, 2 * HEAD)
    return jnp.concatenate([ref[:, pl.ds(first, HEAD)], ref[:, pl.ds(first + HEAD, HEAD)]])


def _store_heads(ref, pair, value):
    first = pl.multiple_of(pair * 2 * HEAD, 2 * HEAD)
    rows = ref.shape[0]
    ref[:, pl.ds(first, HEAD)] = value[:rows].astype(ref.dtype)
    ref[:, pl.ds(first + HEAD, HEAD)] = value[rows:].astype(ref.dtype)


def _attend_kernel(table, *refs, cores, chunk, rows):
    pieces, refs = refs[:cores], refs[cores:]
    q_ref, at_ref, opens_ref, o_ref, l_ref, bias_ref, k_ref, v_ref = refs

    @pl.when(pl.program_id(0) == 0)
    def _():
        _place_keys(table, pieces, k_ref, v_ref, rows)
        v_ref[:, HEAD:] = jnp.ones((v_ref.shape[0], HEAD), BF)

    number = pl.program_id(0)
    for n in range(STEPS):

        @pl.when(number == n)
        def _(n=n):
            keys, masked = _spans(n, chunk)
            _mask_bias(at_ref, opens_ref, bias_ref, masked, keys)

            def pair_of_heads(pair, carry):
                query = _two_heads(q_ref, pair)
                out = None
                for low in range(0, keys, chunk):
                    s = times_transposed(query, k_ref[low : low + chunk, :])
                    if low >= masked:
                        s = s + bias_ref[:, low : low + chunk]
                    o = jnp.dot(
                        jnp.exp2(s).astype(BF),
                        v_ref[low : low + chunk, :],
                        preferred_element_type=F32,
                    )
                    out = o if out is None else out + o
                total = out[:, HEAD:]
                _store_heads(o_ref, pair, out[:, :HEAD] / total)
                log_total = jnp.log2(total)
                l_ref[2 * pair] = log_total[:rows]
                l_ref[2 * pair + 1] = log_total[rows:]
                return carry

            lax.fori_loop(0, q_ref.shape[1] // (2 * HEAD), pair_of_heads, 0, unroll=2)


def attend(table, queries, pieces, query_at, opens, rows):
    tokens, width = queries.shape
    heads, cores = width // HEAD, len(pieces)
    group = cores * tokens
    chunk = group // STEPS
    column = pl.BlockSpec((rows, 1), lambda i, o: (i, 0))
    tile = pl.BlockSpec((rows, width), lambda i, o: (i, 0))
    return run(
        partial(_attend_kernel, cores=cores, chunk=chunk, rows=rows),
        "attend",
        (STEPS,),
        (*pieces, queries, query_at, opens),
        [full(tokens, 2 * HEAD)] * cores + [tile, column, column],
        [((tokens, width), BF), ((heads, tokens, HEAD), F32)],
        [tile, pl.BlockSpec((heads, rows, HEAD), lambda i, o: (0, i, 0))],
        scalars=table,
        scratch=[
            pltpu.VMEM((2 * rows, group), F32),
            pltpu.VMEM((group, HEAD), BF),
            pltpu.VMEM((group, 2 * HEAD), BF),
        ],
    )


def _beside(value, column):
    high = column.astype(BF)
    low = (column - high.astype(F32)).astype(BF)
    lane = lax.broadcasted_iota(jnp.int32, value.shape, 1)
    zero = jnp.zeros(value.shape, BF)
    extra = jnp.where(lane == 0, -high, jnp.where(lane == 1, -low, zero))
    return jnp.concatenate([value, extra], axis=1)


def _attend_back_kernel(table, *refs, cores, chunk, rows):
    pieces, refs = refs[:cores], refs[cores:]
    q_ref, do_ref, o_ref, l_ref, at_ref, opens_ref, dq_ref = refs[:7]
    sums, refs = refs[7 : 7 + cores], refs[7 + cores :]
    bias_ref, k_ref, v_ref, dk_ref, dv_ref = refs

    @pl.when(pl.program_id(0) == 0)
    def _():
        _place_keys(table, pieces, k_ref, v_ref, rows)
        ones = jnp.ones((k_ref.shape[0], HEAD), BF)
        k_ref[:, HEAD:] = ones
        v_ref[:, HEAD:] = ones
        dk_ref[...] = jnp.zeros_like(dk_ref)
        dv_ref[...] = jnp.zeros_like(dv_ref)

    number = pl.program_id(0)
    for n in range(STEPS):

        @pl.when(number == n)
        def _(n=n):
            keys, masked = _spans(n, chunk)
            _mask_bias(at_ref, opens_ref, bias_ref, masked, keys)

            def pair_of_heads(pair, carry):
                query, grad = _two_heads(q_ref, pair), _two_heads(do_ref, pair)
                out = _two_heads(o_ref, pair)
                centre = jnp.sum(grad.astype(F32) * out.astype(F32), axis=-1, keepdims=True)
                log_total = jnp.concatenate([l_ref[2 * pair], l_ref[2 * pair + 1]])
                query_wide = _beside(query, log_total)
                grad_wide = _beside(grad, jnp.broadcast_to(centre, grad.shape))
                dq = None
                for low in range(0, keys, chunk):
                    span = slice(low, low + chunk)
                    s = times_transposed(query_wide, k_ref[span, :])
                    if low >= masked:
                        s = s + bias_ref[:, span]
                    p = jnp.exp2(s)
                    ds = (p * times_transposed(grad_wide, v_ref[span, :])).astype(BF)
                    dv_ref[span, :] += contract_rows(p.astype(BF), grad)
                    dk_ref[span, :] += contract_rows(ds, query)
                    part = jnp.dot(ds, k_ref[span, :HEAD], preferred_element_type=F32)
                    dq = part if dq is None else dq + part
                _store_heads(dq_ref, pair, dq)
                return carry

            lax.fori_loop(0, q_ref.shape[1] // (2 * HEAD), pair_of_heads, 0)

    @pl.when(number == STEPS - 1)
    def _():
        for k, piece in enumerate(sums):
            for i in range(STEPS):
                place = pl.ds(pl.multiple_of(table[k * STEPS + i], rows), rows)
                piece[i * rows : (i + 1) * rows, :HEAD] = dk_ref[place, :] * (1.0 / LOG2E)
                piece[i * rows : (i + 1) * rows, HEAD:] = dv_ref[place, :]


def attend_back(table, queries, grads, mixed, log_totals, pieces, query_at, opens, rows):
    tokens, width = queries.shape
    heads, cores = width // HEAD, len(pieces)
    group = cores * tokens
    chunk = group // STEPS
    piece = full(tokens, 2 * HEAD)
    column = pl.BlockSpec((rows, 1), lambda i, o: (i, 0))
    tile = pl.BlockSpec((rows, width), lambda i, o: (i, 0))
    return run(
        partial(_attend_back_kernel, cores=cores, chunk=chunk, rows=rows),
        "attend_back",
        (STEPS,),
        (*pieces, queries, grads, mixed, log_totals, query_at, opens),
        [piece] * cores
        + [tile, tile, tile, pl.BlockSpec((heads, rows, HEAD), lambda i, o: (0, i, 0))]
        + [column, column],
        [((tokens, width), BF)] + [((tokens, 2 * HEAD), F32)] * cores,
        [tile] + [piece] * cores,
        scalars=table,
        scratch=[
            pltpu.VMEM((2 * rows, group), F32),
            pltpu.VMEM((group, 2 * HEAD), BF),
            pltpu.VMEM((group, 2 * HEAD), BF),
            pltpu.VMEM((group, HEAD), F32),
            pltpu.VMEM((group, HEAD), F32),
        ],
    )


def _expert_kernel(
    x_ref, pulled_ref, chosen_ref, own_ref, router_ref, gate_ref, up_ref,
    dx_ref, dg_ref, du_ref, h_ref, c_ref,
):
    rows = x_ref[...]
    logits = jnp.dot(rows, router_ref[...], preferred_element_type=F32)
    chosen = chosen_ref[...].astype(F32)
    logits = jnp.where(chosen > 0.0, logits, -1e30)
    raised = jnp.exp(logits - jnp.max(logits, axis=-1, keepdims=True)) * chosen
    weight = jnp.sum(raised * own_ref[...], axis=-1, keepdims=True)
    weight = weight / jnp.maximum(jnp.sum(raised, axis=-1, keepdims=True), 1e-30)
    gate = jnp.dot(rows, gate_ref[...], preferred_element_type=F32)
    up = jnp.dot(rows, up_ref[...], preferred_element_type=F32)
    sigma = jax.nn.sigmoid(gate)
    swish = gate * sigma
    hidden = swish * up
    pulled = pulled_ref[...].astype(F32)
    c_ref[...] = jnp.sum(hidden * pulled, axis=-1, keepdims=True)
    h_ref[...] = (weight * hidden).astype(BF)
    pulled = weight * pulled
    gate_grad = (pulled * up * sigma * (1.0 + gate * (1.0 - sigma))).astype(BF)
    up_grad = (pulled * swish).astype(BF)
    dg_ref[...] = gate_grad
    du_ref[...] = up_grad
    dx = times_transposed(gate_grad, gate_ref[...]) + times_transposed(up_grad, up_ref[...])
    dx_ref[...] = dx.astype(BF)


def expert(rows, pulled, chosen, own, router, gate, up):
    count, width = rows.shape
    hidden = gate.shape[1]
    lanes = chosen.shape[1]
    step = min(count, 256)
    across = pl.BlockSpec((step, width), lambda i: (i, 0))
    thin = pl.BlockSpec((step, hidden), lambda i: (i, 0))
    column = pl.BlockSpec((step, 1), lambda i: (i, 0))
    return run(
        _expert_kernel,
        "expert",
        (count // step,),
        (rows, pulled, chosen, own, router, gate, up),
        [across, thin, pl.BlockSpec((step, lanes), lambda i: (i, 0)), full(1, lanes)]
        + [full(width, lanes), full(width, hidden), full(width, hidden)],
        [((count, width), BF)] + [((count, hidden), BF)] * 3 + [((count, 1), F32)],
        [across, thin, thin, thin, column],
    )


def _rows_kernel(*refs):
    count = (len(refs) - 1) // 2
    total = None
    for left, right in zip(refs[:count], refs[count:-1]):
        part = contract_rows(left[...], right[...])
        total = part if total is None else total + part
    refs[-1][...] = total


def contract_chunks(lefts, rights):
    count, tall = lefts[0].shape
    wide = rights[0].shape[1]
    step = min(tall, 256)
    return run(
        _rows_kernel,
        "contract_chunks",
        (tall // step,),
        (*lefts, *rights),
        [pl.BlockSpec((count, step), lambda i: (0, i))] * len(lefts)
        + [full(count, wide)] * len(rights),
        [((tall, wide), F32)],
        [pl.BlockSpec((step, wide), lambda i: (i, 0))],
    )[0]


def body(
    layer_input,
    attn_gain,
    w_query,
    key_matrix,
    value_matrix,
    query_gain,
    key_gain,
    w_out,
    moe_gain,
    router,
    expert_gate,
    expert_up,
    expert_down,
    expert_ids,
    cont_segment,
    out_grad,
):
    tokens, width = layer_input.shape
    dps, _, cores = sizes = [lax.axis_size(a) for a in ALL]
    devices = math.prod(sizes)
    dp, z, c = [lax.axis_index(a) for a in ALL]
    experts = router.shape[1]
    capacity = tokens * TOP // experts
    plane = dps * cores
    slots = plane * capacity
    order = jnp.array(ORDER, jnp.int32)[z]
    where_block = jnp.array([[o.index(b) for b in range(STEPS)] for o in ORDER], jnp.int32)[z]
    own_heads = HQ // (STEPS * cores)
    heads = HQ // STEPS
    head_cols = heads * HEAD
    own_cols = own_heads * HEAD

    rows_dev = router.shape[0]
    id_cols = tokens * TOP // rows_dev
    router_pad = -(experts + 2 + id_cols) % 128
    small = jnp.concatenate(
        [
            router,
            attn_gain[:, None],
            moe_gain[:, None],
            expert_ids.astype(BF).reshape(rows_dev, id_cols),
            jnp.zeros((rows_dev, router_pad), BF),
        ],
        axis=1,
    )
    packed = jnp.concatenate(
        [
            key_matrix.reshape(rows_dev, STEPS, HEAD).transpose(1, 0, 2),
            value_matrix.reshape(rows_dev, STEPS, HEAD).transpose(1, 0, 2),
            jnp.broadcast_to(small[None], (STEPS, *small.shape)),
        ],
        axis=2,
    )
    flat = [(b, (b % dps) * (devices // dps) + b // dps) for b in range(devices)]
    w_back = lax.ppermute(w_out, ALL, flat)
    query_own = from_dps(w_query, dp).reshape(width, own_cols)
    packed = lax.all_to_all(packed, "z", split_axis=0, concat_axis=0, tiled=True)
    packed, w_back, own_input, order, where_block = hold(
        packed, w_back, layer_input, order, where_block
    )
    arrived = lax.all_gather(own_input, "z", axis=0, tiled=True)
    w_back = lax.all_gather(w_back, PLANE, axis=0, tiled=True)

    at_slot = jnp.arange(capacity, dtype=jnp.int32)
    earlier = (jnp.arange(tokens)[:, None] > jnp.arange(tokens)[None, :]).astype(BF)

    def plan(ids):
        chosen = jnp.any(ids[:, :, None] == jnp.arange(experts, dtype=jnp.int32), axis=1)
        ranks = jnp.dot(earlier, chosen.astype(BF), preferred_element_type=F32).astype(jnp.int32)
        ranks = jnp.where(chosen & (ranks < capacity), ranks, -1)
        in_plane = lax.dynamic_index_in_dim(
            ranks.reshape(tokens, dps, STEPS, cores), z, 2, keepdims=False
        ).reshape(tokens, plane)
        pick = (in_plane[:, :, None] == at_slot).reshape(tokens, slots).astype(BF)
        back = (in_plane.T[:, None, :] == at_slot[:, None]).reshape(slots, tokens).astype(BF)
        return chosen, ranks, pick, back

    def to_plane(rows):
        return lax.all_to_all(rows, PLANE, split_axis=0, concat_axis=0, tiled=True)

    zs = jnp.stack([z, jnp.int32(0)])
    own_chosen, own_ranks, own_pick, own_back = plan(expert_ids)
    own_slots = own_ranks[:, :, None] == at_slot
    first_id = 2 * HEAD + experts + 2
    ids = packed[:, :, first_id : first_id + id_cols].astype(jnp.int32)
    ids = ids.reshape(STEPS, tokens, TOP)
    ids = [lax.dynamic_index_in_dim(ids, order[i], 0, keepdims=False) for i in range(STEPS)]
    packed = jnp.stack(cores_in_order(packed, c), axis=1).reshape(w_query.shape[0], -1)
    packed = from_dps(packed, dp).reshape(width, -1)
    w_in = cores_in_order(query_own, c)
    *w_in, packed, ids, upstream_block = hold(*w_in, packed, ids, out_grad)
    g0 = to_plane(dispatch(zs, own_back, [upstream_block], (0, 0, 0, 0)))
    rest = packed[:, 2 * HEAD :]
    lanes = rest.shape[1]
    router_all = rest[:, :experts]
    attn_gain_all = rest[:, experts].astype(F32)[None, :]
    moe_gain_all = rest[:, experts + 1].astype(F32)[None, :]
    w_in = jnp.concatenate([*w_in, packed[:, : 2 * HEAD]], axis=1)
    plans = [(own_chosen, own_ranks, own_pick, own_back)] + [plan(i) for i in ids[1:]]
    pick = [p[2] for p in plans]
    back = [p[3] for p in plans]
    slot_chosen = jnp.stack(
        [
            jnp.dot(back[i], jnp.pad(p[0].astype(BF), ((0, 0), (0, lanes - experts))))
            for i, p in enumerate(plans)
        ]
    ).reshape(STEPS, plane, capacity, lanes)
    slot_chosen = slot_chosen.transpose(1, 0, 2, 3)
    own_expert = dp * (STEPS * cores) + z * cores + c
    own_expert = (jnp.arange(lanes)[None, :] == own_expert).astype(F32)

    where_at, opens = group_layout(cont_segment[0])
    group = where_at.shape[0]

    def own_rows(table):
        mine = lax.dynamic_index_in_dim(table.reshape(STEPS, cores, tokens), c, 1, keepdims=False)
        return mine.reshape(-1)

    cosine, sine = angle_tables(own_rows(where_at), HEAD)
    query_at = own_rows(jnp.arange(group, dtype=jnp.int32))[:, None]
    opens = own_rows(opens)[:, None]
    numbers = jnp.arange(STEPS, dtype=jnp.int32)
    table = jnp.concatenate([(numbers * cores + (c + k) % cores) * tokens for k in range(cores)])
    query_gain_f = query_gain.astype(F32)[None, :]
    key_gain_f = key_gain.astype(F32)[None, :]
    scale = LOG2E / math.sqrt(HEAD)
    query_gain_s = query_gain_f * scale
    gate_w, up_w, down_w = expert_gate[0], expert_up[0], expert_down[0]
    at_block = [jnp.stack([z, order[i]]) for i in range(STEPS)]

    (
        arrived, upstream_block, w_in, pick, back, slot_chosen, cosine, sine, query_at, opens, table,
        query_gain_s, key_gain_f, at_block, own_expert, attn_gain_all, moe_gain_all, g0,
    ) = hold(
        arrived, upstream_block, w_in, pick, back, slot_chosen, cosine, sine, query_at, opens, table,
        query_gain_s, key_gain_f, at_block, own_expert, attn_gain_all, moe_gain_all, g0,
    )
    g_up, g_down = spread_first(upstream_block)
    normed, raw, queries, key_value_rows = project(
        arrived, attn_gain_all, w_in, cosine, sine, query_gain_s, key_gain_f, tokens
    )
    pieces = [key_value_rows, *other_cores(key_value_rows)]
    pulled0 = matmul(g0, down_w, "nt", 2, "rows", F32)
    queries, g_up, g_down, pulled0, *pieces = hold(queries, g_up, g_down, pulled0, *pieces)
    g_up2, g_down2 = spread_second(g_up, g_down)
    g1 = to_plane(dispatch(zs, back[1], [g_up, g_down], FIRST))
    mixed, log_totals = attend(table, queries, pieces, query_at, opens, tokens)
    mixed, g1, w_back, g_up2, g_down2 = hold(mixed, g1, w_back, g_up2, g_down2)
    g_last = spread_third(g_up2, g_down2, z)
    w_back = w_back.reshape(dps, cores, -1, width).transpose(1, 0, 2, 3).reshape(head_cols, width)
    attended = matmul(mixed, w_back, "nn", 4, "columns")
    attended, g1, g_up2, g_down2, g_last = hold(attended, g1, g_up2, g_down2, g_last)
    attended = lax.psum_scatter(attended, "z", scatter_dimension=0, tiled=True)
    g2 = to_plane(dispatch(zs, back[2], [g_up, g_down, g_up2, g_down2], SECOND))
    pulled1 = matmul(g1, down_w, "nt", 2, "rows", F32)
    g2, g_last, pulled1 = hold(g2, g_last, pulled1)
    g3 = to_plane(dispatch(zs, back[3], [g_up2, g_down2, g_last], THIRD))
    pulled2 = matmul(g2, down_w, "nt", 2, "rows", F32)
    g3, pulled2, slot_chosen = hold(g3, pulled2, slot_chosen)
    slot_chosen = to_plane(slot_chosen)
    slot_chosen = slot_chosen.transpose(1, 0, 2, 3).reshape(STEPS, slots, lanes)
    pulled3 = matmul(g3, down_w, "nt", 2, "rows", F32)
    attended, pulled3, slot_chosen = hold(attended, pulled3, slot_chosen)
    upstream_slots = [g0, g1, g2, g3]
    resid, moe_low = add_and_norm(layer_input, moe_gain_all, (attended,))

    def through(i, rows, pulled):
        return expert(rows, pulled, slot_chosen[i], own_expert, rest, gate_w, up_w)

    m_up, m_down = spread_first(moe_low)
    r0 = to_plane(dispatch(zs, back[0], [moe_low], (0, 0, 0, 0)))
    m_up, m_down = hold(m_up, m_down)
    m_up2, m_down2 = spread_second(m_up, m_down)
    r1 = dispatch(zs, back[1], [m_up, m_down], FIRST)
    r1, r0 = hold(r1, r0)
    r1 = to_plane(r1)
    e0 = through(0, r0, pulled0)
    m_up2, m_down2, e0 = hold(m_up2, m_down2, e0)
    m_last = spread_third(m_up2, m_down2, z)
    r2 = dispatch(zs, back[2], [m_up, m_down, m_up2, m_down2], SECOND)
    r2, r1 = hold(r2, r1)
    r2 = to_plane(r2)
    e1 = through(1, r1, pulled1)
    m_last, e1 = hold(m_last, e1)
    r3 = dispatch(zs, back[3], [m_up2, m_down2, m_last], THIRD)
    r3, r2 = hold(r3, r2)
    r3 = to_plane(r3)
    e2 = through(2, r2, pulled2)
    r3, e2 = hold(r3, e2)
    e3 = through(3, r3, pulled3)
    rows = [r0, r1, r2, r3]
    slot_grads, gate_grads, up_grads, hiddens, centres = [list(v) for v in zip(e0, e1, e2, e3)]
    d0, d1, d2, d3 = slot_grads
    b3 = to_plane(d3)
    moe_row, d2, centres, hiddens = hold(moe_low, d2, centres, hiddens)
    logits = jnp.dot(moe_row, router_all, preferred_element_type=F32)
    logits = jnp.where(own_chosen, logits, -jnp.inf)
    raised = jnp.exp(logits - jnp.max(logits, axis=-1, keepdims=True))
    gates = raised / jnp.sum(raised, axis=-1, keepdims=True)
    stacked = jnp.stack([v.reshape(dps, cores, capacity) for v in centres])
    centre_back = jnp.stack(
        [
            lax.dynamic_index_in_dim(stacked, where_block[b], 0, keepdims=False)
            for b in range(STEPS)
        ],
        axis=1,
    ).reshape(experts, capacity)
    p3, p2, p1, p0 = [matmul(hiddens[i], down_w, "nn", 4, "columns") for i in (3, 2, 1, 0)]
    b3, d2, p3, p2, p1, p0, centre_back, gates = hold(
        b3, d2, p3, p2, p1, p0, centre_back, gates
    )
    (c3,) = line_part(zs, pick[3], b3, tokens)
    c3, d2 = hold(c3, d2)
    got = sum_first(c3)
    b2 = to_plane(d2)
    got, b2, d1 = hold(got, b2, d1)
    c2, middle = line_part(zs, pick[2], b2, tokens, 1, (c3, got))
    middle, c2, d1 = hold(middle, c2, d1)
    s_up, s_down = sum_second(middle)
    b1 = to_plane(d1)
    s_up, s_down, b1, centre_back, d0 = hold(s_up, s_down, b1, centre_back, d0)
    s_up, s_down = line_part(zs, pick[1], b1, tokens, 2, (c2, s_up, s_down))
    s_up, s_down, d0, centre_back = hold(s_up, s_down, d0, centre_back)
    s_up, s_down = sum_third(s_up, s_down)
    b0 = to_plane(d0)
    b0, centre_back = hold(b0, centre_back)
    centre_back = lax.all_to_all(centre_back, ALL, split_axis=0, concat_axis=0, tiled=True)
    (c0,) = line_part(zs, pick[0], b0, tokens)
    weight_grad = jnp.sum(jnp.where(own_slots, centre_back[None], 0.0), axis=2)
    logit_grad = (
        gates * (weight_grad - jnp.sum(gates * weight_grad, axis=-1, keepdims=True))
    ).astype(BF)
    logit_wide = jnp.pad(logit_grad, ((0, 0), (0, lanes - experts)))
    s_up, s_down, c0, logit_wide = hold(s_up, s_down, c0, logit_wide)
    resid_grad, resid_low, moe_gain_grad = norm_back(
        resid, moe_gain_all, out_grad, (c0, s_up, s_down), logit_wide, rest
    )

    def by_core(value, axis):
        size = value.shape[axis] // cores
        return [
            lax.dynamic_slice_in_dim(value, (c + k) % cores * size, size, axis)
            for k in range(cores)
        ]

    resid_low, p3, logit_grad, hiddens, rows = hold(resid_low, p3, logit_grad, hiddens, rows)
    resid_all = lax.all_gather(resid_low, "z", axis=0, tiled=True)
    o3 = to_plane(p3)
    down_weight_grad = contract_chunks(hiddens, upstream_slots)
    router_grad = contract_rows(moe_low, logit_grad)
    o3, p2, rows, down_weight_grad, router_grad = hold(
        o3, p2, rows, down_weight_grad, router_grad
    )
    (o3,) = line_part(zs, pick[3], o3, tokens)
    t_got = sum_first(o3)
    o2 = to_plane(p2)
    up_weight_grad = contract_chunks(rows, up_grads)
    o2, o3, t_got, p1, rows, up_weight_grad = hold(o2, o3, t_got, p1, rows, up_weight_grad)
    o2, middle = line_part(zs, pick[2], o2, tokens, 1, (o3, t_got))
    middle, o2, p1 = hold(middle, o2, p1)
    t_up, t_down = sum_second(middle)
    o1 = to_plane(p1)
    gate_weight_grad = contract_chunks(rows, gate_grads)
    resid_all, o2, gate_weight_grad = hold(resid_all, o2, gate_weight_grad)
    mixed_grad = matmul(resid_all, w_back, "nt", 4, "rows")
    mixed_grad, resid_all = hold(mixed_grad, resid_all)
    out_weight_grad = matmul(mixed, resid_all, "tn", 4, "columns")
    out_weight_grad = out_weight_grad.reshape(cores, dps, -1, width).transpose(1, 0, 2, 3)
    out_weight_grad = out_weight_grad.reshape(head_cols, width)
    mixed_grad, t_up, t_down, o1, o2, p0, out_weight_grad = hold(
        mixed_grad, t_up, t_down, o1, o2, p0, out_weight_grad
    )
    out_weight_grad = lax.psum_scatter(out_weight_grad, PLANE, scatter_dimension=0, tiled=True)
    t_up, t_down = line_part(zs, pick[1], o1, tokens, 2, (o2, t_up, t_down))
    t_up, t_down, p0 = hold(t_up, t_down, p0)
    t_up, t_down = sum_third(t_up, t_down)
    o0 = to_plane(p0)
    query_grads, *sums = attend_back(
        table, queries, mixed_grad, mixed, log_totals, pieces, query_at, opens, tokens
    )
    query_grads, t_up, t_down, o0, out_weight_grad, *sums = hold(
        query_grads, t_up, t_down, o0, out_weight_grad, *sums
    )
    out_weight_grad = lax.ppermute(out_weight_grad, ALL, [(b, a) for a, b in flat]).astype(F32)
    sums = sum_over_cores(sums)
    normed_grad, raw_grad, query_gain_grad, key_gain_grad = project_back(
        raw, query_grads, sums, w_in, cosine, sine, query_gain_f, key_gain_f, tokens
    )
    normed_grad, raw_grad, o0, out_weight_grad = hold(normed_grad, raw_grad, o0, out_weight_grad)
    normed_sum = lax.psum_scatter(normed_grad, "z", scatter_dimension=0, tiled=True)
    in_grad = matmul(normed, raw_grad, "tn", 4, "rows")
    inputs = arrived.astype(F32)
    input_factor = lax.rsqrt(jnp.mean(inputs * inputs, axis=-1, keepdims=True) + EPS)
    attn_gain_grad = jnp.sum(normed_grad.astype(F32) * inputs * input_factor, axis=0)[None, :]
    query_share = sum_over_cores(by_core(in_grad[:, :head_cols], 1)).astype(BF)
    key_value_grad = in_grad[:, head_cols:].reshape(dps, STEPS, cores, rows_dev, 2 * HEAD)
    key_value_grad = sum_over_cores(
        [part[:, :, 0] for part in by_core(key_value_grad, 2)]
    ).astype(BF)
    query_share, key_value_grad, o0, attn_gain_grad = hold(
        query_share, key_value_grad, o0, attn_gain_grad
    )
    query_weight_grad = over_dps(query_share.reshape(dps, -1, own_cols), dp)
    key_value_grad = over_dps(key_value_grad, dp).astype(BF)
    (o0,) = line_part(zs, pick[0], o0, tokens)
    output = resid + (o0.astype(F32) + t_up.astype(F32) + t_down.astype(F32))
    output = output.astype(BF)

    def to_owners(value):
        columns = value.shape[0]
        split = value.reshape(columns, devices, rows_dev).transpose(1, 0, 2)
        return split.reshape(devices, columns * rows_dev)

    gain_row = jnp.concatenate([query_gain_grad, key_gain_grad], axis=1)
    late = jnp.concatenate(
        [
            to_owners(jnp.concatenate([router_grad.T, moe_gain_grad, attn_gain_grad])),
            jnp.broadcast_to(gain_row, (devices, 2 * HEAD)),
        ],
        axis=1,
    )
    late = jnp.sum(lax.all_to_all(late, ALL, split_axis=0, concat_axis=0, tiled=True), axis=0)
    gain_sums = late[-2 * HEAD :].reshape(2, HEAD)
    owned = late[: -2 * HEAD].reshape(experts + 2, rows_dev)
    key_value_grad = lax.all_to_all(key_value_grad, "z", split_axis=0, concat_axis=0, tiled=True)
    key_value_grad = key_value_grad.transpose(1, 0, 2).astype(F32)
    key_weight_grad = key_value_grad[:, :, :HEAD].reshape(rows_dev, -1)
    value_weight_grad = key_value_grad[:, :, HEAD:].reshape(rows_dev, -1)
    (input_grad,) = norm_back(layer_input, attn_gain_all, resid_grad, (normed_sum,))
    return (
        output,
        input_grad,
        owned[experts + 1],
        query_weight_grad,
        key_weight_grad,
        value_weight_grad,
        gain_sums[0],
        gain_sums[1],
        out_weight_grad,
        owned[experts],
        owned[:experts].T,
        gate_weight_grad[None],
        up_weight_grad[None],
        down_weight_grad[None],
    )


def solution(mesh):
    dps, sequence = mesh.devices.shape
    inner = Mesh(mesh.devices.reshape(dps, STEPS, sequence // STEPS), ALL)
    rows = P(ALL, None)
    placed = (
        rows,
        P(ALL),
        P("dp", ("z", "core")),
        rows,
        rows,
        P(),
        P(),
        rows,
        P(ALL),
        rows,
        P(ALL, None, None),
        P(ALL, None, None),
        P(ALL, None, None),
        rows,
        P("dp", None),
        rows,
    )
    return jax.shard_map(
        body,
        mesh=inner,
        in_specs=placed,
        out_specs=(
            rows,
            rows,
            P(ALL),
            P("dp", ("z", "core")),
            rows,
            rows,
            P(),
            P(),
            rows,
            P(ALL),
            rows,
            P(ALL, None, None),
            P(ALL, None, None),
            P(ALL, None, None),
        ),
        check_vma=False,
    )
```

```python
from functools import partial
import math

import jax
import jax.numpy as jnp
from jax import lax
from jax.experimental import pallas as pl
from jax.experimental.pallas import tpu as pltpu
from jax.sharding import Mesh, PartitionSpec as P

HQ = 32
KEY_VALUE_HEADS = 4
TOP = 8
PROMPT = 1024
NCONT = 4
HEAD = 128

EPS = 1e-06
THETA = 1000000.0
LOG2E = 1.4426950408889634
BF = jnp.bfloat16
F32 = jnp.float32

STEPS = 4
ORDER = ((0, 1, 2, 3), (1, 0, 2, 3), (2, 3, 1, 0), (3, 2, 1, 0))
PLANE = ("dp", "core")
ALL = ("dp", "z", "core")


def angle_tables(where_at, head_width):
    ranks = jnp.arange(head_width // 2, dtype=F32) * (2.0 / head_width)
    inverse = jnp.exp(-ranks * math.log(THETA))
    angles = where_at.astype(F32)[:, None] * inverse[None, :]
    cosine, sine = jnp.cos(angles), jnp.sin(angles)
    return (
        jnp.concatenate([cosine, cosine], axis=-1),
        jnp.concatenate([-sine, sine], axis=-1),
    )


def group_layout(segment):
    length = segment.shape[0]
    one_hot = (segment[:, None] == jnp.arange(NCONT, dtype=jnp.int32)[None, :]).astype(jnp.int32)
    counted = jnp.sum(one_hot, axis=0)
    before = jnp.arange(NCONT)[:, None] > jnp.arange(NCONT)[None, :]
    starts = jnp.sum(jnp.where(before, counted[None, :], 0), axis=1)
    begins = jnp.sum(one_hot * starts[None, :], axis=1)
    within = jnp.arange(length, dtype=jnp.int32) - begins
    where_at = jnp.concatenate([jnp.arange(PROMPT, dtype=jnp.int32), PROMPT + within])
    opens = jnp.concatenate([jnp.full((PROMPT,), PROMPT, jnp.int32), PROMPT + begins])
    return (where_at, opens)


def contract_rows(left, right):
    return lax.dot_general(left, right, (((0,), (0,)), ((), ())), preferred_element_type=F32)


def times_transposed(left, right):
    return lax.dot_general(left, right, (((1,), (1,)), ((), ())), preferred_element_type=F32)


def hold(*values):
    return lax.optimization_barrier(values)


def spread_first(block):
    return (
        lax.ppermute(block, "z", [(0, 1), (1, 2), (2, 3)]),
        lax.ppermute(block, "z", [(1, 0), (2, 1), (3, 2)]),
    )


def spread_second(up, down):
    return (
        lax.ppermute(up, "z", [(1, 2), (2, 3)]),
        lax.ppermute(down, "z", [(2, 1), (1, 0)]),
    )


def spread_third(up2, down2, z):
    return lax.ppermute(jnp.where(z == 2, up2, down2), "z", [(2, 3), (1, 0)])


FIRST = (1, 0, 1, 0)
SECOND = (3, 1, 0, 2)
THIRD = (2, 1, 0, 2)


def sum_first(third):
    return lax.ppermute(third, "z", [(0, 1), (3, 2)])


def sum_second(middle):
    return (
        lax.ppermute(middle, "z", [(0, 1), (1, 2)]),
        lax.ppermute(middle, "z", [(3, 2), (2, 1)]),
    )


def sum_third(up, down):
    return (
        lax.ppermute(up, "z", [(0, 1), (1, 2), (2, 3)]),
        lax.ppermute(down, "z", [(3, 2), (2, 1), (1, 0)]),
    )


def over_dps(value, dp):
    dps = value.shape[0]
    total = lax.dynamic_index_in_dim(value, dp, 0, keepdims=False).astype(F32)
    for k in range(1, dps):
        piece = lax.dynamic_index_in_dim(value, dp ^ k, 0, keepdims=False)
        total = total + lax.ppermute(piece, "dp", [(i, i ^ k) for i in range(dps)]).astype(F32)
    return total


def from_dps(value, dp):
    dps = lax.axis_size("dp")
    whole = jnp.zeros((dps, *value.shape), value.dtype)
    whole = lax.dynamic_update_index_in_dim(whole, value, dp, 0)
    for k in range(1, dps):
        got = lax.ppermute(value, "dp", [(i, i ^ k) for i in range(dps)])
        whole = lax.dynamic_update_index_in_dim(whole, got, dp ^ k, 0)
    return whole


def other_cores(value):
    cores = lax.axis_size("core")
    return [
        lax.ppermute(value, "core", [((i + k) % cores, i) for i in range(cores)])
        for k in range(1, cores)
    ]


def cores_in_order(value, c):
    cores = lax.axis_size("core")
    pieces = [value, *other_cores(value)]
    ordered = []
    for n in range(cores):
        piece = pieces[0]
        for k in range(1, cores):
            piece = jnp.where((n - c) % cores == k, pieces[k], piece)
        ordered.append(piece)
    return ordered


def sum_over_cores(pieces):
    cores = lax.axis_size("core")
    total = pieces[0].astype(F32)
    for k in range(1, cores):
        got = lax.ppermute(pieces[k], "core", [(i, (i + k) % cores) for i in range(cores)])
        total = total + got.astype(F32)
    return total


CHEAP = pl.CostEstimate(flops=1, bytes_accessed=1, transcendentals=0)
DEAR = pl.CostEstimate(flops=10**11, bytes_accessed=1, transcendentals=0)


def run(kernel, name, grid, operands, in_specs, outs, out_specs, scalars=None, scratch=(), free=(), dear=False):
    prefetch = () if scalars is None else (scalars,)
    operands = [
        v if i in free else pltpu.with_memory_space_constraint(v, pltpu.HBM)
        for i, v in enumerate(operands)
    ]
    got = pl.pallas_call(
        kernel,
        grid_spec=pltpu.PrefetchScalarGridSpec(
            num_scalar_prefetch=len(prefetch),
            grid=grid,
            in_specs=in_specs,
            out_specs=out_specs,
            scratch_shapes=scratch,
        ),
        out_shape=[pltpu.HBM(shape, kind) for shape, kind in outs],
        compiler_params=pltpu.CompilerParams(vmem_limit_bytes=52 * 1024 * 1024),
        cost_estimate=DEAR if dear else CHEAP,
        name=name,
    )(*prefetch, *operands)
    return got


def full(*shape):
    return pl.BlockSpec(shape, lambda *_: (0,) * len(shape))


def _matmul_kernel(a_ref, b_ref, o_ref, *, dims):
    part = lax.dot_general(a_ref[...], b_ref[...], (dims, ((), ())), preferred_element_type=F32)
    o_ref[...] = part.astype(o_ref.dtype)


def matmul(a, b, kind, steps, by, out=BF, dear=False):
    dims = {"nn": ((1,), (0,)), "nt": ((1,), (1,)), "tn": ((0,), (0,))}[kind]
    rows = a.shape[1 - dims[0][0]]
    columns = b.shape[1 - dims[1][0]]
    a_spec, b_spec = full(*a.shape), full(*b.shape)
    if by == "rows":
        size = rows // steps
        if kind == "tn":
            a_spec = pl.BlockSpec((a.shape[0], size), lambda i: (0, i))
        else:
            a_spec = pl.BlockSpec((size, a.shape[1]), lambda i: (i, 0))
        o_spec = pl.BlockSpec((size, columns), lambda i: (i, 0))
    else:
        size = columns // steps
        if kind == "nt":
            b_spec = pl.BlockSpec((size, b.shape[1]), lambda i: (i, 0))
        else:
            b_spec = pl.BlockSpec((b.shape[0], size), lambda i: (0, i))
        o_spec = pl.BlockSpec((rows, size), lambda i: (0, i))
    return run(
        partial(_matmul_kernel, dims=dims),
        "matmul_" + kind,
        (steps,),
        (a, b),
        [a_spec, b_spec],
        [((rows, columns), out)],
        [o_spec],
        dear=dear,
    )[0]


def _dispatch_kernel(s_ref, pick_ref, *refs, sources):
    z, rows = s_ref[0], refs[0][...]
    for n in range(1, len(refs) - 1):
        here = False
        for at, source in enumerate(sources):
            if source == n:
                here = here | (z == at)
        rows = jnp.where(here, refs[n][...], rows)
    refs[-1][...] = jnp.dot(pick_ref[...], rows, preferred_element_type=F32).astype(BF)


def dispatch(scalars, pick, blocks, sources):
    slots, tokens = pick.shape
    width = blocks[0].shape[1]
    tile = pl.BlockSpec((tokens, 1024), lambda j, s: (0, j))
    return run(
        partial(_dispatch_kernel, sources=sources),
        "dispatch",
        (width // 1024,),
        (pick, *blocks),
        [full(slots, tokens)] + [tile] * len(blocks),
        [((slots, width), BF)],
        [pl.BlockSpec((slots, 1024), lambda j, s: (0, j))],
        scalars=scalars,
        free=(1, 2, 3, 4),
    )[0]


def _part_kernel(s_ref, a_ref, b_ref, *refs, step):
    z = s_ref[0]
    part = jnp.dot(a_ref[...], b_ref[...], preferred_element_type=F32)
    if step == 0:
        refs[0][...] = part.astype(BF)
    elif step == 1:
        third, got, part_ref, middle_ref = refs
        part_ref[...] = part.astype(BF)
        middle = jnp.where((z == 0) | (z == 3), part, third[...].astype(F32))
        middle_ref[...] = (middle + got[...].astype(F32)).astype(BF)
    else:
        second, up, down, up_ref, down_ref = refs
        other = second[...].astype(F32)
        up_ref[...] = (jnp.where(z == 1, other, part) + up[...].astype(F32)).astype(BF)
        down_ref[...] = (jnp.where(z == 2, other, part) + down[...].astype(F32)).astype(BF)


def line_part(scalars, a, b, tokens, step=0, more=()):
    width = b.shape[1]
    tile = pl.BlockSpec((tokens, 1024), lambda j, s: (0, j))
    return run(
        partial(_part_kernel, step=step),
        "line_part",
        (width // 1024,),
        (a, b, *more),
        [
            pl.BlockSpec((tokens, a.shape[1]), lambda j, s: (s[1], 0)),
            pl.BlockSpec((b.shape[0], 1024), lambda j, s: (0, j)),
        ]
        + [tile] * len(more),
        [((tokens, width), BF)] * (1 if step == 0 else 2),
        [tile] * (1 if step == 0 else 2),
        scalars=scalars,
        free=(1, 2, 3, 4),
    )


def _norm_kernel(x_ref, gain_ref, *refs):
    terms, (resid_ref, low_ref) = refs[:-2], refs[-2:]
    value = x_ref[...].astype(F32)
    for term in terms:
        value = value + term[...].astype(F32)
    resid_ref[...] = value
    factor = lax.rsqrt(jnp.mean(value * value, axis=-1, keepdims=True) + EPS)
    low_ref[...] = (value * factor * gain_ref[...]).astype(BF)


def add_and_norm(x, gain, terms):
    tokens, width = x.shape
    step = min(tokens, 64)
    tile = pl.BlockSpec((step, width), lambda i: (i, 0))
    return run(
        _norm_kernel,
        "add_and_norm",
        (tokens // step,),
        (x, gain, *terms),
        [tile, full(1, width)] + [tile] * len(terms),
        [((tokens, width), F32), ((tokens, width), BF)],
        [tile, tile],
    )


def _norm_back_kernel(v_ref, gain_ref, above_ref, *refs, logits):
    if logits:
        logit_ref, router_ref, *terms, total_ref, low_ref, gain_grad_ref = refs
    else:
        *terms, total_ref = refs
    grad = sum([term[...].astype(F32) for term in terms])
    if logits:
        grad = grad + times_transposed(logit_ref[...], router_ref[...])
    value = v_ref[...].astype(F32)
    factor = lax.rsqrt(jnp.mean(value * value, axis=-1, keepdims=True) + EPS)
    unit = value * factor
    if logits:

        @pl.when(pl.program_id(0) == 0)
        def _():
            gain_grad_ref[...] = jnp.zeros_like(gain_grad_ref)

        gain_grad_ref[...] += jnp.sum(grad * unit, axis=0, keepdims=True)
    grad = grad * gain_ref[...]
    shift = jnp.mean(grad * unit, axis=-1, keepdims=True)
    total = above_ref[...].astype(F32) + factor * (grad - unit * shift)
    total_ref[...] = total
    if logits:
        low_ref[...] = total.astype(BF)


def norm_back(value, gain, above, terms, logit_grad=None, router=None):
    tokens, width = value.shape
    step = min(tokens, 64)
    tile = pl.BlockSpec((step, width), lambda i: (i, 0))
    operands, specs = [value, gain, above], [tile, full(1, width), tile]
    outs, out_specs = [((tokens, width), F32)], [tile]
    if logit_grad is not None:
        lanes = logit_grad.shape[1]
        operands += [logit_grad, router]
        specs += [pl.BlockSpec((step, lanes), lambda i: (i, 0)), full(width, lanes)]
        outs += [((tokens, width), BF), ((1, width), F32)]
        out_specs += [tile, full(1, width)]
    return run(
        partial(_norm_back_kernel, logits=logit_grad is not None),
        "norm_back",
        (tokens // step,),
        (*operands, *terms),
        specs + [tile] * len(terms),
        outs,
        out_specs,
    )


def _pack_kernel(key_ref, value_ref, small_ref, out_ref):
    for at in range(STEPS):
        cols = slice(at * HEAD, (at + 1) * HEAD)
        out_ref[at, :, :HEAD] = key_ref[:, cols]
        out_ref[at, :, HEAD : 2 * HEAD] = value_ref[:, cols]
        out_ref[at, :, 2 * HEAD :] = small_ref[...]


def pack(key, value, small):
    rows = small.shape[0]
    lanes = 2 * HEAD + small.shape[1]
    return run(
        _pack_kernel,
        "pack",
        (1,),
        (key, value, small),
        [full(*key.shape), full(*value.shape), full(*small.shape)],
        [((STEPS, rows, lanes), BF)],
        [full(STEPS, rows, lanes)],
    )[0]


def _lane_mean(value):
    ones = jnp.full((HEAD, HEAD), 1.0 / HEAD, BF)
    return jnp.dot(value.astype(BF), ones, preferred_element_type=F32)


def _project_kernel(
    x_ref, gain_ref, w_ref, cos_ref, sin_ref, qg_ref, kg_ref, n_ref, raw_ref, q_ref, kv_ref
):
    x = x_ref[...].astype(F32)
    factor = lax.rsqrt(jnp.mean(x * x, axis=-1, keepdims=True) + EPS)
    normed = (x * factor * gain_ref[...]).astype(BF)
    n_ref[...] = normed
    raw_ref[...] = jnp.dot(normed, w_ref[...], preferred_element_type=F32)
    cosine, sine = cos_ref[...], sin_ref[...]
    heads = q_ref.shape[1] // HEAD
    for h in range(heads + 1):
        cols = slice(h * HEAD, (h + 1) * HEAD)
        value = raw_ref[:, cols]
        factor = lax.rsqrt(_lane_mean(value * value) + EPS)
        value = value * factor * (qg_ref[...] if h < heads else kg_ref[...])
        value = (value * cosine + pltpu.roll(value, HEAD // 2, 1) * sine).astype(BF)
        if h < heads:
            q_ref[:, cols] = value
        else:
            kv_ref[:, :HEAD] = value
    kv_ref[:, HEAD:] = raw_ref[:, (heads + 1) * HEAD :].astype(BF)


def project(x, gain, w_in, cosine, sine, query_gain, key_gain, rows):
    tokens, width = x.shape
    columns = w_in.shape[1]

    def tile(size):
        return pl.BlockSpec((rows, size), lambda i: (i, 0))

    return run(
        _project_kernel,
        "project",
        (tokens // rows,),
        (x, gain, w_in, cosine, sine, query_gain, key_gain),
        [tile(width), full(1, width), full(width, columns), tile(HEAD), tile(HEAD)]
        + [full(1, HEAD)] * 2,
        [
            ((tokens, width), BF),
            ((tokens, columns), F32),
            ((tokens, columns - 2 * HEAD), BF),
            ((tokens, 2 * HEAD), BF),
        ],
        [tile(width), tile(columns), tile(columns - 2 * HEAD), tile(2 * HEAD)],
        dear=True,
    )


def _project_back_kernel(
    raw_ref, dq_ref, dkv_ref, w_ref, cos_ref, sin_ref, qg_ref, kg_ref, ng_ref, rg_ref, dqg_ref, dkg_ref
):
    @pl.when(pl.program_id(0) == 0)
    def _():
        dqg_ref[...] = jnp.zeros_like(dqg_ref)
        dkg_ref[...] = jnp.zeros_like(dkg_ref)

    cosine, sine = cos_ref[...], sin_ref[...]
    heads = dq_ref.shape[1] // HEAD
    for h in range(heads + 1):
        cols = slice(h * HEAD, (h + 1) * HEAD)
        value = raw_ref[:, cols]
        factor = lax.rsqrt(_lane_mean(value * value) + EPS)
        unit = value * factor
        if h < heads:
            grad = dq_ref[:, cols].astype(F32) * (1.0 / math.sqrt(HEAD))
        else:
            grad = dkv_ref[:, :HEAD]
        grad = grad * cosine + pltpu.roll(grad * sine, HEAD // 2, 1)
        gain_grad = jnp.sum(grad * unit, axis=0, keepdims=True)
        if h < heads:
            dqg_ref[...] += gain_grad
            grad = grad * qg_ref[...]
        else:
            dkg_ref[...] += gain_grad
            grad = grad * kg_ref[...]
        shift = _lane_mean(grad * unit)
        rg_ref[:, cols] = (factor * (grad - unit * shift)).astype(BF)
    rg_ref[:, (heads + 1) * HEAD :] = dkv_ref[:, HEAD:].astype(BF)
    ng_ref[...] = times_transposed(rg_ref[...], w_ref[...]).astype(BF)


def project_back(raw, query_grads, key_value_grads, w_in, cosine, sine, query_gain, key_gain, rows):
    tokens, columns = raw.shape
    width = w_in.shape[0]

    def tile(size):
        return pl.BlockSpec((rows, size), lambda i: (i, 0))

    return run(
        _project_back_kernel,
        "project_back",
        (tokens // rows,),
        (raw, query_grads, key_value_grads, w_in, cosine, sine, query_gain, key_gain),
        [
            tile(columns),
            tile(columns - 2 * HEAD),
            tile(2 * HEAD),
            full(width, columns),
            tile(HEAD),
            tile(HEAD),
            full(1, HEAD),
            full(1, HEAD),
        ],
        [((tokens, width), BF), ((tokens, columns), BF), ((1, HEAD), F32), ((1, HEAD), F32)],
        [tile(width), tile(columns), full(1, HEAD), full(1, HEAD)],
    )


def _mask_bias(at_ref, opens_ref, bias_ref, low, high):
    rows = at_ref.shape[0]
    key_at = low + lax.broadcasted_iota(jnp.int32, (rows, high - low), 1)
    query_at = at_ref[...]
    allowed = (key_at <= query_at) & ((key_at < PROMPT) | (key_at >= opens_ref[...]))
    bias = jnp.where(allowed, 0.0, -1e30).astype(F32)
    bias_ref[:rows, low:high] = bias
    bias_ref[rows:, low:high] = bias


def _spans(number, chunk):
    return (number + 1) * chunk, min(number * chunk, PROMPT)


def _place_keys(table, pieces, k_ref, v_ref, rows):
    for k, piece in enumerate(pieces):
        for i in range(STEPS):
            place = pl.ds(pl.multiple_of(table[k * STEPS + i], rows), rows)
            k_ref[place, :HEAD] = piece[i * rows : (i + 1) * rows, :HEAD]
            v_ref[place, :HEAD] = piece[i * rows : (i + 1) * rows, HEAD:]


def _two_heads(ref, pair):
    first = pl.multiple_of(pair * 2 * HEAD, 2 * HEAD)
    return jnp.concatenate([ref[:, pl.ds(first, HEAD)], ref[:, pl.ds(first + HEAD, HEAD)]])


def _store_heads(ref, pair, value):
    first = pl.multiple_of(pair * 2 * HEAD, 2 * HEAD)
    rows = ref.shape[0]
    ref[:, pl.ds(first, HEAD)] = value[:rows].astype(ref.dtype)
    ref[:, pl.ds(first + HEAD, HEAD)] = value[rows:].astype(ref.dtype)


def _attend_kernel(table, *refs, cores, chunk, rows):
    pieces, refs = refs[:cores], refs[cores:]
    q_ref, at_ref, opens_ref, o_ref, l_ref, bias_ref, k_ref, v_ref = refs

    @pl.when(pl.program_id(0) == 0)
    def _():
        _place_keys(table, pieces, k_ref, v_ref, rows)
        v_ref[:, HEAD:] = jnp.ones((v_ref.shape[0], HEAD), BF)

    number = pl.program_id(0)
    for n in range(STEPS):

        @pl.when(number == n)
        def _(n=n):
            keys, masked = _spans(n, chunk)
            _mask_bias(at_ref, opens_ref, bias_ref, masked, keys)

            def pair_of_heads(pair, carry):
                query = _two_heads(q_ref, pair)
                out = None
                for low in range(0, keys, chunk):
                    s = times_transposed(query, k_ref[low : low + chunk, :])
                    if low >= masked:
                        s = s + bias_ref[:, low : low + chunk]
                    o = jnp.dot(
                        jnp.exp2(s).astype(BF),
                        v_ref[low : low + chunk, :],
                        preferred_element_type=F32,
                    )
                    out = o if out is None else out + o
                total = out[:, HEAD:]
                _store_heads(o_ref, pair, out[:, :HEAD] / total)
                log_total = jnp.log2(total)
                l_ref[2 * pair] = log_total[:rows]
                l_ref[2 * pair + 1] = log_total[rows:]
                return carry

            lax.fori_loop(0, q_ref.shape[1] // (2 * HEAD), pair_of_heads, 0, unroll=2)


def attend(table, queries, pieces, query_at, opens, rows):
    tokens, width = queries.shape
    heads, cores = width // HEAD, len(pieces)
    group = cores * tokens
    chunk = group // STEPS
    column = pl.BlockSpec((rows, 1), lambda i, o: (i, 0))
    tile = pl.BlockSpec((rows, width), lambda i, o: (i, 0))
    return run(
        partial(_attend_kernel, cores=cores, chunk=chunk, rows=rows),
        "attend",
        (STEPS,),
        (*pieces, queries, query_at, opens),
        [full(tokens, 2 * HEAD)] * cores + [tile, column, column],
        [((tokens, width), BF), ((heads, tokens, HEAD), F32)],
        [tile, pl.BlockSpec((heads, rows, HEAD), lambda i, o: (0, i, 0))],
        scalars=table,
        dear=True,
        scratch=[
            pltpu.VMEM((2 * rows, group), F32),
            pltpu.VMEM((group, HEAD), BF),
            pltpu.VMEM((group, 2 * HEAD), BF),
        ],
    )


def _beside(value, column):
    high = column.astype(BF)
    low = (column - high.astype(F32)).astype(BF)
    lane = lax.broadcasted_iota(jnp.int32, value.shape, 1)
    zero = jnp.zeros(value.shape, BF)
    extra = jnp.where(lane == 0, -high, jnp.where(lane == 1, -low, zero))
    return jnp.concatenate([value, extra], axis=1)


def _attend_back_kernel(table, *refs, cores, chunk, rows):
    pieces, refs = refs[:cores], refs[cores:]
    q_ref, do_ref, o_ref, l_ref, at_ref, opens_ref, dq_ref = refs[:7]
    sums, refs = refs[7 : 7 + cores], refs[7 + cores :]
    bias_ref, k_ref, v_ref, dk_ref, dv_ref = refs

    @pl.when(pl.program_id(0) == 0)
    def _():
        _place_keys(table, pieces, k_ref, v_ref, rows)
        ones = jnp.ones((k_ref.shape[0], HEAD), BF)
        k_ref[:, HEAD:] = ones
        v_ref[:, HEAD:] = ones
        dk_ref[...] = jnp.zeros_like(dk_ref)
        dv_ref[...] = jnp.zeros_like(dv_ref)

    number = pl.program_id(0)
    for n in range(STEPS):

        @pl.when(number == n)
        def _(n=n):
            keys, masked = _spans(n, chunk)
            _mask_bias(at_ref, opens_ref, bias_ref, masked, keys)

            def pair_of_heads(pair, carry):
                query, grad = _two_heads(q_ref, pair), _two_heads(do_ref, pair)
                out = _two_heads(o_ref, pair)
                centre = jnp.sum(grad.astype(F32) * out.astype(F32), axis=-1, keepdims=True)
                log_total = jnp.concatenate([l_ref[2 * pair], l_ref[2 * pair + 1]])
                query_wide = _beside(query, log_total)
                grad_wide = _beside(grad, jnp.broadcast_to(centre, grad.shape))
                dq = None
                for low in range(0, keys, chunk):
                    span = slice(low, low + chunk)
                    s = times_transposed(query_wide, k_ref[span, :])
                    if low >= masked:
                        s = s + bias_ref[:, span]
                    p = jnp.exp2(s)
                    ds = (p * times_transposed(grad_wide, v_ref[span, :])).astype(BF)
                    dv_ref[span, :] += contract_rows(p.astype(BF), grad)
                    dk_ref[span, :] += contract_rows(ds, query)
                    part = jnp.dot(ds, k_ref[span, :HEAD], preferred_element_type=F32)
                    dq = part if dq is None else dq + part
                _store_heads(dq_ref, pair, dq)
                return carry

            lax.fori_loop(0, q_ref.shape[1] // (2 * HEAD), pair_of_heads, 0)

    @pl.when(number == STEPS - 1)
    def _():
        for k, piece in enumerate(sums):
            for i in range(STEPS):
                place = pl.ds(pl.multiple_of(table[k * STEPS + i], rows), rows)
                piece[i * rows : (i + 1) * rows, :HEAD] = dk_ref[place, :] * (1.0 / LOG2E)
                piece[i * rows : (i + 1) * rows, HEAD:] = dv_ref[place, :]


def attend_back(table, queries, grads, mixed, log_totals, pieces, query_at, opens, rows):
    tokens, width = queries.shape
    heads, cores = width // HEAD, len(pieces)
    group = cores * tokens
    chunk = group // STEPS
    piece = full(tokens, 2 * HEAD)
    column = pl.BlockSpec((rows, 1), lambda i, o: (i, 0))
    tile = pl.BlockSpec((rows, width), lambda i, o: (i, 0))
    return run(
        partial(_attend_back_kernel, cores=cores, chunk=chunk, rows=rows),
        "attend_back",
        (STEPS,),
        (*pieces, queries, grads, mixed, log_totals, query_at, opens),
        [piece] * cores
        + [tile, tile, tile, pl.BlockSpec((heads, rows, HEAD), lambda i, o: (0, i, 0))]
        + [column, column],
        [((tokens, width), BF)] + [((tokens, 2 * HEAD), F32)] * cores,
        [tile] + [piece] * cores,
        scalars=table,
        dear=True,
        scratch=[
            pltpu.VMEM((2 * rows, group), F32),
            pltpu.VMEM((group, 2 * HEAD), BF),
            pltpu.VMEM((group, 2 * HEAD), BF),
            pltpu.VMEM((group, HEAD), F32),
            pltpu.VMEM((group, HEAD), F32),
        ],
    )


def _expert_kernel(
    x_ref, pulled_ref, chosen_ref, own_ref, router_ref, gate_ref, up_ref,
    dx_ref, dg_ref, du_ref, h_ref, c_ref,
):
    rows = x_ref[...]
    logits = jnp.dot(rows, router_ref[...], preferred_element_type=F32)
    chosen = chosen_ref[...].astype(F32)
    logits = jnp.where(chosen > 0.0, logits, -1e30)
    raised = jnp.exp(logits - jnp.max(logits, axis=-1, keepdims=True)) * chosen
    weight = jnp.sum(raised * own_ref[...], axis=-1, keepdims=True)
    weight = weight / jnp.maximum(jnp.sum(raised, axis=-1, keepdims=True), 1e-30)
    gate = jnp.dot(rows, gate_ref[...], preferred_element_type=F32)
    up = jnp.dot(rows, up_ref[...], preferred_element_type=F32)
    sigma = jax.nn.sigmoid(gate)
    swish = gate * sigma
    hidden = swish * up
    pulled = pulled_ref[...].astype(F32)
    c_ref[...] = jnp.sum(hidden * pulled, axis=-1, keepdims=True)
    h_ref[...] = (weight * hidden).astype(BF)
    pulled = weight * pulled
    gate_grad = (pulled * up * sigma * (1.0 + gate * (1.0 - sigma))).astype(BF)
    up_grad = (pulled * swish).astype(BF)
    dg_ref[...] = gate_grad
    du_ref[...] = up_grad
    dx = times_transposed(gate_grad, gate_ref[...]) + times_transposed(up_grad, up_ref[...])
    dx_ref[...] = dx.astype(BF)


def expert(rows, pulled, chosen, own, router, gate, up):
    count, width = rows.shape
    hidden = gate.shape[1]
    lanes = chosen.shape[1]
    step = min(count, 256)
    across = pl.BlockSpec((step, width), lambda i: (i, 0))
    thin = pl.BlockSpec((step, hidden), lambda i: (i, 0))
    column = pl.BlockSpec((step, 1), lambda i: (i, 0))
    return run(
        _expert_kernel,
        "expert",
        (count // step,),
        (rows, pulled, chosen, own, router, gate, up),
        [across, thin, pl.BlockSpec((step, lanes), lambda i: (i, 0)), full(1, lanes)]
        + [full(width, lanes), full(width, hidden), full(width, hidden)],
        [((count, width), BF)] + [((count, hidden), BF)] * 3 + [((count, 1), F32)],
        [across, thin, thin, thin, column],
        free=(0,),
        dear=True,
    )


def _rows_kernel(*refs):
    count = (len(refs) - 1) // 2
    total = None
    for left, right in zip(refs[:count], refs[count:-1]):
        part = contract_rows(left[...], right[...])
        total = part if total is None else total + part
    refs[-1][...] = total


def contract_chunks(lefts, rights):
    count, tall = lefts[0].shape
    wide = rights[0].shape[1]
    step = min(tall, 256)
    return run(
        _rows_kernel,
        "contract_chunks",
        (tall // step,),
        (*lefts, *rights),
        [pl.BlockSpec((count, step), lambda i: (0, i))] * len(lefts)
        + [full(count, wide)] * len(rights),
        [((tall, wide), F32)],
        [pl.BlockSpec((step, wide), lambda i: (i, 0))],
    )[0]


def body(
    layer_input,
    attn_gain,
    w_query,
    key_matrix,
    value_matrix,
    query_gain,
    key_gain,
    w_out,
    moe_gain,
    router,
    expert_gate,
    expert_up,
    expert_down,
    expert_ids,
    cont_segment,
    out_grad,
):
    tokens, width = layer_input.shape
    dps, _, cores = sizes = [lax.axis_size(a) for a in ALL]
    devices = math.prod(sizes)
    dp, z, c = [lax.axis_index(a) for a in ALL]
    experts = router.shape[1]
    capacity = tokens * TOP // experts
    plane = dps * cores
    slots = plane * capacity
    order = jnp.array(ORDER, jnp.int32)[z]
    where_block = jnp.array([[o.index(b) for b in range(STEPS)] for o in ORDER], jnp.int32)[z]
    own_heads = HQ // (STEPS * cores)
    heads = HQ // STEPS
    head_cols = heads * HEAD
    own_cols = own_heads * HEAD

    rows_dev = router.shape[0]
    id_cols = tokens * TOP // rows_dev
    router_pad = -(experts + 2 + id_cols) % 128
    small = jnp.concatenate(
        [
            router,
            attn_gain[:, None],
            moe_gain[:, None],
            expert_ids.astype(BF).reshape(rows_dev, id_cols),
            jnp.zeros((rows_dev, router_pad), BF),
        ],
        axis=1,
    )
    packed = pack(key_matrix, value_matrix, small)
    arrived = lax.all_gather(layer_input, "z", axis=0, tiled=True)
    query_own = from_dps(w_query, dp).reshape(width, own_cols)
    packed = lax.all_to_all(packed, "z", split_axis=0, concat_axis=0, tiled=True)
    packed, w_out, order, where_block = hold(packed, w_out, order, where_block)
    w_back = lax.all_to_all(w_out, "dp", split_axis=0, concat_axis=0, tiled=True)

    at_slot = jnp.arange(capacity, dtype=jnp.int32)
    earlier = (jnp.arange(tokens)[:, None] > jnp.arange(tokens)[None, :]).astype(BF)

    def plan(ids):
        chosen = jnp.any(ids[:, :, None] == jnp.arange(experts, dtype=jnp.int32), axis=1)
        ranks = jnp.dot(earlier, chosen.astype(BF), preferred_element_type=F32).astype(jnp.int32)
        ranks = jnp.where(chosen & (ranks < capacity), ranks, -1)
        in_plane = lax.dynamic_index_in_dim(
            ranks.reshape(tokens, dps, STEPS, cores), z, 2, keepdims=False
        ).reshape(tokens, plane)
        pick = (in_plane[:, :, None] == at_slot).reshape(tokens, slots).astype(BF)
        back = (in_plane.T[:, None, :] == at_slot[:, None]).reshape(slots, tokens).astype(BF)
        return chosen, ranks, pick, back

    def to_plane(rows):
        return lax.all_to_all(rows, PLANE, split_axis=0, concat_axis=0, tiled=True)

    zs = jnp.stack([z, jnp.int32(0)])
    own_chosen, own_ranks, own_pick, own_back = plan(expert_ids)
    own_slots = own_ranks[:, :, None] == at_slot
    first_id = 2 * HEAD + experts + 2
    ids = packed[:, :, first_id : first_id + id_cols].astype(jnp.int32)
    ids = ids.reshape(STEPS, tokens, TOP)
    ids = [lax.dynamic_index_in_dim(ids, order[i], 0, keepdims=False) for i in range(STEPS)]
    packed = jnp.stack(cores_in_order(packed, c), axis=1).reshape(w_query.shape[0], -1)
    packed = from_dps(packed, dp).reshape(width, -1)
    w_in = cores_in_order(query_own, c)
    *w_in, packed, ids, w_back = hold(*w_in, packed, ids, w_back)
    w_back = lax.all_to_all(w_back, "z", split_axis=0, concat_axis=0, tiled=True)
    w_back = lax.all_gather(w_back, PLANE, axis=0, tiled=True)
    rest = packed[:, 2 * HEAD :]
    lanes = rest.shape[1]
    router_all = rest[:, :experts]
    attn_gain_all = rest[:, experts].astype(F32)[None, :]
    moe_gain_all = rest[:, experts + 1].astype(F32)[None, :]
    w_in = jnp.concatenate([*w_in, packed[:, : 2 * HEAD]], axis=1)
    plans = [(own_chosen, own_ranks, own_pick, own_back)] + [plan(i) for i in ids[1:]]
    pick = [p[2] for p in plans]
    back = [p[3] for p in plans]
    slot_chosen = jnp.stack(
        [
            jnp.dot(back[i], jnp.pad(p[0].astype(BF), ((0, 0), (0, lanes - experts))))
            for i, p in enumerate(plans)
        ]
    ).reshape(STEPS, plane, capacity, lanes)
    slot_chosen = slot_chosen.transpose(1, 0, 2, 3)
    own_expert = dp * (STEPS * cores) + z * cores + c
    own_expert = (jnp.arange(lanes)[None, :] == own_expert).astype(F32)

    where_at, opens = group_layout(cont_segment[0])
    group = where_at.shape[0]

    def own_rows(table):
        mine = lax.dynamic_index_in_dim(table.reshape(STEPS, cores, tokens), c, 1, keepdims=False)
        return mine.reshape(-1)

    cosine, sine = angle_tables(own_rows(where_at), HEAD)
    query_at = own_rows(jnp.arange(group, dtype=jnp.int32))[:, None]
    opens = own_rows(opens)[:, None]
    numbers = jnp.arange(STEPS, dtype=jnp.int32)
    table = jnp.concatenate([(numbers * cores + (c + k) % cores) * tokens for k in range(cores)])
    query_gain_f = query_gain.astype(F32)[None, :]
    key_gain_f = key_gain.astype(F32)[None, :]
    scale = LOG2E / math.sqrt(HEAD)
    query_gain_s = query_gain_f * scale
    gate_w, up_w, down_w = expert_gate[0], expert_up[0], expert_down[0]
    at_block = [jnp.stack([z, order[i]]) for i in range(STEPS)]

    (
        upstream_block, w_in, pick, back, slot_chosen, cosine, sine, query_at, opens, table,
        query_gain_s, key_gain_f, at_block, own_expert, attn_gain_all, moe_gain_all, rest,
    ) = hold(
        out_grad, w_in, pick, back, slot_chosen, cosine, sine, query_at, opens, table,
        query_gain_s, key_gain_f, at_block, own_expert, attn_gain_all, moe_gain_all, rest,
    )
    g_up, g_down = spread_first(upstream_block)
    g0 = to_plane(dispatch(zs, back[0], [upstream_block], (0, 0, 0, 0)))
    normed, raw, queries, key_value_rows = project(
        arrived, attn_gain_all, w_in, cosine, sine, query_gain_s, key_gain_f, tokens
    )
    pieces = [key_value_rows, *other_cores(key_value_rows)]
    queries, g_up, g_down, g0, *pieces = hold(queries, g_up, g_down, g0, *pieces)
    g_up2, g_down2 = spread_second(g_up, g_down)
    g1 = to_plane(dispatch(zs, back[1], [g_up, g_down], FIRST))
    mixed, log_totals = attend(table, queries, pieces, query_at, opens, tokens)
    mixed, w_back, g_up2, g_down2 = hold(mixed, w_back, g_up2, g_down2)
    g_last = spread_third(g_up2, g_down2, z)
    w_back = w_back.reshape(dps, cores, STEPS, dps // STEPS, -1, width).transpose(3, 2, 1, 0, 4, 5)
    w_back = w_back.reshape(head_cols, width)
    attended = matmul(mixed, w_back, "nn", 4, "columns")
    attended, g_last, g0, g1, g_up2, g_down2 = hold(attended, g_last, g0, g1, g_up2, g_down2)
    attended = lax.psum_scatter(attended, "z", scatter_dimension=0, tiled=True)
    g2 = to_plane(dispatch(zs, back[2], [g_up, g_down, g_up2, g_down2], SECOND))
    pulled0 = matmul(g0, down_w, "nt", 2, "rows", F32)
    g2, g_last, pulled0 = hold(g2, g_last, pulled0)
    g3 = to_plane(dispatch(zs, back[3], [g_up2, g_down2, g_last], THIRD))
    pulled1 = matmul(g1, down_w, "nt", 2, "rows", F32)
    pulled2 = matmul(g2, down_w, "nt", 2, "rows", F32)
    g3, pulled1, pulled2, slot_chosen = hold(g3, pulled1, pulled2, slot_chosen)
    slot_chosen = to_plane(slot_chosen)
    slot_chosen = slot_chosen.transpose(1, 0, 2, 3).reshape(STEPS, slots, lanes)
    slot_chosen = [slot_chosen[i] for i in range(STEPS)]
    pulled3 = matmul(g3, down_w, "nt", 2, "rows", F32)
    attended, pulled3, slot_chosen = hold(attended, pulled3, slot_chosen)
    upstream_slots = [g0, g1, g2, g3]
    resid, moe_low = add_and_norm(layer_input, moe_gain_all, (attended,))

    def through(i, rows, pulled):
        return expert(rows, pulled, slot_chosen[i], own_expert, rest, gate_w, up_w)

    m_up, m_down = spread_first(moe_low)
    r0 = to_plane(dispatch(zs, back[0], [moe_low], (0, 0, 0, 0)))
    m_up, m_down = hold(m_up, m_down)
    m_up2, m_down2 = spread_second(m_up, m_down)
    r1 = dispatch(zs, back[1], [m_up, m_down], FIRST)
    r1, r0 = hold(r1, r0)
    r1 = to_plane(r1)
    e0 = through(0, r0, pulled0)
    m_up2, m_down2, e0 = hold(m_up2, m_down2, e0)
    m_last = spread_third(m_up2, m_down2, z)
    r2 = dispatch(zs, back[2], [m_up, m_down, m_up2, m_down2], SECOND)
    r2, r1 = hold(r2, r1)
    r2 = to_plane(r2)
    e1 = through(1, r1, pulled1)
    m_last, e1 = hold(m_last, e1)
    r3 = dispatch(zs, back[3], [m_up2, m_down2, m_last], THIRD)
    r3, r2 = hold(r3, r2)
    r3 = to_plane(r3)
    e2 = through(2, r2, pulled2)
    r3, e2 = hold(r3, e2)
    e3 = through(3, r3, pulled3)
    rows = [r0, r1, r2, r3]
    slot_grads, gate_grads, up_grads, hiddens, centres = [list(v) for v in zip(e0, e1, e2, e3)]
    d0, d1, d2, d3 = slot_grads
    b3 = to_plane(d3)
    moe_row, d2, centres, hiddens = hold(moe_low, d2, centres, hiddens)
    logits = jnp.dot(moe_row, router_all, preferred_element_type=F32)
    logits = jnp.where(own_chosen, logits, -jnp.inf)
    raised = jnp.exp(logits - jnp.max(logits, axis=-1, keepdims=True))
    gates = raised / jnp.sum(raised, axis=-1, keepdims=True)
    stacked = jnp.stack([v.reshape(dps, cores, capacity) for v in centres])
    centre_back = jnp.stack(
        [
            lax.dynamic_index_in_dim(stacked, where_block[b], 0, keepdims=False)
            for b in range(STEPS)
        ],
        axis=1,
    ).reshape(experts, capacity)
    h0, h1, h2, h3 = hiddens

    def produced(value):
        return matmul(value, down_w, "nn", 2, "columns", dear=True)

    p3 = produced(h3)
    b3, d2, p3, centre_back, gates, h0, h1, h2 = hold(
        b3, d2, p3, centre_back, gates, h0, h1, h2
    )
    b2 = to_plane(d2)
    (c3,) = line_part(zs, pick[3], b3, tokens)
    got = sum_first(c3)
    p2 = produced(h2)
    b2, d1, h1, p2 = hold(b2, d1, h1, p2)
    b1 = to_plane(d1)
    p1 = produced(h1)
    got, b2, p1 = hold(got, b2, p1)
    c2, middle = line_part(zs, pick[2], b2, tokens, 1, (c3, got))
    s_up, s_down = sum_second(middle)
    b1, d0, h0 = hold(b1, d0, h0)
    b0 = to_plane(d0)
    p0 = produced(h0)
    s_up, s_down, b1, p0 = hold(s_up, s_down, b1, p0)
    s_up, s_down = line_part(zs, pick[1], b1, tokens, 2, (c2, s_up, s_down))
    s_up, s_down = sum_third(s_up, s_down)
    b0, centre_back = hold(b0, centre_back)
    centre_back = lax.all_to_all(centre_back, ALL, split_axis=0, concat_axis=0, tiled=True)
    (c0,) = line_part(zs, pick[0], b0, tokens)
    weight_grad = jnp.sum(jnp.where(own_slots, centre_back[None], 0.0), axis=2)
    logit_grad = (
        gates * (weight_grad - jnp.sum(gates * weight_grad, axis=-1, keepdims=True))
    ).astype(BF)
    logit_wide = jnp.pad(logit_grad, ((0, 0), (0, lanes - experts)))
    s_up, s_down, c0, logit_wide = hold(s_up, s_down, c0, logit_wide)
    resid_grad, resid_low, moe_gain_grad = norm_back(
        resid, moe_gain_all, out_grad, (c0, s_up, s_down), logit_wide, rest
    )

    def by_core(value, axis):
        size = value.shape[axis] // cores
        return [
            lax.dynamic_slice_in_dim(value, (c + k) % cores * size, size, axis)
            for k in range(cores)
        ]

    resid_low, p3, logit_grad, hiddens, rows = hold(resid_low, p3, logit_grad, hiddens, rows)
    resid_all = lax.all_gather(resid_low, "z", axis=0, tiled=True)
    o3 = to_plane(p3)
    down_weight_grad = contract_chunks(hiddens, upstream_slots)
    router_grad = contract_rows(moe_low, logit_grad)
    o3, p2, rows, down_weight_grad, router_grad = hold(
        o3, p2, rows, down_weight_grad, router_grad
    )
    (o3,) = line_part(zs, pick[3], o3, tokens)
    t_got = sum_first(o3)
    o2 = to_plane(p2)
    up_weight_grad = contract_chunks(rows, up_grads)
    rows, up_weight_grad, up_grads = hold(rows, up_weight_grad, up_grads)
    gate_weight_grad = contract_chunks(rows, gate_grads)
    o2, t_got, gate_weight_grad = hold(o2, t_got, gate_weight_grad)
    o2, middle = line_part(zs, pick[2], o2, tokens, 1, (o3, t_got))
    middle, o2, p1 = hold(middle, o2, p1)
    t_up, t_down = sum_second(middle)
    o1 = to_plane(p1)
    resid_all, o2 = hold(resid_all, o2)
    mixed_grad = matmul(resid_all, w_back, "nt", 4, "rows", dear=True)
    mixed_grad, resid_all = hold(mixed_grad, resid_all)
    out_weight_grad = matmul(mixed, resid_all, "tn", 4, "columns")
    out_weight_grad = out_weight_grad.reshape(dps // STEPS, STEPS, cores, dps, -1, width)
    out_weight_grad = out_weight_grad.transpose(3, 2, 1, 0, 4, 5).reshape(head_cols, width)
    out_weight_grad, mixed_grad, t_up, t_down, o1 = hold(
        out_weight_grad, mixed_grad, t_up, t_down, o1
    )
    out_weight_grad = lax.psum_scatter(out_weight_grad, PLANE, scatter_dimension=0, tiled=True)
    t_up, t_down = line_part(zs, pick[1], o1, tokens, 2, (o2, t_up, t_down))
    t_up, t_down, p0 = hold(t_up, t_down, p0)
    t_up, t_down = sum_third(t_up, t_down)
    o0 = to_plane(p0)
    query_grads, *sums = attend_back(
        table, queries, mixed_grad, mixed, log_totals, pieces, query_at, opens, tokens
    )
    query_grads, t_up, t_down, o0, *sums = hold(query_grads, t_up, t_down, o0, *sums)
    sums = sum_over_cores(sums)
    normed_grad, raw_grad, query_gain_grad, key_gain_grad = project_back(
        raw, query_grads, sums, w_in, cosine, sine, query_gain_f, key_gain_f, tokens
    )
    normed_grad, raw_grad = hold(normed_grad, raw_grad)
    normed_sum = lax.psum_scatter(normed_grad, "z", scatter_dimension=0, tiled=True)
    in_grad = matmul(normed, raw_grad, "tn", 4, "rows")
    query_share = sum_over_cores(by_core(in_grad[:, :head_cols], 1)).astype(BF)
    key_value_grad = in_grad[:, head_cols:].reshape(dps, STEPS, cores, rows_dev, 2 * HEAD)
    key_value_grad = sum_over_cores(
        [part[:, :, 0] for part in by_core(key_value_grad, 2)]
    ).astype(BF)
    attn_gain_grad = jnp.sum(normed_grad.astype(F32) * normed.astype(F32), axis=0)[None, :]
    attn_gain_grad = attn_gain_grad / attn_gain_all

    def to_owners(value):
        columns = value.shape[0]
        split = value.reshape(columns, devices, rows_dev).transpose(1, 0, 2)
        return split.reshape(devices, columns * rows_dev)

    gain_row = jnp.concatenate([query_gain_grad, key_gain_grad], axis=1)
    late = jnp.concatenate(
        [
            to_owners(jnp.concatenate([router_grad.T, moe_gain_grad, attn_gain_grad])),
            jnp.broadcast_to(gain_row, (devices, 2 * HEAD)),
        ],
        axis=1,
    )
    late = lax.all_to_all(late, ALL, split_axis=0, concat_axis=0, tiled=True)
    late, out_weight_grad, o0, query_share, key_value_grad = hold(
        late, out_weight_grad, o0, query_share, key_value_grad
    )
    query_weight_grad = over_dps(query_share.reshape(dps, -1, own_cols), dp)
    key_value_grad = over_dps(key_value_grad, dp).astype(BF)
    out_weight_grad = lax.all_to_all(out_weight_grad, "z", split_axis=0, concat_axis=0, tiled=True)
    (o0,) = line_part(zs, pick[0], o0, tokens)
    output = resid + (o0.astype(F32) + t_up.astype(F32) + t_down.astype(F32))
    output = output.astype(BF)
    late = jnp.sum(late, axis=0)
    out_weight_grad, key_value_grad, output, late, query_weight_grad = hold(
        out_weight_grad, key_value_grad, output, late, query_weight_grad
    )
    gain_sums = late[-2 * HEAD :].reshape(2, HEAD)
    owned = late[: -2 * HEAD].reshape(experts + 2, rows_dev)
    key_value_grad = lax.all_to_all(key_value_grad, "z", split_axis=0, concat_axis=0, tiled=True)
    key_value_grad, out_weight_grad = hold(key_value_grad, out_weight_grad)
    out_weight_grad = lax.all_to_all(out_weight_grad, "dp", split_axis=0, concat_axis=0, tiled=True)
    out_weight_grad = out_weight_grad.astype(F32)
    key_value_grad = key_value_grad.transpose(1, 0, 2).astype(F32)
    key_weight_grad = key_value_grad[:, :, :HEAD].reshape(rows_dev, -1)
    value_weight_grad = key_value_grad[:, :, HEAD:].reshape(rows_dev, -1)
    (input_grad,) = norm_back(layer_input, attn_gain_all, resid_grad, (normed_sum,))
    return (
        output,
        input_grad,
        owned[experts + 1],
        query_weight_grad,
        key_weight_grad,
        value_weight_grad,
        gain_sums[0],
        gain_sums[1],
        out_weight_grad,
        owned[experts],
        owned[:experts].T,
        gate_weight_grad[None],
        up_weight_grad[None],
        down_weight_grad[None],
    )


def solution(mesh):
    dps, sequence = mesh.devices.shape
    inner = Mesh(mesh.devices.reshape(dps, STEPS, sequence // STEPS), ALL)
    rows = P(ALL, None)
    placed = (
        rows,
        P(ALL),
        P("dp", ("z", "core")),
        rows,
        rows,
        P(),
        P(),
        rows,
        P(ALL),
        rows,
        P(ALL, None, None),
        P(ALL, None, None),
        P(ALL, None, None),
        rows,
        P("dp", None),
        rows,
    )
    return jax.shard_map(
        body,
        mesh=inner,
        in_specs=placed,
        out_specs=(
            rows,
            rows,
            P(ALL),
            P("dp", ("z", "core")),
            rows,
            rows,
            P(),
            P(),
            rows,
            P(ALL),
            rows,
            P(ALL, None, None),
            P(ALL, None, None),
            P(ALL, None, None),
        ),
        check_vma=False,
    )
```

```python
from functools import partial
import math

import jax
import jax.numpy as jnp
from jax import lax
from jax.experimental import pallas as pl
from jax.experimental.pallas import tpu as pltpu
from jax.sharding import Mesh, PartitionSpec as P

HQ = 32
KEY_VALUE_HEADS = 4
TOP = 8
PROMPT = 1024
NCONT = 4
HEAD = 128

EPS = 1e-06
THETA = 1000000.0
LOG2E = 1.4426950408889634
BF = jnp.bfloat16
F32 = jnp.float32

STEPS = 4
ORDER = ((0, 1, 2, 3), (1, 0, 2, 3), (2, 3, 1, 0), (3, 2, 1, 0))
PLANE = ("dp", "core")
ALL = ("dp", "z", "core")


def angle_tables(where_at, head_width):
    ranks = jnp.arange(head_width // 2, dtype=F32) * (2.0 / head_width)
    inverse = jnp.exp(-ranks * math.log(THETA))
    angles = where_at.astype(F32)[:, None] * inverse[None, :]
    cosine, sine = jnp.cos(angles), jnp.sin(angles)
    return (
        jnp.concatenate([cosine, cosine], axis=-1),
        jnp.concatenate([-sine, sine], axis=-1),
    )


def group_layout(segment):
    length = segment.shape[0]
    one_hot = (segment[:, None] == jnp.arange(NCONT, dtype=jnp.int32)[None, :]).astype(jnp.int32)
    counted = jnp.sum(one_hot, axis=0)
    before = jnp.arange(NCONT)[:, None] > jnp.arange(NCONT)[None, :]
    starts = jnp.sum(jnp.where(before, counted[None, :], 0), axis=1)
    begins = jnp.sum(one_hot * starts[None, :], axis=1)
    within = jnp.arange(length, dtype=jnp.int32) - begins
    where_at = jnp.concatenate([jnp.arange(PROMPT, dtype=jnp.int32), PROMPT + within])
    opens = jnp.concatenate([jnp.full((PROMPT,), PROMPT, jnp.int32), PROMPT + begins])
    return (where_at, opens)


def contract_rows(left, right):
    return lax.dot_general(left, right, (((0,), (0,)), ((), ())), preferred_element_type=F32)


def times_transposed(left, right):
    return lax.dot_general(left, right, (((1,), (1,)), ((), ())), preferred_element_type=F32)


def hold(*values):
    return lax.optimization_barrier(values)


def spread_first(block):
    return (
        lax.ppermute(block, "z", [(0, 1), (1, 2), (2, 3)]),
        lax.ppermute(block, "z", [(1, 0), (2, 1), (3, 2)]),
    )


def spread_second(up, down):
    return (
        lax.ppermute(up, "z", [(1, 2), (2, 3)]),
        lax.ppermute(down, "z", [(2, 1), (1, 0)]),
    )


def spread_third(up2, down2, z):
    return lax.ppermute(jnp.where(z == 2, up2, down2), "z", [(2, 3), (1, 0)])


FIRST = (1, 0, 1, 0)
SECOND = (3, 1, 0, 2)
THIRD = (2, 1, 0, 2)


def sum_first(third):
    return lax.ppermute(third, "z", [(0, 1), (3, 2)])


def sum_second(middle):
    return (
        lax.ppermute(middle, "z", [(0, 1), (1, 2)]),
        lax.ppermute(middle, "z", [(3, 2), (2, 1)]),
    )


def sum_third(up, down):
    return (
        lax.ppermute(up, "z", [(0, 1), (1, 2), (2, 3)]),
        lax.ppermute(down, "z", [(3, 2), (2, 1), (1, 0)]),
    )


def over_dps(value, dp):
    dps = value.shape[0]
    total = lax.dynamic_index_in_dim(value, dp, 0, keepdims=False).astype(F32)
    for k in range(1, dps):
        piece = lax.dynamic_index_in_dim(value, dp ^ k, 0, keepdims=False)
        total = total + lax.ppermute(piece, "dp", [(i, i ^ k) for i in range(dps)]).astype(F32)
    return total


def exchange(value, axis):
    size, me = value.shape[0], lax.axis_index(axis)
    own = lax.dynamic_index_in_dim(value, me, 0, keepdims=False)
    whole = lax.dynamic_update_index_in_dim(jnp.zeros_like(value), own, me, 0)
    for k in range(1, size):
        piece = lax.dynamic_index_in_dim(value, me ^ k, 0, keepdims=False)
        got = lax.ppermute(piece, axis, [(i, i ^ k) for i in range(size)])
        whole = lax.dynamic_update_index_in_dim(whole, got, me ^ k, 0)
    return whole


def from_dps(value, dp):
    dps = lax.axis_size("dp")
    whole = jnp.zeros((dps, *value.shape), value.dtype)
    whole = lax.dynamic_update_index_in_dim(whole, value, dp, 0)
    for k in range(1, dps):
        got = lax.ppermute(value, "dp", [(i, i ^ k) for i in range(dps)])
        whole = lax.dynamic_update_index_in_dim(whole, got, dp ^ k, 0)
    return whole


def other_cores(value):
    cores = lax.axis_size("core")
    return [
        lax.ppermute(value, "core", [((i + k) % cores, i) for i in range(cores)])
        for k in range(1, cores)
    ]


def cores_in_order(value, c):
    cores = lax.axis_size("core")
    pieces = [value, *other_cores(value)]
    ordered = []
    for n in range(cores):
        piece = pieces[0]
        for k in range(1, cores):
            piece = jnp.where((n - c) % cores == k, pieces[k], piece)
        ordered.append(piece)
    return ordered


def sum_over_cores(pieces):
    cores = lax.axis_size("core")
    total = pieces[0].astype(F32)
    for k in range(1, cores):
        got = lax.ppermute(pieces[k], "core", [(i, (i + k) % cores) for i in range(cores)])
        total = total + got.astype(F32)
    return total


CHEAP = pl.CostEstimate(flops=1, bytes_accessed=1, transcendentals=0)
DEAR = pl.CostEstimate(flops=10**11, bytes_accessed=1, transcendentals=0)


def run(kernel, name, grid, operands, in_specs, outs, out_specs, scalars=None, scratch=(), free=(), dear=False):
    prefetch = () if scalars is None else (scalars,)
    operands = [
        v if i in free else pltpu.with_memory_space_constraint(v, pltpu.HBM)
        for i, v in enumerate(operands)
    ]
    got = pl.pallas_call(
        kernel,
        grid_spec=pltpu.PrefetchScalarGridSpec(
            num_scalar_prefetch=len(prefetch),
            grid=grid,
            in_specs=in_specs,
            out_specs=out_specs,
            scratch_shapes=scratch,
        ),
        out_shape=[pltpu.HBM(shape, kind) for shape, kind in outs],
        compiler_params=pltpu.CompilerParams(vmem_limit_bytes=52 * 1024 * 1024),
        cost_estimate=DEAR if dear else CHEAP,
        name=name,
    )(*prefetch, *operands)
    return got


def full(*shape):
    return pl.BlockSpec(shape, lambda *_: (0,) * len(shape))


def _matmul_kernel(a_ref, b_ref, o_ref, *, dims):
    part = lax.dot_general(a_ref[...], b_ref[...], (dims, ((), ())), preferred_element_type=F32)
    o_ref[...] = part.astype(o_ref.dtype)


def matmul(a, b, kind, steps, by, out=BF, dear=False):
    dims = {"nn": ((1,), (0,)), "nt": ((1,), (1,)), "tn": ((0,), (0,))}[kind]
    rows = a.shape[1 - dims[0][0]]
    columns = b.shape[1 - dims[1][0]]
    a_spec, b_spec = full(*a.shape), full(*b.shape)
    if by == "rows":
        size = rows // steps
        if kind == "tn":
            a_spec = pl.BlockSpec((a.shape[0], size), lambda i: (0, i))
        else:
            a_spec = pl.BlockSpec((size, a.shape[1]), lambda i: (i, 0))
        o_spec = pl.BlockSpec((size, columns), lambda i: (i, 0))
    else:
        size = columns // steps
        if kind == "nt":
            b_spec = pl.BlockSpec((size, b.shape[1]), lambda i: (i, 0))
        else:
            b_spec = pl.BlockSpec((b.shape[0], size), lambda i: (0, i))
        o_spec = pl.BlockSpec((rows, size), lambda i: (0, i))
    return run(
        partial(_matmul_kernel, dims=dims),
        "matmul_" + kind,
        (steps,),
        (a, b),
        [a_spec, b_spec],
        [((rows, columns), out)],
        [o_spec],
        dear=dear,
    )[0]


def _dispatch_kernel(s_ref, pick_ref, *refs, sources):
    z, rows = s_ref[0], refs[0][...]
    for n in range(1, len(refs) - 1):
        here = False
        for at, source in enumerate(sources):
            if source == n:
                here = here | (z == at)
        rows = jnp.where(here, refs[n][...], rows)
    refs[-1][...] = jnp.dot(pick_ref[...], rows, preferred_element_type=F32).astype(BF)


def dispatch(scalars, pick, blocks, sources):
    slots, tokens = pick.shape
    width = blocks[0].shape[1]
    tile = pl.BlockSpec((tokens, 1024), lambda j, s: (0, j))
    return run(
        partial(_dispatch_kernel, sources=sources),
        "dispatch",
        (width // 1024,),
        (pick, *blocks),
        [full(slots, tokens)] + [tile] * len(blocks),
        [((slots, width), BF)],
        [pl.BlockSpec((slots, 1024), lambda j, s: (0, j))],
        scalars=scalars,
        free=(1, 2, 3, 4),
    )[0]


def _part_kernel(s_ref, a_ref, b_ref, *refs, step):
    z = s_ref[0]
    part = jnp.dot(a_ref[...], b_ref[...], preferred_element_type=F32)
    if step == 0:
        refs[0][...] = part.astype(BF)
    elif step == 1:
        third, got, part_ref, middle_ref = refs
        part_ref[...] = part.astype(BF)
        middle = jnp.where((z == 0) | (z == 3), part, third[...].astype(F32))
        middle_ref[...] = (middle + got[...].astype(F32)).astype(BF)
    else:
        second, up, down, up_ref, down_ref = refs
        other = second[...].astype(F32)
        up_ref[...] = (jnp.where(z == 1, other, part) + up[...].astype(F32)).astype(BF)
        down_ref[...] = (jnp.where(z == 2, other, part) + down[...].astype(F32)).astype(BF)


def line_part(scalars, a, b, tokens, step=0, more=()):
    width = b.shape[1]
    tile = pl.BlockSpec((tokens, 1024), lambda j, s: (0, j))
    return run(
        partial(_part_kernel, step=step),
        "line_part",
        (width // 1024,),
        (a, b, *more),
        [
            pl.BlockSpec((tokens, a.shape[1]), lambda j, s: (s[1], 0)),
            pl.BlockSpec((b.shape[0], 1024), lambda j, s: (0, j)),
        ]
        + [tile] * len(more),
        [((tokens, width), BF)] * (1 if step == 0 else 2),
        [tile] * (1 if step == 0 else 2),
        scalars=scalars,
        free=(1, 2, 3, 4),
    )


def _norm_kernel(x_ref, gain_ref, *refs):
    terms, (resid_ref, low_ref) = refs[:-2], refs[-2:]
    value = x_ref[...].astype(F32)
    for term in terms:
        value = value + term[...].astype(F32)
    resid_ref[...] = value
    factor = lax.rsqrt(jnp.mean(value * value, axis=-1, keepdims=True) + EPS)
    low_ref[...] = (value * factor * gain_ref[...]).astype(BF)


def add_and_norm(x, gain, terms):
    tokens, width = x.shape
    step = min(tokens, 64)
    tile = pl.BlockSpec((step, width), lambda i: (i, 0))
    return run(
        _norm_kernel,
        "add_and_norm",
        (tokens // step,),
        (x, gain, *terms),
        [tile, full(1, width)] + [tile] * len(terms),
        [((tokens, width), F32), ((tokens, width), BF)],
        [tile, tile],
    )


def _norm_back_kernel(v_ref, gain_ref, above_ref, *refs, logits):
    if logits:
        logit_ref, router_ref, *terms, total_ref, low_ref, gain_grad_ref = refs
    else:
        *terms, total_ref = refs
    grad = sum([term[...].astype(F32) for term in terms])
    if logits:
        grad = grad + times_transposed(logit_ref[...], router_ref[...])
    value = v_ref[...].astype(F32)
    factor = lax.rsqrt(jnp.mean(value * value, axis=-1, keepdims=True) + EPS)
    unit = value * factor
    if logits:

        @pl.when(pl.program_id(0) == 0)
        def _():
            gain_grad_ref[...] = jnp.zeros_like(gain_grad_ref)

        gain_grad_ref[...] += jnp.sum(grad * unit, axis=0, keepdims=True)
    grad = grad * gain_ref[...]
    shift = jnp.mean(grad * unit, axis=-1, keepdims=True)
    total = above_ref[...].astype(F32) + factor * (grad - unit * shift)
    total_ref[...] = total
    if logits:
        low_ref[...] = total.astype(BF)


def norm_back(value, gain, above, terms, logit_grad=None, router=None):
    tokens, width = value.shape
    step = min(tokens, 64)
    tile = pl.BlockSpec((step, width), lambda i: (i, 0))
    operands, specs = [value, gain, above], [tile, full(1, width), tile]
    outs, out_specs = [((tokens, width), F32)], [tile]
    if logit_grad is not None:
        lanes = logit_grad.shape[1]
        operands += [logit_grad, router]
        specs += [pl.BlockSpec((step, lanes), lambda i: (i, 0)), full(width, lanes)]
        outs += [((tokens, width), BF), ((1, width), F32)]
        out_specs += [tile, full(1, width)]
    return run(
        partial(_norm_back_kernel, logits=logit_grad is not None),
        "norm_back",
        (tokens // step,),
        (*operands, *terms),
        specs + [tile] * len(terms),
        outs,
        out_specs,
    )


def _pack_kernel(key_ref, value_ref, small_ref, out_ref):
    for at in range(STEPS):
        cols = slice(at * HEAD, (at + 1) * HEAD)
        out_ref[at, :, :HEAD] = key_ref[:, cols]
        out_ref[at, :, HEAD : 2 * HEAD] = value_ref[:, cols]
        out_ref[at, :, 2 * HEAD :] = small_ref[...]


def pack(key, value, small):
    rows = small.shape[0]
    lanes = 2 * HEAD + small.shape[1]
    return run(
        _pack_kernel,
        "pack",
        (1,),
        (key, value, small),
        [full(*key.shape), full(*value.shape), full(*small.shape)],
        [((STEPS, rows, lanes), BF)],
        [full(STEPS, rows, lanes)],
    )[0]


def _lane_mean(value):
    ones = jnp.full((HEAD, HEAD), 1.0 / HEAD, BF)
    return jnp.dot(value.astype(BF), ones, preferred_element_type=F32)


def _project_kernel(
    x_ref, gain_ref, w_ref, cos_ref, sin_ref, qg_ref, kg_ref, n_ref, raw_ref, q_ref, kv_ref
):
    x = x_ref[...].astype(F32)
    factor = lax.rsqrt(jnp.mean(x * x, axis=-1, keepdims=True) + EPS)
    normed = (x * factor * gain_ref[...]).astype(BF)
    n_ref[...] = normed
    raw_ref[...] = jnp.dot(normed, w_ref[...], preferred_element_type=F32)
    cosine, sine = cos_ref[...], sin_ref[...]
    heads = q_ref.shape[1] // HEAD
    for h in range(heads + 1):
        cols = slice(h * HEAD, (h + 1) * HEAD)
        value = raw_ref[:, cols]
        factor = lax.rsqrt(_lane_mean(value * value) + EPS)
        value = value * factor * (qg_ref[...] if h < heads else kg_ref[...])
        value = (value * cosine + pltpu.roll(value, HEAD // 2, 1) * sine).astype(BF)
        if h < heads:
            q_ref[:, cols] = value
        else:
            kv_ref[:, :HEAD] = value
    kv_ref[:, HEAD:] = raw_ref[:, (heads + 1) * HEAD :].astype(BF)


def project(x, gain, w_in, cosine, sine, query_gain, key_gain, rows):
    tokens, width = x.shape
    columns = w_in.shape[1]

    def tile(size):
        return pl.BlockSpec((rows, size), lambda i: (i, 0))

    return run(
        _project_kernel,
        "project",
        (tokens // rows,),
        (x, gain, w_in, cosine, sine, query_gain, key_gain),
        [tile(width), full(1, width), full(width, columns), tile(HEAD), tile(HEAD)]
        + [full(1, HEAD)] * 2,
        [
            ((tokens, width), BF),
            ((tokens, columns), F32),
            ((tokens, columns - 2 * HEAD), BF),
            ((tokens, 2 * HEAD), BF),
        ],
        [tile(width), tile(columns), tile(columns - 2 * HEAD), tile(2 * HEAD)],
        dear=True,
    )


def _project_back_kernel(
    raw_ref, near_ref, last_ref, dkv_ref, w_ref, cos_ref, sin_ref, qg_ref, kg_ref,
    ng_ref, rg_ref, dqg_ref, dkg_ref,
):
    @pl.when(pl.program_id(0) == 0)
    def _():
        dqg_ref[...] = jnp.zeros_like(dqg_ref)
        dkg_ref[...] = jnp.zeros_like(dkg_ref)

    cosine, sine = cos_ref[...], sin_ref[...]
    heads = near_ref.shape[1] // HEAD
    at_last = pl.program_id(0) == STEPS - 1
    for h in range(heads + 1):
        cols = slice(h * HEAD, (h + 1) * HEAD)
        value = raw_ref[:, cols]
        factor = lax.rsqrt(_lane_mean(value * value) + EPS)
        unit = value * factor
        if h < heads:
            grad = jnp.where(at_last, last_ref[:, cols], near_ref[:, cols]).astype(F32) * (1.0 / math.sqrt(HEAD))
        else:
            grad = dkv_ref[:, :HEAD]
        grad = grad * cosine + pltpu.roll(grad * sine, HEAD // 2, 1)
        gain_grad = jnp.sum(grad * unit, axis=0, keepdims=True)
        if h < heads:
            dqg_ref[...] += gain_grad
            grad = grad * qg_ref[...]
        else:
            dkg_ref[...] += gain_grad
            grad = grad * kg_ref[...]
        shift = _lane_mean(grad * unit)
        rg_ref[:, cols] = (factor * (grad - unit * shift)).astype(BF)
    rg_ref[:, (heads + 1) * HEAD :] = dkv_ref[:, HEAD:].astype(BF)
    ng_ref[...] = times_transposed(rg_ref[...], w_ref[...]).astype(BF)


def project_back(raw, near, last, key_value_grads, w_in, cosine, sine, query_gain, key_gain, rows):
    tokens, columns = raw.shape
    width = w_in.shape[0]

    def tile(size):
        return pl.BlockSpec((rows, size), lambda i: (i, 0))

    return run(
        _project_back_kernel,
        "project_back",
        (tokens // rows,),
        (raw, near, last, key_value_grads, w_in, cosine, sine, query_gain, key_gain),
        [
            tile(columns),
            pl.BlockSpec((rows, columns - 2 * HEAD), lambda i: (jnp.minimum(i, STEPS - 2), 0)),
            full(rows, columns - 2 * HEAD),
            tile(2 * HEAD),
            full(width, columns),
            tile(HEAD),
            tile(HEAD),
            full(1, HEAD),
            full(1, HEAD),
        ],
        [((tokens, width), BF), ((tokens, columns), BF), ((1, HEAD), F32), ((1, HEAD), F32)],
        [tile(width), tile(columns), full(1, HEAD), full(1, HEAD)],
        dear=True,
    )


def _mask_bias(at_ref, opens_ref, bias_ref, low, high):
    rows = at_ref.shape[0]
    key_at = low + lax.broadcasted_iota(jnp.int32, (rows, high - low), 1)
    query_at = at_ref[...]
    allowed = (key_at <= query_at) & ((key_at < PROMPT) | (key_at >= opens_ref[...]))
    bias = jnp.where(allowed, 0.0, -1e30).astype(F32)
    bias_ref[:rows, low:high] = bias
    bias_ref[rows:, low:high] = bias


def _spans(number, chunk):
    return (number + 1) * chunk, min(number * chunk, PROMPT)


def _place_keys(table, pieces, k_ref, v_ref, rows):
    for k, piece in enumerate(pieces):
        for i in range(STEPS):
            place = pl.ds(pl.multiple_of(table[k * STEPS + i], rows), rows)
            k_ref[place, :HEAD] = piece[i * rows : (i + 1) * rows, :HEAD]
            v_ref[place, :HEAD] = piece[i * rows : (i + 1) * rows, HEAD:]


def _two_heads(ref, pair):
    first = pl.multiple_of(pair * 2 * HEAD, 2 * HEAD)
    return jnp.concatenate([ref[:, pl.ds(first, HEAD)], ref[:, pl.ds(first + HEAD, HEAD)]])


def _store_heads(ref, pair, value):
    first = pl.multiple_of(pair * 2 * HEAD, 2 * HEAD)
    rows = ref.shape[0]
    ref[:, pl.ds(first, HEAD)] = value[:rows].astype(ref.dtype)
    ref[:, pl.ds(first + HEAD, HEAD)] = value[rows:].astype(ref.dtype)


def _attend_kernel(table, *refs, cores, chunk, rows):
    pieces, refs = refs[:cores], refs[cores:]
    q_ref, at_ref, opens_ref, o_ref, l_ref, bias_ref, k_ref, v_ref = refs

    @pl.when(pl.program_id(0) == 0)
    def _():
        _place_keys(table, pieces, k_ref, v_ref, rows)
        v_ref[:, HEAD:] = jnp.ones((v_ref.shape[0], HEAD), BF)

    number = pl.program_id(0)
    for n in range(STEPS):

        @pl.when(number == n)
        def _(n=n):
            keys, masked = _spans(n, chunk)
            _mask_bias(at_ref, opens_ref, bias_ref, masked, keys)

            def pair_of_heads(pair, carry):
                query = _two_heads(q_ref, pair)
                out = None
                for low in range(0, keys, chunk):
                    s = times_transposed(query, k_ref[low : low + chunk, :])
                    if low >= masked:
                        s = s + bias_ref[:, low : low + chunk]
                    o = jnp.dot(
                        jnp.exp2(s).astype(BF),
                        v_ref[low : low + chunk, :],
                        preferred_element_type=F32,
                    )
                    out = o if out is None else out + o
                total = out[:, HEAD:]
                _store_heads(o_ref, pair, out[:, :HEAD] / total)
                log_total = jnp.log2(total)
                l_ref[2 * pair] = log_total[:rows]
                l_ref[2 * pair + 1] = log_total[rows:]
                return carry

            lax.fori_loop(0, q_ref.shape[1] // (2 * HEAD), pair_of_heads, 0, unroll=2)


def attend(table, queries, pieces, query_at, opens, rows):
    tokens, width = queries.shape
    heads, cores = width // HEAD, len(pieces)
    group = cores * tokens
    chunk = group // STEPS
    column = pl.BlockSpec((rows, 1), lambda i, o: (i, 0))
    tile = pl.BlockSpec((rows, width), lambda i, o: (i, 0))
    return run(
        partial(_attend_kernel, cores=cores, chunk=chunk, rows=rows),
        "attend",
        (STEPS,),
        (*pieces, queries, query_at, opens),
        [full(tokens, 2 * HEAD)] * cores + [tile, column, column],
        [((tokens, width), BF), ((heads, tokens, HEAD), F32)],
        [tile, pl.BlockSpec((heads, rows, HEAD), lambda i, o: (0, i, 0))],
        scalars=table,
        dear=True,
        scratch=[
            pltpu.VMEM((2 * rows, group), F32),
            pltpu.VMEM((group, HEAD), BF),
            pltpu.VMEM((group, 2 * HEAD), BF),
        ],
    )


def _beside(value, column):
    high = column.astype(BF)
    low = (column - high.astype(F32)).astype(BF)
    lane = lax.broadcasted_iota(jnp.int32, value.shape, 1)
    zero = jnp.zeros(value.shape, BF)
    extra = jnp.where(lane == 0, -high, jnp.where(lane == 1, -low, zero))
    return jnp.concatenate([value, extra], axis=1)


def _attend_back_kernel(table, *refs, cores, chunk, rows, first, count):
    pieces, refs = refs[:cores], refs[cores:]
    q_ref, do_ref, o_ref, l_ref, at_ref, opens_ref, dq_ref = refs[:7]
    sums, refs = refs[7 : 7 + cores], refs[7 + cores :]
    bias_ref, k_ref, v_ref, dk_ref, dv_ref = refs

    @pl.when(pl.program_id(0) == 0)
    def _():
        _place_keys(table, pieces, k_ref, v_ref, rows)
        ones = jnp.ones((k_ref.shape[0], HEAD), BF)
        k_ref[:, HEAD:] = ones
        v_ref[:, HEAD:] = ones
        dk_ref[...] = jnp.zeros_like(dk_ref)
        dv_ref[...] = jnp.zeros_like(dv_ref)

    number = first + pl.program_id(0)
    for n in range(first, first + count):

        @pl.when(number == n)
        def _(n=n):
            keys, masked = _spans(n, chunk)
            _mask_bias(at_ref, opens_ref, bias_ref, masked, keys)

            def pair_of_heads(pair, carry):
                query, grad = _two_heads(q_ref, pair), _two_heads(do_ref, pair)
                out = _two_heads(o_ref, pair)
                centre = jnp.sum(grad.astype(F32) * out.astype(F32), axis=-1, keepdims=True)
                log_total = jnp.concatenate([l_ref[2 * pair], l_ref[2 * pair + 1]])
                query_wide = _beside(query, log_total)
                grad_wide = _beside(grad, jnp.broadcast_to(centre, grad.shape))
                dq = None
                for low in range(0, keys, chunk):
                    span = slice(low, low + chunk)
                    s = times_transposed(query_wide, k_ref[span, :])
                    if low >= masked:
                        s = s + bias_ref[:, span]
                    p = jnp.exp2(s)
                    ds = (p * times_transposed(grad_wide, v_ref[span, :])).astype(BF)
                    dv_ref[span, :] += contract_rows(p.astype(BF), grad)
                    dk_ref[span, :] += contract_rows(ds, query)
                    part = jnp.dot(ds, k_ref[span, :HEAD], preferred_element_type=F32)
                    dq = part if dq is None else dq + part
                _store_heads(dq_ref, pair, dq)
                return carry

            lax.fori_loop(0, q_ref.shape[1] // (2 * HEAD), pair_of_heads, 0)

    @pl.when(number == first + count - 1)
    def _():
        for k, piece in enumerate(sums):
            for i in range(STEPS):
                place = pl.ds(pl.multiple_of(table[k * STEPS + i], rows), rows)
                piece[i * rows : (i + 1) * rows, :HEAD] = dk_ref[place, :] * (1.0 / LOG2E)
                piece[i * rows : (i + 1) * rows, HEAD:] = dv_ref[place, :]


def attend_back(table, queries, grads, mixed, log_totals, pieces, query_at, opens, rows, first, count):
    tokens, width = queries.shape
    heads, cores = width // HEAD, len(pieces)
    group = cores * tokens
    chunk = group // STEPS
    piece = full(tokens, 2 * HEAD)
    column = pl.BlockSpec((rows, 1), lambda i, o: (i + first, 0))
    tile = pl.BlockSpec((rows, width), lambda i, o: (i + first, 0))
    return run(
        partial(_attend_back_kernel, cores=cores, chunk=chunk, rows=rows, first=first, count=count),
        "attend_back",
        (count,),
        (*pieces, queries, grads, mixed, log_totals, query_at, opens),
        [piece] * cores
        + [tile, tile, tile, pl.BlockSpec((heads, rows, HEAD), lambda i, o: (0, i + first, 0))]
        + [column, column],
        [((count * rows, width), BF)] + [((tokens, 2 * HEAD), F32)] * cores,
        [pl.BlockSpec((rows, width), lambda i, o: (i, 0))] + [piece] * cores,
        scalars=table,
        dear=True,
        scratch=[
            pltpu.VMEM((2 * rows, group), F32),
            pltpu.VMEM((group, 2 * HEAD), BF),
            pltpu.VMEM((group, 2 * HEAD), BF),
            pltpu.VMEM((group, HEAD), F32),
            pltpu.VMEM((group, HEAD), F32),
        ],
    )


def _expert_kernel(
    x_ref, pulled_ref, chosen_ref, own_ref, router_ref, gate_ref, up_ref,
    dx_ref, dg_ref, du_ref, h_ref, c_ref,
):
    rows = x_ref[...]
    logits = jnp.dot(rows, router_ref[...], preferred_element_type=F32)
    chosen = chosen_ref[...].astype(F32)
    logits = jnp.where(chosen > 0.0, logits, -1e30)
    raised = jnp.exp(logits - jnp.max(logits, axis=-1, keepdims=True)) * chosen
    weight = jnp.sum(raised * own_ref[...], axis=-1, keepdims=True)
    weight = weight / jnp.maximum(jnp.sum(raised, axis=-1, keepdims=True), 1e-30)
    gate = jnp.dot(rows, gate_ref[...], preferred_element_type=F32)
    up = jnp.dot(rows, up_ref[...], preferred_element_type=F32)
    sigma = jax.nn.sigmoid(gate)
    swish = gate * sigma
    hidden = swish * up
    pulled = pulled_ref[...].astype(F32)
    c_ref[...] = jnp.sum(hidden * pulled, axis=-1, keepdims=True)
    h_ref[...] = (weight * hidden).astype(BF)
    pulled = weight * pulled
    gate_grad = (pulled * up * sigma * (1.0 + gate * (1.0 - sigma))).astype(BF)
    up_grad = (pulled * swish).astype(BF)
    dg_ref[...] = gate_grad
    du_ref[...] = up_grad
    dx = times_transposed(gate_grad, gate_ref[...]) + times_transposed(up_grad, up_ref[...])
    dx_ref[...] = dx.astype(BF)


def expert(rows, pulled, chosen, own, router, gate, up):
    count, width = rows.shape
    hidden = gate.shape[1]
    lanes = chosen.shape[1]
    step = min(count, 256)
    across = pl.BlockSpec((step, width), lambda i: (i, 0))
    thin = pl.BlockSpec((step, hidden), lambda i: (i, 0))
    column = pl.BlockSpec((step, 1), lambda i: (i, 0))
    return run(
        _expert_kernel,
        "expert",
        (count // step,),
        (rows, pulled, chosen, own, router, gate, up),
        [across, thin, pl.BlockSpec((step, lanes), lambda i: (i, 0)), full(1, lanes)]
        + [full(width, lanes), full(width, hidden), full(width, hidden)],
        [((count, width), BF)] + [((count, hidden), BF)] * 3 + [((count, 1), F32)],
        [across, thin, thin, thin, column],
        free=(0,),
        dear=True,
    )


def _rows_kernel(*refs):
    count = (len(refs) - 1) // 2
    total = None
    for left, right in zip(refs[:count], refs[count:-1]):
        part = contract_rows(left[...], right[...])
        total = part if total is None else total + part
    refs[-1][...] = total


def contract_chunks(lefts, rights):
    count, tall = lefts[0].shape
    wide = rights[0].shape[1]
    step = min(tall, 256)
    return run(
        _rows_kernel,
        "contract_chunks",
        (tall // step,),
        (*lefts, *rights),
        [pl.BlockSpec((count, step), lambda i: (0, i))] * len(lefts)
        + [full(count, wide)] * len(rights),
        [((tall, wide), F32)],
        [pl.BlockSpec((step, wide), lambda i: (i, 0))],
    )[0]


def body(
    layer_input,
    attn_gain,
    w_query,
    key_matrix,
    value_matrix,
    query_gain,
    key_gain,
    w_out,
    moe_gain,
    router,
    expert_gate,
    expert_up,
    expert_down,
    expert_ids,
    cont_segment,
    out_grad,
):
    tokens, width = layer_input.shape
    dps, _, cores = sizes = [lax.axis_size(a) for a in ALL]
    devices = math.prod(sizes)
    dp, z, c = [lax.axis_index(a) for a in ALL]
    experts = router.shape[1]
    capacity = tokens * TOP // experts
    plane = dps * cores
    slots = plane * capacity
    order = jnp.array(ORDER, jnp.int32)[z]
    where_block = jnp.array([[o.index(b) for b in range(STEPS)] for o in ORDER], jnp.int32)[z]
    own_heads = HQ // (STEPS * cores)
    heads = HQ // STEPS
    head_cols = heads * HEAD
    own_cols = own_heads * HEAD

    rows_dev = router.shape[0]
    id_cols = tokens * TOP // rows_dev
    router_pad = -(experts + 2 + id_cols) % 128
    small = jnp.concatenate(
        [
            router,
            attn_gain[:, None],
            moe_gain[:, None],
            expert_ids.astype(BF).reshape(rows_dev, id_cols),
            jnp.zeros((rows_dev, router_pad), BF),
        ],
        axis=1,
    )
    packed = pack(key_matrix, value_matrix, small)
    arrived = lax.all_gather(layer_input, "z", axis=0, tiled=True)
    query_own = from_dps(w_query, dp).reshape(width, own_cols)
    packed = lax.all_to_all(packed, "z", split_axis=0, concat_axis=0, tiled=True)
    packed, w_out, order, where_block = hold(packed, w_out, order, where_block)
    w_back = lax.all_to_all(w_out, "dp", split_axis=0, concat_axis=0, tiled=True)

    at_slot = jnp.arange(capacity, dtype=jnp.int32)
    earlier = (jnp.arange(tokens)[:, None] > jnp.arange(tokens)[None, :]).astype(BF)

    def plan(ids):
        chosen = jnp.any(ids[:, :, None] == jnp.arange(experts, dtype=jnp.int32), axis=1)
        ranks = jnp.dot(earlier, chosen.astype(BF), preferred_element_type=F32).astype(jnp.int32)
        ranks = jnp.where(chosen & (ranks < capacity), ranks, -1)
        in_plane = lax.dynamic_index_in_dim(
            ranks.reshape(tokens, dps, STEPS, cores), z, 2, keepdims=False
        ).reshape(tokens, plane)
        pick = (in_plane[:, :, None] == at_slot).reshape(tokens, slots).astype(BF)
        back = (in_plane.T[:, None, :] == at_slot[:, None]).reshape(slots, tokens).astype(BF)
        return chosen, ranks, pick, back

    def to_plane(rows):
        return lax.all_to_all(rows, PLANE, split_axis=0, concat_axis=0, tiled=True)

    zs = jnp.stack([z, jnp.int32(0)])
    own_chosen, own_ranks, own_pick, own_back = plan(expert_ids)
    own_slots = own_ranks[:, :, None] == at_slot
    first_id = 2 * HEAD + experts + 2
    ids = packed[:, :, first_id : first_id + id_cols].astype(jnp.int32)
    ids = ids.reshape(STEPS, tokens, TOP)
    ids = [lax.dynamic_index_in_dim(ids, order[i], 0, keepdims=False) for i in range(STEPS)]
    packed = jnp.stack(cores_in_order(packed, c), axis=1).reshape(w_query.shape[0], -1)
    packed = from_dps(packed, dp).reshape(width, -1)
    w_in = cores_in_order(query_own, c)
    *w_in, packed, ids, w_back = hold(*w_in, packed, ids, w_back)
    w_back = lax.all_to_all(w_back, "z", split_axis=0, concat_axis=0, tiled=True)
    w_back = lax.all_gather(w_back, PLANE, axis=0, tiled=True)
    rest = packed[:, 2 * HEAD :]
    lanes = rest.shape[1]
    router_all = rest[:, :experts]
    attn_gain_all = rest[:, experts].astype(F32)[None, :]
    moe_gain_all = rest[:, experts + 1].astype(F32)[None, :]
    w_in = jnp.concatenate([*w_in, packed[:, : 2 * HEAD]], axis=1)
    plans = [(own_chosen, own_ranks, own_pick, own_back)] + [plan(i) for i in ids[1:]]
    pick = [p[2] for p in plans]
    back = [p[3] for p in plans]
    slot_chosen = jnp.stack(
        [
            jnp.dot(back[i], jnp.pad(p[0].astype(BF), ((0, 0), (0, lanes - experts))))
            for i, p in enumerate(plans)
        ]
    ).reshape(STEPS, plane, capacity, lanes)
    slot_chosen = slot_chosen.transpose(1, 0, 2, 3)
    own_expert = dp * (STEPS * cores) + z * cores + c
    own_expert = (jnp.arange(lanes)[None, :] == own_expert).astype(F32)

    where_at, opens = group_layout(cont_segment[0])
    group = where_at.shape[0]

    def own_rows(table):
        mine = lax.dynamic_index_in_dim(table.reshape(STEPS, cores, tokens), c, 1, keepdims=False)
        return mine.reshape(-1)

    cosine, sine = angle_tables(own_rows(where_at), HEAD)
    query_at = own_rows(jnp.arange(group, dtype=jnp.int32))[:, None]
    opens = own_rows(opens)[:, None]
    numbers = jnp.arange(STEPS, dtype=jnp.int32)
    table = jnp.concatenate([(numbers * cores + (c + k) % cores) * tokens for k in range(cores)])
    query_gain_f = query_gain.astype(F32)[None, :]
    key_gain_f = key_gain.astype(F32)[None, :]
    scale = LOG2E / math.sqrt(HEAD)
    query_gain_s = query_gain_f * scale
    gate_w, up_w, down_w = expert_gate[0], expert_up[0], expert_down[0]
    at_block = [jnp.stack([z, order[i]]) for i in range(STEPS)]

    (
        upstream_block, w_in, pick, back, slot_chosen, cosine, sine, query_at, opens, table,
        query_gain_s, key_gain_f, at_block, own_expert, attn_gain_all, moe_gain_all, rest,
    ) = hold(
        out_grad, w_in, pick, back, slot_chosen, cosine, sine, query_at, opens, table,
        query_gain_s, key_gain_f, at_block, own_expert, attn_gain_all, moe_gain_all, rest,
    )
    g_up, g_down = spread_first(upstream_block)
    g0 = to_plane(dispatch(zs, back[0], [upstream_block], (0, 0, 0, 0)))
    normed, raw, queries, key_value_rows = project(
        arrived, attn_gain_all, w_in, cosine, sine, query_gain_s, key_gain_f, tokens
    )
    pieces = [key_value_rows, *other_cores(key_value_rows)]
    queries, g_up, g_down, g0, *pieces = hold(queries, g_up, g_down, g0, *pieces)
    g_up2, g_down2 = spread_second(g_up, g_down)
    g1 = to_plane(dispatch(zs, back[1], [g_up, g_down], FIRST))
    mixed, log_totals = attend(table, queries, pieces, query_at, opens, tokens)
    mixed, g_up2, g_down2 = hold(mixed, g_up2, g_down2)
    g_last = spread_third(g_up2, g_down2, z)
    w_back = w_back.reshape(dps, cores, STEPS, dps // STEPS, -1, width).transpose(3, 2, 1, 0, 4, 5)
    w_back = w_back.reshape(head_cols, width)
    attended = matmul(mixed, w_back, "nn", 4, "columns")
    attended, g_last, g0, g1, g_up2, g_down2 = hold(attended, g_last, g0, g1, g_up2, g_down2)
    attended = lax.psum_scatter(attended, "z", scatter_dimension=0, tiled=True)
    g2 = to_plane(dispatch(zs, back[2], [g_up, g_down, g_up2, g_down2], SECOND))
    pulled0 = matmul(g0, down_w, "nt", 2, "rows", F32)
    g2, g_last, pulled0 = hold(g2, g_last, pulled0)
    g3 = to_plane(dispatch(zs, back[3], [g_up2, g_down2, g_last], THIRD))
    pulled1 = matmul(g1, down_w, "nt", 2, "rows", F32)
    pulled2 = matmul(g2, down_w, "nt", 2, "rows", F32)
    g3, pulled1, pulled2, slot_chosen = hold(g3, pulled1, pulled2, slot_chosen)
    slot_chosen = to_plane(slot_chosen)
    slot_chosen = slot_chosen.transpose(1, 0, 2, 3).reshape(STEPS, slots, lanes)
    slot_chosen = [slot_chosen[i] for i in range(STEPS)]
    pulled3 = matmul(g3, down_w, "nt", 2, "rows", F32)
    attended, pulled3, slot_chosen = hold(attended, pulled3, slot_chosen)
    upstream_slots = [g0, g1, g2, g3]
    resid, moe_low = add_and_norm(layer_input, moe_gain_all, (attended,))

    def through(i, rows, pulled):
        return expert(rows, pulled, slot_chosen[i], own_expert, rest, gate_w, up_w)

    m_up, m_down = spread_first(moe_low)
    r0 = to_plane(dispatch(zs, back[0], [moe_low], (0, 0, 0, 0)))
    m_up, m_down = hold(m_up, m_down)
    m_up2, m_down2 = spread_second(m_up, m_down)
    r1 = dispatch(zs, back[1], [m_up, m_down], FIRST)
    r1, r0 = hold(r1, r0)
    r1 = to_plane(r1)
    e0 = through(0, r0, pulled0)
    m_up2, m_down2, e0 = hold(m_up2, m_down2, e0)
    m_last = spread_third(m_up2, m_down2, z)
    r2 = dispatch(zs, back[2], [m_up, m_down, m_up2, m_down2], SECOND)
    r2, r1 = hold(r2, r1)
    r2 = to_plane(r2)
    e1 = through(1, r1, pulled1)
    m_last, e1 = hold(m_last, e1)
    r3 = dispatch(zs, back[3], [m_up2, m_down2, m_last], THIRD)
    r3, r2 = hold(r3, r2)
    r3 = to_plane(r3)
    e2 = through(2, r2, pulled2)
    r3, e2 = hold(r3, e2)
    e3 = through(3, r3, pulled3)
    rows = [r0, r1, r2, r3]
    slot_grads, gate_grads, up_grads, hiddens, centres = [list(v) for v in zip(e0, e1, e2, e3)]
    d0, d1, d2, d3 = slot_grads
    b3 = to_plane(d3)
    moe_row, d2, centres, hiddens = hold(moe_low, d2, centres, hiddens)
    logits = jnp.dot(moe_row, router_all, preferred_element_type=F32)
    logits = jnp.where(own_chosen, logits, -jnp.inf)
    raised = jnp.exp(logits - jnp.max(logits, axis=-1, keepdims=True))
    gates = raised / jnp.sum(raised, axis=-1, keepdims=True)
    stacked = jnp.stack([v.reshape(dps, cores, capacity) for v in centres])
    centre_back = jnp.stack(
        [
            lax.dynamic_index_in_dim(stacked, where_block[b], 0, keepdims=False)
            for b in range(STEPS)
        ],
        axis=1,
    ).reshape(experts, capacity)
    h0, h1, h2, h3 = hiddens

    def produced(value):
        return matmul(value, down_w, "nn", 2, "columns", dear=True)

    p3 = produced(h3)
    b3, d2, p3, centre_back, gates, h0, h1, h2 = hold(
        b3, d2, p3, centre_back, gates, h0, h1, h2
    )
    b2 = to_plane(d2)
    (c3,) = line_part(zs, pick[3], b3, tokens)
    c3, h2 = hold(c3, h2)
    got = sum_first(c3)
    p2 = produced(h2)
    b2, d1, h1, p2 = hold(b2, d1, h1, p2)
    b1 = to_plane(d1)
    p1 = produced(h1)
    got, b2, p1 = hold(got, b2, p1)
    c2, middle = line_part(zs, pick[2], b2, tokens, 1, (c3, got))
    s_up, s_down = sum_second(middle)
    b1, d0, h0 = hold(b1, d0, h0)
    b0 = to_plane(d0)
    p0 = produced(h0)
    s_up, s_down, b1, p0 = hold(s_up, s_down, b1, p0)
    s_up, s_down = line_part(zs, pick[1], b1, tokens, 2, (c2, s_up, s_down))
    s_up, s_down = sum_third(s_up, s_down)
    b0, centre_back = hold(b0, centre_back)
    centre_back = lax.all_to_all(centre_back, ALL, split_axis=0, concat_axis=0, tiled=True)
    (c0,) = line_part(zs, pick[0], b0, tokens)
    weight_grad = jnp.sum(jnp.where(own_slots, centre_back[None], 0.0), axis=2)
    logit_grad = (
        gates * (weight_grad - jnp.sum(gates * weight_grad, axis=-1, keepdims=True))
    ).astype(BF)
    logit_wide = jnp.pad(logit_grad, ((0, 0), (0, lanes - experts)))
    s_up, s_down, c0, logit_wide = hold(s_up, s_down, c0, logit_wide)
    resid_grad, resid_low, moe_gain_grad = norm_back(
        resid, moe_gain_all, out_grad, (c0, s_up, s_down), logit_wide, rest
    )

    def by_core(value, axis):
        size = value.shape[axis] // cores
        return [
            lax.dynamic_slice_in_dim(value, (c + k) % cores * size, size, axis)
            for k in range(cores)
        ]

    resid_low, p3, logit_grad, hiddens, rows = hold(resid_low, p3, logit_grad, hiddens, rows)
    resid_all = lax.all_gather(resid_low, "z", axis=0, tiled=True)
    o3 = to_plane(p3)
    down_weight_grad = contract_chunks(hiddens, upstream_slots)
    router_grad = contract_rows(moe_low, logit_grad)
    o3, p2, rows, down_weight_grad, router_grad = hold(
        o3, p2, rows, down_weight_grad, router_grad
    )
    o2 = to_plane(p2)
    (o3,) = line_part(zs, pick[3], o3, tokens)
    up_weight_grad = contract_chunks(rows, up_grads)
    o2, p1, rows, up_weight_grad = hold(o2, p1, rows, up_weight_grad)
    o1 = to_plane(p1)
    gate_weight_grad = contract_chunks(rows, gate_grads)
    resid_all, o3, o2, gate_weight_grad = hold(resid_all, o3, o2, gate_weight_grad)
    t_got = sum_first(o3)
    mixed_grad = matmul(resid_all, w_back, "nt", 4, "rows", dear=True)
    mixed_grad, resid_all = hold(mixed_grad, resid_all)
    out_weight_grad = matmul(mixed, resid_all, "tn", 4, "columns")
    out_weight_grad = out_weight_grad.reshape(dps // STEPS, STEPS, cores, dps, -1, width)
    out_weight_grad = out_weight_grad.transpose(3, 2, 1, 0, 4, 5).reshape(head_cols, width)
    out_weight_grad, mixed_grad, t_got, o2, o3 = hold(out_weight_grad, mixed_grad, t_got, o2, o3)
    out_weight_grad = lax.psum_scatter(out_weight_grad, PLANE, scatter_dimension=0, tiled=True)
    o2, middle = line_part(zs, pick[2], o2, tokens, 1, (o3, t_got))
    middle, o2, mixed_grad = hold(middle, o2, mixed_grad)
    t_up, t_down = sum_second(middle)
    back = partial(attend_back, table, queries, mixed_grad, mixed, log_totals, pieces, query_at)
    near_grads, *near_sums = back(opens, tokens, 0, STEPS - 1)
    near_grads, t_up, t_down, o1, o2, mixed_grad = hold(
        near_grads, t_up, t_down, o1, o2, mixed_grad
    )
    t_up, t_down = line_part(zs, pick[1], o1, tokens, 2, (o2, t_up, t_down))
    t_up, t_down, mixed_grad = hold(t_up, t_down, mixed_grad)
    t_up, t_down = sum_third(t_up, t_down)
    last_grads, *last_sums = attend_back(
        table, queries, mixed_grad, mixed, log_totals, pieces, query_at, opens, tokens, STEPS - 1, 1
    )
    last_grads, out_weight_grad, *last_sums = hold(last_grads, out_weight_grad, *last_sums)
    own_sums, *other_sums = [a + b for a, b in zip(near_sums, last_sums)]
    sums = sum_over_cores([own_sums, *[v.astype(BF) for v in other_sums]])
    sums, t_up, t_down = hold(sums, t_up, t_down)
    normed_grad, raw_grad, query_gain_grad, key_gain_grad = project_back(
        raw, near_grads, last_grads, sums, w_in, cosine, sine, query_gain_f, key_gain_f, tokens
    )
    normed_grad, raw_grad, out_weight_grad, p0 = hold(normed_grad, raw_grad, out_weight_grad, p0)
    normed_sum = lax.psum_scatter(normed_grad, "z", scatter_dimension=0, tiled=True)
    o0 = to_plane(p0)
    in_grad = matmul(normed, raw_grad, "tn", 4, "rows")
    in_grad, o0 = hold(in_grad, o0)
    out_weight_grad = exchange(out_weight_grad.reshape(STEPS, -1, width), "z")
    query_share = sum_over_cores(by_core(in_grad[:, :head_cols], 1)).astype(BF)
    key_value_grad = in_grad[:, head_cols:].reshape(dps, STEPS, cores, rows_dev, 2 * HEAD)
    key_value_grad = sum_over_cores(
        [part[:, :, 0] for part in by_core(key_value_grad, 2)]
    ).astype(BF)
    attn_gain_grad = jnp.sum(normed_grad.astype(F32) * normed.astype(F32), axis=0)[None, :]
    attn_gain_grad = attn_gain_grad / attn_gain_all

    def to_owners(value):
        columns = value.shape[0]
        split = value.reshape(columns, devices, rows_dev).transpose(1, 0, 2)
        return split.reshape(devices, columns * rows_dev)

    gain_row = jnp.concatenate([query_gain_grad, key_gain_grad], axis=1)
    late = jnp.concatenate(
        [
            to_owners(jnp.concatenate([router_grad.T, moe_gain_grad, attn_gain_grad])),
            jnp.broadcast_to(gain_row, (devices, 2 * HEAD)),
        ],
        axis=1,
    )
    query_share, key_value_grad, late, out_weight_grad, o0 = hold(
        query_share, key_value_grad, late, out_weight_grad, o0
    )
    late = lax.all_to_all(late, ALL, split_axis=0, concat_axis=0, tiled=True)
    query_weight_grad = over_dps(query_share.reshape(dps, -1, own_cols), dp)
    key_value_grad = over_dps(key_value_grad, dp).astype(BF)
    out_weight_grad = exchange(out_weight_grad.reshape(dps, -1, width), "dp")
    out_weight_grad = out_weight_grad.reshape(-1, width).astype(F32)
    (o0,) = line_part(zs, pick[0], o0, tokens)
    output = resid + (o0.astype(F32) + t_up.astype(F32) + t_down.astype(F32))
    output = output.astype(BF)
    late = jnp.sum(late, axis=0)
    gain_sums = late[-2 * HEAD :].reshape(2, HEAD)
    owned = late[: -2 * HEAD].reshape(experts + 2, rows_dev)
    key_value_grad = exchange(key_value_grad, "z")
    key_value_grad = key_value_grad.transpose(1, 0, 2).astype(F32)
    key_weight_grad = key_value_grad[:, :, :HEAD].reshape(rows_dev, -1)
    value_weight_grad = key_value_grad[:, :, HEAD:].reshape(rows_dev, -1)
    (input_grad,) = norm_back(layer_input, attn_gain_all, resid_grad, (normed_sum,))
    return (
        output,
        input_grad,
        owned[experts + 1],
        query_weight_grad,
        key_weight_grad,
        value_weight_grad,
        gain_sums[0],
        gain_sums[1],
        out_weight_grad,
        owned[experts],
        owned[:experts].T,
        gate_weight_grad[None],
        up_weight_grad[None],
        down_weight_grad[None],
    )


def solution(mesh):
    dps, sequence = mesh.devices.shape
    inner = Mesh(mesh.devices.reshape(dps, STEPS, sequence // STEPS), ALL)
    rows = P(ALL, None)
    placed = (
        rows,
        P(ALL),
        P("dp", ("z", "core")),
        rows,
        rows,
        P(),
        P(),
        rows,
        P(ALL),
        rows,
        P(ALL, None, None),
        P(ALL, None, None),
        P(ALL, None, None),
        rows,
        P("dp", None),
        rows,
    )
    return jax.shard_map(
        body,
        mesh=inner,
        in_specs=placed,
        out_specs=(
            rows,
            rows,
            P(ALL),
            P("dp", ("z", "core")),
            rows,
            rows,
            P(),
            P(),
            rows,
            P(ALL),
            rows,
            P(ALL, None, None),
            P(ALL, None, None),
            P(ALL, None, None),
        ),
        check_vma=False,
    )
```

```python
from functools import partial
import math

import jax
import jax.numpy as jnp
from jax import lax
from jax.experimental import pallas as pl
from jax.experimental.pallas import tpu as pltpu
from jax.sharding import Mesh, PartitionSpec as P

HQ = 32
KEY_VALUE_HEADS = 4
TOP = 8
PROMPT = 1024
NCONT = 4
HEAD = 128

EPS = 1e-06
THETA = 1000000.0
LOG2E = 1.4426950408889634
BF = jnp.bfloat16
F32 = jnp.float32

STEPS = 4
ORDER = ((0, 1, 2, 3), (1, 0, 2, 3), (2, 3, 1, 0), (3, 2, 1, 0))
PLANE = ("dp", "core")
ALL = ("dp", "z", "core")


def angle_tables(where_at, head_width):
    ranks = jnp.arange(head_width // 2, dtype=F32) * (2.0 / head_width)
    inverse = jnp.exp(-ranks * math.log(THETA))
    angles = where_at.astype(F32)[:, None] * inverse[None, :]
    cosine, sine = jnp.cos(angles), jnp.sin(angles)
    return (
        jnp.concatenate([cosine, cosine], axis=-1),
        jnp.concatenate([-sine, sine], axis=-1),
    )


def group_layout(segment):
    length = segment.shape[0]
    one_hot = (segment[:, None] == jnp.arange(NCONT, dtype=jnp.int32)[None, :]).astype(jnp.int32)
    counted = jnp.sum(one_hot, axis=0)
    before = jnp.arange(NCONT)[:, None] > jnp.arange(NCONT)[None, :]
    starts = jnp.sum(jnp.where(before, counted[None, :], 0), axis=1)
    begins = jnp.sum(one_hot * starts[None, :], axis=1)
    within = jnp.arange(length, dtype=jnp.int32) - begins
    where_at = jnp.concatenate([jnp.arange(PROMPT, dtype=jnp.int32), PROMPT + within])
    opens = jnp.concatenate([jnp.full((PROMPT,), PROMPT, jnp.int32), PROMPT + begins])
    return (where_at, opens)


def contract_rows(left, right):
    return lax.dot_general(left, right, (((0,), (0,)), ((), ())), preferred_element_type=F32)


def times_transposed(left, right):
    return lax.dot_general(left, right, (((1,), (1,)), ((), ())), preferred_element_type=F32)


def hold(*values):
    return lax.optimization_barrier(values)


def spread_first(block):
    return (
        lax.ppermute(block, "z", [(0, 1), (1, 2), (2, 3)]),
        lax.ppermute(block, "z", [(1, 0), (2, 1), (3, 2)]),
    )


def spread_second(up, down):
    return (
        lax.ppermute(up, "z", [(1, 2), (2, 3)]),
        lax.ppermute(down, "z", [(2, 1), (1, 0)]),
    )


def spread_third(up2, down2, z):
    return lax.ppermute(jnp.where(z == 2, up2, down2), "z", [(2, 3), (1, 0)])


FIRST = (1, 0, 1, 0)
SECOND = (3, 1, 0, 2)
THIRD = (2, 1, 0, 2)


def sum_first(third):
    return lax.ppermute(third, "z", [(0, 1), (3, 2)])


def sum_second(middle):
    return (
        lax.ppermute(middle, "z", [(0, 1), (1, 2)]),
        lax.ppermute(middle, "z", [(3, 2), (2, 1)]),
    )


def sum_third(up, down):
    return (
        lax.ppermute(up, "z", [(0, 1), (1, 2), (2, 3)]),
        lax.ppermute(down, "z", [(3, 2), (2, 1), (1, 0)]),
    )


def over_dps(value, dp):
    dps = value.shape[0]
    total = lax.dynamic_index_in_dim(value, dp, 0, keepdims=False).astype(F32)
    for k in range(1, dps):
        piece = lax.dynamic_index_in_dim(value, dp ^ k, 0, keepdims=False)
        total = total + lax.ppermute(piece, "dp", [(i, i ^ k) for i in range(dps)]).astype(F32)
    return total


def exchange(value, axis):
    size, me = value.shape[0], lax.axis_index(axis)
    own = lax.dynamic_index_in_dim(value, me, 0, keepdims=False)
    whole = lax.dynamic_update_index_in_dim(jnp.zeros_like(value), own, me, 0)
    for k in range(1, size):
        piece = lax.dynamic_index_in_dim(value, me ^ k, 0, keepdims=False)
        got = lax.ppermute(piece, axis, [(i, i ^ k) for i in range(size)])
        whole = lax.dynamic_update_index_in_dim(whole, got, me ^ k, 0)
    return whole


def from_dps(value, dp):
    dps = lax.axis_size("dp")
    whole = jnp.zeros((dps, *value.shape), value.dtype)
    whole = lax.dynamic_update_index_in_dim(whole, value, dp, 0)
    for k in range(1, dps):
        got = lax.ppermute(value, "dp", [(i, i ^ k) for i in range(dps)])
        whole = lax.dynamic_update_index_in_dim(whole, got, dp ^ k, 0)
    return whole


def other_cores(value):
    cores = lax.axis_size("core")
    return [
        lax.ppermute(value, "core", [((i + k) % cores, i) for i in range(cores)])
        for k in range(1, cores)
    ]


def cores_in_order(value, c):
    cores = lax.axis_size("core")
    pieces = [value, *other_cores(value)]
    ordered = []
    for n in range(cores):
        piece = pieces[0]
        for k in range(1, cores):
            piece = jnp.where((n - c) % cores == k, pieces[k], piece)
        ordered.append(piece)
    return ordered


def sum_over_cores(pieces):
    cores = lax.axis_size("core")
    total = pieces[0].astype(F32)
    for k in range(1, cores):
        got = lax.ppermute(pieces[k], "core", [(i, (i + k) % cores) for i in range(cores)])
        total = total + got.astype(F32)
    return total


CHEAP = pl.CostEstimate(flops=1, bytes_accessed=1, transcendentals=0)
DEAR = pl.CostEstimate(flops=10**11, bytes_accessed=1, transcendentals=0)


def run(kernel, name, grid, operands, in_specs, outs, out_specs, scalars=None, scratch=(), free=(), dear=False):
    prefetch = () if scalars is None else (scalars,)
    operands = [
        v if i in free else pltpu.with_memory_space_constraint(v, pltpu.HBM)
        for i, v in enumerate(operands)
    ]
    got = pl.pallas_call(
        kernel,
        grid_spec=pltpu.PrefetchScalarGridSpec(
            num_scalar_prefetch=len(prefetch),
            grid=grid,
            in_specs=in_specs,
            out_specs=out_specs,
            scratch_shapes=scratch,
        ),
        out_shape=[pltpu.HBM(shape, kind) for shape, kind in outs],
        compiler_params=pltpu.CompilerParams(vmem_limit_bytes=52 * 1024 * 1024),
        cost_estimate=DEAR if dear else CHEAP,
        name=name,
    )(*prefetch, *operands)
    return got


def full(*shape):
    return pl.BlockSpec(shape, lambda *_: (0,) * len(shape))


def _matmul_kernel(a_ref, b_ref, o_ref, *, dims):
    part = lax.dot_general(a_ref[...], b_ref[...], (dims, ((), ())), preferred_element_type=F32)
    o_ref[...] = part.astype(o_ref.dtype)


def matmul(a, b, kind, steps, by, out=BF, dear=False):
    dims = {"nn": ((1,), (0,)), "nt": ((1,), (1,)), "tn": ((0,), (0,))}[kind]
    rows = a.shape[1 - dims[0][0]]
    columns = b.shape[1 - dims[1][0]]
    a_spec, b_spec = full(*a.shape), full(*b.shape)
    if by == "rows":
        size = rows // steps
        if kind == "tn":
            a_spec = pl.BlockSpec((a.shape[0], size), lambda i: (0, i))
        else:
            a_spec = pl.BlockSpec((size, a.shape[1]), lambda i: (i, 0))
        o_spec = pl.BlockSpec((size, columns), lambda i: (i, 0))
    else:
        size = columns // steps
        if kind == "nt":
            b_spec = pl.BlockSpec((size, b.shape[1]), lambda i: (i, 0))
        else:
            b_spec = pl.BlockSpec((b.shape[0], size), lambda i: (0, i))
        o_spec = pl.BlockSpec((rows, size), lambda i: (0, i))
    return run(
        partial(_matmul_kernel, dims=dims),
        "matmul_" + kind,
        (steps,),
        (a, b),
        [a_spec, b_spec],
        [((rows, columns), out)],
        [o_spec],
        dear=dear,
    )[0]


def _dispatch_kernel(s_ref, pick_ref, *refs, sources):
    z, rows = s_ref[0], refs[0][...]
    for n in range(1, len(refs) - 1):
        here = False
        for at, source in enumerate(sources):
            if source == n:
                here = here | (z == at)
        rows = jnp.where(here, refs[n][...], rows)
    refs[-1][...] = jnp.dot(pick_ref[...], rows, preferred_element_type=F32).astype(BF)


def dispatch(scalars, pick, blocks, sources):
    slots, tokens = pick.shape
    width = blocks[0].shape[1]
    tile = pl.BlockSpec((tokens, 1024), lambda j, s: (0, j))
    return run(
        partial(_dispatch_kernel, sources=sources),
        "dispatch",
        (width // 1024,),
        (pick, *blocks),
        [full(slots, tokens)] + [tile] * len(blocks),
        [((slots, width), BF)],
        [pl.BlockSpec((slots, 1024), lambda j, s: (0, j))],
        scalars=scalars,
        free=(1, 2, 3, 4),
    )[0]


def _part_kernel(s_ref, a_ref, b_ref, *refs, step):
    z = s_ref[0]
    part = jnp.dot(a_ref[...], b_ref[...], preferred_element_type=F32)
    if step == 0:
        refs[0][...] = part.astype(BF)
    elif step == 1:
        third, got, part_ref, middle_ref = refs
        part_ref[...] = part.astype(BF)
        middle = jnp.where((z == 0) | (z == 3), part, third[...].astype(F32))
        middle_ref[...] = (middle + got[...].astype(F32)).astype(BF)
    else:
        second, up, down, up_ref, down_ref = refs
        other = second[...].astype(F32)
        up_ref[...] = (jnp.where(z == 1, other, part) + up[...].astype(F32)).astype(BF)
        down_ref[...] = (jnp.where(z == 2, other, part) + down[...].astype(F32)).astype(BF)


def line_part(scalars, a, b, tokens, step=0, more=()):
    width = b.shape[1]
    tile = pl.BlockSpec((tokens, 1024), lambda j, s: (0, j))
    return run(
        partial(_part_kernel, step=step),
        "line_part",
        (width // 1024,),
        (a, b, *more),
        [
            pl.BlockSpec((tokens, a.shape[1]), lambda j, s: (s[1], 0)),
            pl.BlockSpec((b.shape[0], 1024), lambda j, s: (0, j)),
        ]
        + [tile] * len(more),
        [((tokens, width), BF)] * (1 if step == 0 else 2),
        [tile] * (1 if step == 0 else 2),
        scalars=scalars,
        free=(1, 2, 3, 4),
    )


def _norm_kernel(x_ref, gain_ref, *refs):
    terms, (resid_ref, low_ref) = refs[:-2], refs[-2:]
    value = x_ref[...].astype(F32)
    for term in terms:
        value = value + term[...].astype(F32)
    resid_ref[...] = value
    factor = lax.rsqrt(jnp.mean(value * value, axis=-1, keepdims=True) + EPS)
    low_ref[...] = (value * factor * gain_ref[...]).astype(BF)


def add_and_norm(x, gain, terms):
    tokens, width = x.shape
    step = min(tokens, 64)
    tile = pl.BlockSpec((step, width), lambda i: (i, 0))
    return run(
        _norm_kernel,
        "add_and_norm",
        (tokens // step,),
        (x, gain, *terms),
        [tile, full(1, width)] + [tile] * len(terms),
        [((tokens, width), F32), ((tokens, width), BF)],
        [tile, tile],
    )


def _norm_back_kernel(v_ref, gain_ref, above_ref, *refs, logits):
    if logits:
        logit_ref, router_ref, *terms, total_ref, low_ref, gain_grad_ref = refs
    else:
        *terms, total_ref = refs
    grad = sum([term[...].astype(F32) for term in terms])
    if logits:
        grad = grad + times_transposed(logit_ref[...], router_ref[...])
    value = v_ref[...].astype(F32)
    factor = lax.rsqrt(jnp.mean(value * value, axis=-1, keepdims=True) + EPS)
    unit = value * factor
    if logits:

        @pl.when(pl.program_id(0) == 0)
        def _():
            gain_grad_ref[...] = jnp.zeros_like(gain_grad_ref)

        gain_grad_ref[...] += jnp.sum(grad * unit, axis=0, keepdims=True)
    grad = grad * gain_ref[...]
    shift = jnp.mean(grad * unit, axis=-1, keepdims=True)
    total = above_ref[...].astype(F32) + factor * (grad - unit * shift)
    total_ref[...] = total
    if logits:
        low_ref[...] = total.astype(BF)


def norm_back(value, gain, above, terms, logit_grad=None, router=None):
    tokens, width = value.shape
    step = min(tokens, 64)
    tile = pl.BlockSpec((step, width), lambda i: (i, 0))
    operands, specs = [value, gain, above], [tile, full(1, width), tile]
    outs, out_specs = [((tokens, width), F32)], [tile]
    if logit_grad is not None:
        lanes = logit_grad.shape[1]
        operands += [logit_grad, router]
        specs += [pl.BlockSpec((step, lanes), lambda i: (i, 0)), full(width, lanes)]
        outs += [((tokens, width), BF), ((1, width), F32)]
        out_specs += [tile, full(1, width)]
    return run(
        partial(_norm_back_kernel, logits=logit_grad is not None),
        "norm_back",
        (tokens // step,),
        (*operands, *terms),
        specs + [tile] * len(terms),
        outs,
        out_specs,
    )


def _pack_kernel(key_ref, value_ref, small_ref, out_ref):
    for at in range(STEPS):
        cols = slice(at * HEAD, (at + 1) * HEAD)
        out_ref[at, :, :HEAD] = key_ref[:, cols]
        out_ref[at, :, HEAD : 2 * HEAD] = value_ref[:, cols]
        out_ref[at, :, 2 * HEAD :] = small_ref[...]


def pack(key, value, small):
    rows = small.shape[0]
    lanes = 2 * HEAD + small.shape[1]
    return run(
        _pack_kernel,
        "pack",
        (1,),
        (key, value, small),
        [full(*key.shape), full(*value.shape), full(*small.shape)],
        [((STEPS, rows, lanes), BF)],
        [full(STEPS, rows, lanes)],
    )[0]


def _gain_kernel(grad_ref, value_ref, gain_ref, out_ref):
    @pl.when(pl.program_id(0) == 0)
    def _():
        out_ref[...] = jnp.zeros_like(out_ref)

    product = grad_ref[...].astype(F32) * value_ref[...].astype(F32)
    out_ref[...] += jnp.sum(product, axis=0, keepdims=True)

    @pl.when(pl.program_id(0) == pl.num_programs(0) - 1)
    def _():
        out_ref[...] = out_ref[...] / gain_ref[...]


def gain_sum(grad, value, gain):
    tokens, width = grad.shape
    tile = pl.BlockSpec((tokens // STEPS, width), lambda i: (i, 0))
    return run(
        _gain_kernel,
        "gain_sum",
        (STEPS,),
        (grad, value, gain),
        [tile, tile, full(1, width)],
        [((1, width), F32)],
        [full(1, width)],
    )[0]


def _lane_mean(value):
    ones = jnp.full((HEAD, HEAD), 1.0 / HEAD, BF)
    return jnp.dot(value.astype(BF), ones, preferred_element_type=F32)


def _project_kernel(
    x_ref, gain_ref, w_ref, cos_ref, sin_ref, qg_ref, kg_ref, n_ref, raw_ref, q_ref, kv_ref
):
    x = x_ref[...].astype(F32)
    factor = lax.rsqrt(jnp.mean(x * x, axis=-1, keepdims=True) + EPS)
    normed = (x * factor * gain_ref[...]).astype(BF)
    n_ref[...] = normed
    raw_ref[...] = jnp.dot(normed, w_ref[...], preferred_element_type=F32)
    cosine, sine = cos_ref[...], sin_ref[...]
    heads = q_ref.shape[1] // HEAD
    for h in range(heads + 1):
        cols = slice(h * HEAD, (h + 1) * HEAD)
        value = raw_ref[:, cols]
        factor = lax.rsqrt(_lane_mean(value * value) + EPS)
        value = value * factor * (qg_ref[...] if h < heads else kg_ref[...])
        value = (value * cosine + pltpu.roll(value, HEAD // 2, 1) * sine).astype(BF)
        if h < heads:
            q_ref[:, cols] = value
        else:
            kv_ref[:, :HEAD] = value
    kv_ref[:, HEAD:] = raw_ref[:, (heads + 1) * HEAD :].astype(BF)


def project(x, gain, w_in, cosine, sine, query_gain, key_gain, rows):
    tokens, width = x.shape
    columns = w_in.shape[1]

    def tile(size):
        return pl.BlockSpec((rows, size), lambda i: (i, 0))

    return run(
        _project_kernel,
        "project",
        (tokens // rows,),
        (x, gain, w_in, cosine, sine, query_gain, key_gain),
        [tile(width), full(1, width), full(width, columns), tile(HEAD), tile(HEAD)]
        + [full(1, HEAD)] * 2,
        [
            ((tokens, width), BF),
            ((tokens, columns), F32),
            ((tokens, columns - 2 * HEAD), BF),
            ((tokens, 2 * HEAD), BF),
        ],
        [tile(width), tile(columns), tile(columns - 2 * HEAD), tile(2 * HEAD)],
        dear=True,
    )


def _project_back_kernel(
    raw_ref, near_ref, last_ref, dkv_ref, w_ref, cos_ref, sin_ref, qg_ref, kg_ref,
    ng_ref, rg_ref, dqg_ref, dkg_ref,
):
    @pl.when(pl.program_id(0) == 0)
    def _():
        dqg_ref[...] = jnp.zeros_like(dqg_ref)
        dkg_ref[...] = jnp.zeros_like(dkg_ref)

    cosine, sine = cos_ref[...], sin_ref[...]
    heads = near_ref.shape[1] // HEAD
    at_last = pl.program_id(0) == STEPS - 1
    for h in range(heads + 1):
        cols = slice(h * HEAD, (h + 1) * HEAD)
        value = raw_ref[:, cols]
        factor = lax.rsqrt(_lane_mean(value * value) + EPS)
        unit = value * factor
        if h < heads:
            grad = jnp.where(at_last, last_ref[:, cols], near_ref[:, cols]).astype(F32) * (1.0 / math.sqrt(HEAD))
        else:
            grad = dkv_ref[:, :HEAD]
        grad = grad * cosine + pltpu.roll(grad * sine, HEAD // 2, 1)
        gain_grad = jnp.sum(grad * unit, axis=0, keepdims=True)
        if h < heads:
            dqg_ref[...] += gain_grad
            grad = grad * qg_ref[...]
        else:
            dkg_ref[...] += gain_grad
            grad = grad * kg_ref[...]
        shift = _lane_mean(grad * unit)
        rg_ref[:, cols] = (factor * (grad - unit * shift)).astype(BF)
    rg_ref[:, (heads + 1) * HEAD :] = dkv_ref[:, HEAD:].astype(BF)
    ng_ref[...] = times_transposed(rg_ref[...], w_ref[...]).astype(BF)


def project_back(raw, near, last, key_value_grads, w_in, cosine, sine, query_gain, key_gain, rows):
    tokens, columns = raw.shape
    width = w_in.shape[0]

    def tile(size):
        return pl.BlockSpec((rows, size), lambda i: (i, 0))

    return run(
        _project_back_kernel,
        "project_back",
        (tokens // rows,),
        (raw, near, last, key_value_grads, w_in, cosine, sine, query_gain, key_gain),
        [
            tile(columns),
            pl.BlockSpec((rows, columns - 2 * HEAD), lambda i: (jnp.minimum(i, STEPS - 2), 0)),
            full(rows, columns - 2 * HEAD),
            tile(2 * HEAD),
            full(width, columns),
            tile(HEAD),
            tile(HEAD),
            full(1, HEAD),
            full(1, HEAD),
        ],
        [((tokens, width), BF), ((tokens, columns), BF), ((1, HEAD), F32), ((1, HEAD), F32)],
        [tile(width), tile(columns), full(1, HEAD), full(1, HEAD)],
        dear=True,
    )


def _mask_bias(at_ref, opens_ref, bias_ref, low, high):
    rows = at_ref.shape[0]
    key_at = low + lax.broadcasted_iota(jnp.int32, (rows, high - low), 1)
    query_at = at_ref[...]
    allowed = (key_at <= query_at) & ((key_at < PROMPT) | (key_at >= opens_ref[...]))
    bias = jnp.where(allowed, 0.0, -1e30).astype(F32)
    bias_ref[:rows, low:high] = bias
    bias_ref[rows:, low:high] = bias


def _spans(number, chunk):
    return (number + 1) * chunk, min(number * chunk, PROMPT)


def _place_keys(table, pieces, k_ref, v_ref, rows):
    for k, piece in enumerate(pieces):
        for i in range(STEPS):
            place = pl.ds(pl.multiple_of(table[k * STEPS + i], rows), rows)
            k_ref[place, :HEAD] = piece[i * rows : (i + 1) * rows, :HEAD]
            v_ref[place, :HEAD] = piece[i * rows : (i + 1) * rows, HEAD:]


def _two_heads(ref, pair):
    first = pl.multiple_of(pair * 2 * HEAD, 2 * HEAD)
    return jnp.concatenate([ref[:, pl.ds(first, HEAD)], ref[:, pl.ds(first + HEAD, HEAD)]])


def _store_heads(ref, pair, value):
    first = pl.multiple_of(pair * 2 * HEAD, 2 * HEAD)
    rows = ref.shape[0]
    ref[:, pl.ds(first, HEAD)] = value[:rows].astype(ref.dtype)
    ref[:, pl.ds(first + HEAD, HEAD)] = value[rows:].astype(ref.dtype)


def _attend_kernel(table, *refs, cores, chunk, rows):
    pieces, refs = refs[:cores], refs[cores:]
    q_ref, at_ref, opens_ref, o_ref, l_ref, bias_ref, k_ref, v_ref = refs

    @pl.when(pl.program_id(0) == 0)
    def _():
        _place_keys(table, pieces, k_ref, v_ref, rows)
        v_ref[:, HEAD:] = jnp.ones((v_ref.shape[0], HEAD), BF)

    number = pl.program_id(0)
    for n in range(STEPS):

        @pl.when(number == n)
        def _(n=n):
            keys, masked = _spans(n, chunk)
            _mask_bias(at_ref, opens_ref, bias_ref, masked, keys)

            def pair_of_heads(pair, carry):
                query = _two_heads(q_ref, pair)
                out = None
                for low in range(0, keys, chunk):
                    s = times_transposed(query, k_ref[low : low + chunk, :])
                    if low >= masked:
                        s = s + bias_ref[:, low : low + chunk]
                    o = jnp.dot(
                        jnp.exp2(s).astype(BF),
                        v_ref[low : low + chunk, :],
                        preferred_element_type=F32,
                    )
                    out = o if out is None else out + o
                total = out[:, HEAD:]
                _store_heads(o_ref, pair, out[:, :HEAD] / total)
                log_total = jnp.log2(total)
                l_ref[2 * pair] = log_total[:rows]
                l_ref[2 * pair + 1] = log_total[rows:]
                return carry

            lax.fori_loop(0, q_ref.shape[1] // (2 * HEAD), pair_of_heads, 0, unroll=2)


def attend(table, queries, pieces, query_at, opens, rows):
    tokens, width = queries.shape
    heads, cores = width // HEAD, len(pieces)
    group = cores * tokens
    chunk = group // STEPS
    column = pl.BlockSpec((rows, 1), lambda i, o: (i, 0))
    tile = pl.BlockSpec((rows, width), lambda i, o: (i, 0))
    return run(
        partial(_attend_kernel, cores=cores, chunk=chunk, rows=rows),
        "attend",
        (STEPS,),
        (*pieces, queries, query_at, opens),
        [full(tokens, 2 * HEAD)] * cores + [tile, column, column],
        [((tokens, width), BF), ((heads, tokens, HEAD), F32)],
        [tile, pl.BlockSpec((heads, rows, HEAD), lambda i, o: (0, i, 0))],
        scalars=table,
        dear=True,
        scratch=[
            pltpu.VMEM((2 * rows, group), F32),
            pltpu.VMEM((group, HEAD), BF),
            pltpu.VMEM((group, 2 * HEAD), BF),
        ],
    )


def _beside(value, column):
    high = column.astype(BF)
    low = (column - high.astype(F32)).astype(BF)
    lane = lax.broadcasted_iota(jnp.int32, value.shape, 1)
    zero = jnp.zeros(value.shape, BF)
    extra = jnp.where(lane == 0, -high, jnp.where(lane == 1, -low, zero))
    return jnp.concatenate([value, extra], axis=1)


def _attend_back_kernel(table, *refs, cores, chunk, rows, first, count):
    pieces, refs = refs[:cores], refs[cores:]
    q_ref, do_ref, o_ref, l_ref, at_ref, opens_ref, dq_ref = refs[:7]
    sums, refs = refs[7 : 7 + cores], refs[7 + cores :]
    bias_ref, k_ref, v_ref, dk_ref, dv_ref = refs

    @pl.when(pl.program_id(0) == 0)
    def _():
        _place_keys(table, pieces, k_ref, v_ref, rows)
        ones = jnp.ones((k_ref.shape[0], HEAD), BF)
        k_ref[:, HEAD:] = ones
        v_ref[:, HEAD:] = ones
        dk_ref[...] = jnp.zeros_like(dk_ref)
        dv_ref[...] = jnp.zeros_like(dv_ref)

    number = first + pl.program_id(0)
    for n in range(first, first + count):

        @pl.when(number == n)
        def _(n=n):
            keys, masked = _spans(n, chunk)
            _mask_bias(at_ref, opens_ref, bias_ref, masked, keys)

            def pair_of_heads(pair, carry):
                query, grad = _two_heads(q_ref, pair), _two_heads(do_ref, pair)
                out = _two_heads(o_ref, pair)
                centre = jnp.sum(grad.astype(F32) * out.astype(F32), axis=-1, keepdims=True)
                log_total = jnp.concatenate([l_ref[2 * pair], l_ref[2 * pair + 1]])
                query_wide = _beside(query, log_total)
                grad_wide = _beside(grad, jnp.broadcast_to(centre, grad.shape))
                dq = None
                for low in range(0, keys, chunk):
                    span = slice(low, low + chunk)
                    s = times_transposed(query_wide, k_ref[span, :])
                    if low >= masked:
                        s = s + bias_ref[:, span]
                    p = jnp.exp2(s)
                    ds = (p * times_transposed(grad_wide, v_ref[span, :])).astype(BF)
                    dv_ref[span, :] += contract_rows(p.astype(BF), grad)
                    dk_ref[span, :] += contract_rows(ds, query)
                    part = jnp.dot(ds, k_ref[span, :HEAD], preferred_element_type=F32)
                    dq = part if dq is None else dq + part
                _store_heads(dq_ref, pair, dq)
                return carry

            lax.fori_loop(0, q_ref.shape[1] // (2 * HEAD), pair_of_heads, 0)

    @pl.when(number == first + count - 1)
    def _():
        for k, piece in enumerate(sums):
            for i in range(STEPS):
                place = pl.ds(pl.multiple_of(table[k * STEPS + i], rows), rows)
                piece[i * rows : (i + 1) * rows, :HEAD] = dk_ref[place, :] * (1.0 / LOG2E)
                piece[i * rows : (i + 1) * rows, HEAD:] = dv_ref[place, :]


def attend_back(table, queries, grads, mixed, log_totals, pieces, query_at, opens, rows, first, count):
    tokens, width = queries.shape
    heads, cores = width // HEAD, len(pieces)
    group = cores * tokens
    chunk = group // STEPS
    piece = full(tokens, 2 * HEAD)
    column = pl.BlockSpec((rows, 1), lambda i, o: (i + first, 0))
    tile = pl.BlockSpec((rows, width), lambda i, o: (i + first, 0))
    return run(
        partial(_attend_back_kernel, cores=cores, chunk=chunk, rows=rows, first=first, count=count),
        "attend_back",
        (count,),
        (*pieces, queries, grads, mixed, log_totals, query_at, opens),
        [piece] * cores
        + [tile, tile, tile, pl.BlockSpec((heads, rows, HEAD), lambda i, o: (0, i + first, 0))]
        + [column, column],
        [((count * rows, width), BF)] + [((tokens, 2 * HEAD), F32)] * cores,
        [pl.BlockSpec((rows, width), lambda i, o: (i, 0))] + [piece] * cores,
        scalars=table,
        dear=True,
        scratch=[
            pltpu.VMEM((2 * rows, group), F32),
            pltpu.VMEM((group, 2 * HEAD), BF),
            pltpu.VMEM((group, 2 * HEAD), BF),
            pltpu.VMEM((group, HEAD), F32),
            pltpu.VMEM((group, HEAD), F32),
        ],
    )


def _expert_kernel(
    x_ref, pulled_ref, chosen_ref, own_ref, router_ref, gate_ref, up_ref,
    dx_ref, dg_ref, du_ref, h_ref, c_ref,
):
    rows = x_ref[...]
    logits = jnp.dot(rows, router_ref[...], preferred_element_type=F32)
    chosen = chosen_ref[...].astype(F32)
    logits = jnp.where(chosen > 0.0, logits, -1e30)
    raised = jnp.exp(logits - jnp.max(logits, axis=-1, keepdims=True)) * chosen
    weight = jnp.sum(raised * own_ref[...], axis=-1, keepdims=True)
    weight = weight / jnp.maximum(jnp.sum(raised, axis=-1, keepdims=True), 1e-30)
    gate = jnp.dot(rows, gate_ref[...], preferred_element_type=F32)
    up = jnp.dot(rows, up_ref[...], preferred_element_type=F32)
    sigma = jax.nn.sigmoid(gate)
    swish = gate * sigma
    hidden = swish * up
    pulled = pulled_ref[...].astype(F32)
    c_ref[...] = jnp.sum(hidden * pulled, axis=-1, keepdims=True)
    h_ref[...] = (weight * hidden).astype(BF)
    pulled = weight * pulled
    gate_grad = (pulled * up * sigma * (1.0 + gate * (1.0 - sigma))).astype(BF)
    up_grad = (pulled * swish).astype(BF)
    dg_ref[...] = gate_grad
    du_ref[...] = up_grad
    dx = times_transposed(gate_grad, gate_ref[...]) + times_transposed(up_grad, up_ref[...])
    dx_ref[...] = dx.astype(BF)


def expert(rows, pulled, chosen, own, router, gate, up):
    count, width = rows.shape
    hidden = gate.shape[1]
    lanes = chosen.shape[1]
    step = min(count, 256)
    across = pl.BlockSpec((step, width), lambda i: (i, 0))
    thin = pl.BlockSpec((step, hidden), lambda i: (i, 0))
    column = pl.BlockSpec((step, 1), lambda i: (i, 0))
    return run(
        _expert_kernel,
        "expert",
        (count // step,),
        (rows, pulled, chosen, own, router, gate, up),
        [across, thin, pl.BlockSpec((step, lanes), lambda i: (i, 0)), full(1, lanes)]
        + [full(width, lanes), full(width, hidden), full(width, hidden)],
        [((count, width), BF)] + [((count, hidden), BF)] * 3 + [((count, 1), F32)],
        [across, thin, thin, thin, column],
        free=(0,),
        dear=True,
    )


def _rows_kernel(*refs):
    count = (len(refs) - 1) // 2
    total = None
    for left, right in zip(refs[:count], refs[count:-1]):
        part = contract_rows(left[...], right[...])
        total = part if total is None else total + part
    refs[-1][...] = total


def contract_chunks(lefts, rights):
    count, tall = lefts[0].shape
    wide = rights[0].shape[1]
    step = min(tall, 256)
    return run(
        _rows_kernel,
        "contract_chunks",
        (tall // step,),
        (*lefts, *rights),
        [pl.BlockSpec((count, step), lambda i: (0, i))] * len(lefts)
        + [full(count, wide)] * len(rights),
        [((tall, wide), F32)],
        [pl.BlockSpec((step, wide), lambda i: (i, 0))],
    )[0]


def body(
    layer_input,
    attn_gain,
    w_query,
    key_matrix,
    value_matrix,
    query_gain,
    key_gain,
    w_out,
    moe_gain,
    router,
    expert_gate,
    expert_up,
    expert_down,
    expert_ids,
    cont_segment,
    out_grad,
):
    tokens, width = layer_input.shape
    dps, _, cores = sizes = [lax.axis_size(a) for a in ALL]
    devices = math.prod(sizes)
    dp, z, c = [lax.axis_index(a) for a in ALL]
    experts = router.shape[1]
    capacity = tokens * TOP // experts
    plane = dps * cores
    slots = plane * capacity
    order = jnp.array(ORDER, jnp.int32)[z]
    where_block = jnp.array([[o.index(b) for b in range(STEPS)] for o in ORDER], jnp.int32)[z]
    own_heads = HQ // (STEPS * cores)
    heads = HQ // STEPS
    head_cols = heads * HEAD
    own_cols = own_heads * HEAD

    rows_dev = router.shape[0]
    id_cols = tokens * TOP // rows_dev
    router_pad = -(experts + 2 + id_cols) % 128
    small = jnp.concatenate(
        [
            router,
            attn_gain[:, None],
            moe_gain[:, None],
            expert_ids.astype(BF).reshape(rows_dev, id_cols),
            jnp.zeros((rows_dev, router_pad), BF),
        ],
        axis=1,
    )
    packed = pack(key_matrix, value_matrix, small)
    arrived = lax.all_gather(layer_input, "z", axis=0, tiled=True)
    query_own = from_dps(w_query, dp).reshape(width, own_cols)
    packed = exchange(packed, "z")
    packed, w_out, order, where_block = hold(packed, w_out, order, where_block)
    w_back = lax.all_to_all(w_out, "dp", split_axis=0, concat_axis=0, tiled=True)

    at_slot = jnp.arange(capacity, dtype=jnp.int32)
    earlier = (jnp.arange(tokens)[:, None] > jnp.arange(tokens)[None, :]).astype(BF)

    def plan(ids):
        chosen = jnp.any(ids[:, :, None] == jnp.arange(experts, dtype=jnp.int32), axis=1)
        ranks = jnp.dot(earlier, chosen.astype(BF), preferred_element_type=F32).astype(jnp.int32)
        ranks = jnp.where(chosen & (ranks < capacity), ranks, -1)
        in_plane = lax.dynamic_index_in_dim(
            ranks.reshape(tokens, dps, STEPS, cores), z, 2, keepdims=False
        ).reshape(tokens, plane)
        pick = (in_plane[:, :, None] == at_slot).reshape(tokens, slots).astype(BF)
        back = (in_plane.T[:, None, :] == at_slot[:, None]).reshape(slots, tokens).astype(BF)
        return chosen, ranks, pick, back

    def to_plane(rows):
        return lax.all_to_all(rows, PLANE, split_axis=0, concat_axis=0, tiled=True)

    zs = jnp.stack([z, jnp.int32(0)])
    own_chosen, own_ranks, own_pick, own_back = plan(expert_ids)
    own_slots = own_ranks[:, :, None] == at_slot
    first_id = 2 * HEAD + experts + 2
    ids = packed[:, :, first_id : first_id + id_cols].astype(jnp.int32)
    ids = ids.reshape(STEPS, tokens, TOP)
    ids = [lax.dynamic_index_in_dim(ids, order[i], 0, keepdims=False) for i in range(STEPS)]
    packed = jnp.stack(cores_in_order(packed, c), axis=1).reshape(w_query.shape[0], -1)
    packed = from_dps(packed, dp).reshape(width, -1)
    w_in = cores_in_order(query_own, c)
    *w_in, packed, ids, w_back = hold(*w_in, packed, ids, w_back)
    w_back = lax.all_to_all(w_back, "z", split_axis=0, concat_axis=0, tiled=True)
    w_back = lax.all_gather(w_back, PLANE, axis=0, tiled=True)
    rest = packed[:, 2 * HEAD :]
    lanes = rest.shape[1]
    router_all = rest[:, :experts]
    attn_gain_all = rest[:, experts].astype(F32)[None, :]
    moe_gain_all = rest[:, experts + 1].astype(F32)[None, :]
    w_in = jnp.concatenate([*w_in, packed[:, : 2 * HEAD]], axis=1)
    plans = [(own_chosen, own_ranks, own_pick, own_back)] + [plan(i) for i in ids[1:]]
    pick = [p[2] for p in plans]
    back = [p[3] for p in plans]
    slot_chosen = jnp.stack(
        [
            jnp.dot(back[i], jnp.pad(p[0].astype(BF), ((0, 0), (0, lanes - experts))))
            for i, p in enumerate(plans)
        ]
    ).reshape(STEPS, plane, capacity, lanes)
    slot_chosen = slot_chosen.transpose(1, 0, 2, 3)
    own_expert = dp * (STEPS * cores) + z * cores + c
    own_expert = (jnp.arange(lanes)[None, :] == own_expert).astype(F32)

    where_at, opens = group_layout(cont_segment[0])
    group = where_at.shape[0]

    def own_rows(table):
        mine = lax.dynamic_index_in_dim(table.reshape(STEPS, cores, tokens), c, 1, keepdims=False)
        return mine.reshape(-1)

    cosine, sine = angle_tables(own_rows(where_at), HEAD)
    query_at = own_rows(jnp.arange(group, dtype=jnp.int32))[:, None]
    opens = own_rows(opens)[:, None]
    numbers = jnp.arange(STEPS, dtype=jnp.int32)
    table = jnp.concatenate([(numbers * cores + (c + k) % cores) * tokens for k in range(cores)])
    query_gain_f = query_gain.astype(F32)[None, :]
    key_gain_f = key_gain.astype(F32)[None, :]
    scale = LOG2E / math.sqrt(HEAD)
    query_gain_s = query_gain_f * scale
    gate_w, up_w, down_w = expert_gate[0], expert_up[0], expert_down[0]
    at_block = [jnp.stack([z, order[i]]) for i in range(STEPS)]

    (
        upstream_block, w_in, pick, back, slot_chosen, cosine, sine, query_at, opens, table,
        query_gain_s, key_gain_f, at_block, own_expert, attn_gain_all, moe_gain_all, rest,
    ) = hold(
        out_grad, w_in, pick, back, slot_chosen, cosine, sine, query_at, opens, table,
        query_gain_s, key_gain_f, at_block, own_expert, attn_gain_all, moe_gain_all, rest,
    )
    g_up, g_down = spread_first(upstream_block)
    g0 = to_plane(dispatch(zs, back[0], [upstream_block], (0, 0, 0, 0)))
    normed, raw, queries, key_value_rows = project(
        arrived, attn_gain_all, w_in, cosine, sine, query_gain_s, key_gain_f, tokens
    )
    pieces = [key_value_rows, *other_cores(key_value_rows)]
    queries, g_up, g_down, *pieces = hold(queries, g_up, g_down, *pieces)
    g_up2, g_down2 = spread_second(g_up, g_down)
    g1 = to_plane(dispatch(zs, back[1], [g_up, g_down], FIRST))
    mixed, log_totals = attend(table, queries, pieces, query_at, opens, tokens)
    mixed, g_up2, g_down2 = hold(mixed, g_up2, g_down2)
    g_last = spread_third(g_up2, g_down2, z)
    w_back = w_back.reshape(dps, cores, STEPS, dps // STEPS, -1, width).transpose(3, 2, 1, 0, 4, 5)
    w_back = w_back.reshape(head_cols, width)
    attended = matmul(mixed, w_back, "nn", 4, "columns")
    attended, g_last, g0, g1, g_up2, g_down2 = hold(attended, g_last, g0, g1, g_up2, g_down2)
    attended = lax.psum_scatter(attended, "z", scatter_dimension=0, tiled=True)
    g2 = to_plane(dispatch(zs, back[2], [g_up, g_down, g_up2, g_down2], SECOND))
    pulled0 = matmul(g0, down_w, "nt", 2, "rows", F32)
    g2, g_last, pulled0 = hold(g2, g_last, pulled0)
    g3 = to_plane(dispatch(zs, back[3], [g_up2, g_down2, g_last], THIRD))
    pulled1 = matmul(g1, down_w, "nt", 2, "rows", F32)
    pulled2 = matmul(g2, down_w, "nt", 2, "rows", F32)
    g3, pulled1, pulled2, slot_chosen = hold(g3, pulled1, pulled2, slot_chosen)
    slot_chosen = to_plane(slot_chosen)
    slot_chosen = slot_chosen.transpose(1, 0, 2, 3).reshape(STEPS, slots, lanes)
    slot_chosen = [slot_chosen[i] for i in range(STEPS)]
    pulled3 = matmul(g3, down_w, "nt", 2, "rows", F32)
    attended, pulled3, slot_chosen = hold(attended, pulled3, slot_chosen)
    upstream_slots = [g0, g1, g2, g3]
    resid, moe_low = add_and_norm(layer_input, moe_gain_all, (attended,))

    def through(i, rows, pulled):
        return expert(rows, pulled, slot_chosen[i], own_expert, rest, gate_w, up_w)

    m_up, m_down = spread_first(moe_low)
    r0 = to_plane(dispatch(zs, back[0], [moe_low], (0, 0, 0, 0)))
    m_up, m_down = hold(m_up, m_down)
    m_up2, m_down2 = spread_second(m_up, m_down)
    r1 = dispatch(zs, back[1], [m_up, m_down], FIRST)
    r1, r0 = hold(r1, r0)
    r1 = to_plane(r1)
    e0 = through(0, r0, pulled0)
    m_up2, m_down2, e0 = hold(m_up2, m_down2, e0)
    m_last = spread_third(m_up2, m_down2, z)
    r2 = dispatch(zs, back[2], [m_up, m_down, m_up2, m_down2], SECOND)
    r2, r1 = hold(r2, r1)
    r2 = to_plane(r2)
    e1 = through(1, r1, pulled1)
    m_last, e1 = hold(m_last, e1)
    r3 = dispatch(zs, back[3], [m_up2, m_down2, m_last], THIRD)
    r3, r2 = hold(r3, r2)
    r3 = to_plane(r3)
    e2 = through(2, r2, pulled2)
    r3, e2 = hold(r3, e2)
    e3 = through(3, r3, pulled3)
    rows = [r0, r1, r2, r3]
    slot_grads, gate_grads, up_grads, hiddens, centres = [list(v) for v in zip(e0, e1, e2, e3)]
    d0, d1, d2, d3 = slot_grads
    b3 = to_plane(d3)
    moe_row, d2, centres, hiddens = hold(moe_low, d2, centres, hiddens)
    logits = jnp.dot(moe_row, router_all, preferred_element_type=F32)
    logits = jnp.where(own_chosen, logits, -jnp.inf)
    raised = jnp.exp(logits - jnp.max(logits, axis=-1, keepdims=True))
    gates = raised / jnp.sum(raised, axis=-1, keepdims=True)
    stacked = jnp.stack([v.reshape(dps, cores, capacity) for v in centres])
    centre_back = jnp.stack(
        [
            lax.dynamic_index_in_dim(stacked, where_block[b], 0, keepdims=False)
            for b in range(STEPS)
        ],
        axis=1,
    ).reshape(experts, capacity)
    h0, h1, h2, h3 = hiddens

    def produced(value):
        return matmul(value, down_w, "nn", 2, "columns", dear=True)

    p3 = produced(h3)
    b3, d2, p3, centre_back, gates, h0, h1, h2 = hold(
        b3, d2, p3, centre_back, gates, h0, h1, h2
    )
    b2 = to_plane(d2)
    (c3,) = line_part(zs, pick[3], b3, tokens)
    c3, h2 = hold(c3, h2)
    got = sum_first(c3)
    p2 = produced(h2)
    b2, d1, h1, p2 = hold(b2, d1, h1, p2)
    b1 = to_plane(d1)
    p1 = produced(h1)
    got, b2, p1 = hold(got, b2, p1)
    c2, middle = line_part(zs, pick[2], b2, tokens, 1, (c3, got))
    s_up, s_down = sum_second(middle)
    b1, d0, h0 = hold(b1, d0, h0)
    b0 = to_plane(d0)
    p0 = produced(h0)
    s_up, s_down, b1, p0 = hold(s_up, s_down, b1, p0)
    s_up, s_down = line_part(zs, pick[1], b1, tokens, 2, (c2, s_up, s_down))
    s_up, s_down = sum_third(s_up, s_down)
    b0, centre_back = hold(b0, centre_back)
    centre_back = lax.all_to_all(centre_back, ALL, split_axis=0, concat_axis=0, tiled=True)
    (c0,) = line_part(zs, pick[0], b0, tokens)
    weight_grad = jnp.sum(jnp.where(own_slots, centre_back[None], 0.0), axis=2)
    logit_grad = (
        gates * (weight_grad - jnp.sum(gates * weight_grad, axis=-1, keepdims=True))
    ).astype(BF)
    logit_wide = jnp.pad(logit_grad, ((0, 0), (0, lanes - experts)))
    s_up, s_down, c0, logit_wide = hold(s_up, s_down, c0, logit_wide)
    resid_grad, resid_low, moe_gain_grad = norm_back(
        resid, moe_gain_all, out_grad, (c0, s_up, s_down), logit_wide, rest
    )

    def by_core(value, axis):
        size = value.shape[axis] // cores
        return [
            lax.dynamic_slice_in_dim(value, (c + k) % cores * size, size, axis)
            for k in range(cores)
        ]

    resid_low, p3, logit_grad, hiddens, rows = hold(resid_low, p3, logit_grad, hiddens, rows)
    resid_all = lax.all_gather(resid_low, "z", axis=0, tiled=True)
    o3 = to_plane(p3)
    down_weight_grad = contract_chunks(hiddens, upstream_slots)
    router_grad = contract_rows(moe_low, logit_grad)
    o3, p2, rows, down_weight_grad, router_grad = hold(
        o3, p2, rows, down_weight_grad, router_grad
    )
    o2 = to_plane(p2)
    (o3,) = line_part(zs, pick[3], o3, tokens)
    up_weight_grad = contract_chunks(rows, up_grads)
    o2, p1, rows, up_weight_grad = hold(o2, p1, rows, up_weight_grad)
    o1 = to_plane(p1)
    gate_weight_grad = contract_chunks(rows, gate_grads)
    resid_all, o3, o2, gate_weight_grad = hold(resid_all, o3, o2, gate_weight_grad)
    t_got = sum_first(o3)
    mixed_grad = matmul(resid_all, w_back, "nt", 4, "rows", dear=True)
    mixed_grad, resid_all = hold(mixed_grad, resid_all)
    out_weight_grad = matmul(mixed, resid_all, "tn", 4, "columns")
    out_weight_grad = out_weight_grad.reshape(dps // STEPS, STEPS, cores, dps, -1, width)
    out_weight_grad = out_weight_grad.transpose(3, 2, 1, 0, 4, 5).reshape(head_cols, width)
    out_weight_grad, mixed_grad, t_got, o2, o3 = hold(out_weight_grad, mixed_grad, t_got, o2, o3)
    out_weight_grad = lax.psum_scatter(out_weight_grad, PLANE, scatter_dimension=0, tiled=True)
    o2, middle = line_part(zs, pick[2], o2, tokens, 1, (o3, t_got))
    middle, o2, mixed_grad = hold(middle, o2, mixed_grad)
    t_up, t_down = sum_second(middle)
    back = partial(attend_back, table, queries, mixed_grad, mixed, log_totals, pieces, query_at)
    near_grads, *near_sums = back(opens, tokens, 0, STEPS - 1)
    near_grads, t_up, t_down, o1, o2, mixed_grad = hold(
        near_grads, t_up, t_down, o1, o2, mixed_grad
    )
    t_up, t_down = line_part(zs, pick[1], o1, tokens, 2, (o2, t_up, t_down))
    t_up, t_down, mixed_grad = hold(t_up, t_down, mixed_grad)
    t_up, t_down = sum_third(t_up, t_down)
    last_grads, *last_sums = attend_back(
        table, queries, mixed_grad, mixed, log_totals, pieces, query_at, opens, tokens, STEPS - 1, 1
    )
    last_grads, out_weight_grad, *last_sums = hold(last_grads, out_weight_grad, *last_sums)
    own_sums, *other_sums = [a + b for a, b in zip(near_sums, last_sums)]
    sums = sum_over_cores([own_sums, *[v.astype(BF) for v in other_sums]])
    sums, t_up, t_down = hold(sums, t_up, t_down)
    normed_grad, raw_grad, query_gain_grad, key_gain_grad = project_back(
        raw, near_grads, last_grads, sums, w_in, cosine, sine, query_gain_f, key_gain_f, tokens
    )
    normed_grad, raw_grad, out_weight_grad, p0 = hold(normed_grad, raw_grad, out_weight_grad, p0)
    normed_sum = lax.psum_scatter(normed_grad, "z", scatter_dimension=0, tiled=True)
    o0 = to_plane(p0)
    in_grad = matmul(normed, raw_grad, "tn", 4, "rows")
    in_grad, o0 = hold(in_grad, o0)
    out_weight_grad = exchange(out_weight_grad.reshape(STEPS, -1, width), "z")
    query_share = sum_over_cores(by_core(in_grad[:, :head_cols], 1)).astype(BF)
    key_value_grad = in_grad[:, head_cols:].reshape(dps, STEPS, cores, rows_dev, 2 * HEAD)
    key_value_grad = sum_over_cores(
        [part[:, :, 0] for part in by_core(key_value_grad, 2)]
    ).astype(BF)
    attn_gain_grad = gain_sum(normed_grad, normed, attn_gain_all)

    def to_owners(value):
        columns = value.shape[0]
        split = value.reshape(columns, devices, rows_dev).transpose(1, 0, 2)
        return split.reshape(devices, columns * rows_dev)

    gain_row = jnp.concatenate([query_gain_grad, key_gain_grad], axis=1)
    late = jnp.concatenate(
        [
            to_owners(jnp.concatenate([router_grad.T, moe_gain_grad, attn_gain_grad])),
            jnp.broadcast_to(gain_row, (devices, 2 * HEAD)),
        ],
        axis=1,
    )
    query_share, key_value_grad, late, out_weight_grad, o0 = hold(
        query_share, key_value_grad, late, out_weight_grad, o0
    )
    late = lax.all_to_all(late, ALL, split_axis=0, concat_axis=0, tiled=True)
    query_weight_grad = over_dps(query_share.reshape(dps, -1, own_cols), dp)
    key_value_grad = over_dps(key_value_grad, dp).astype(BF)
    out_weight_grad = exchange(out_weight_grad.reshape(dps, -1, width), "dp")
    out_weight_grad = out_weight_grad.reshape(-1, width).astype(F32)
    (o0,) = line_part(zs, pick[0], o0, tokens)
    output = resid + (o0.astype(F32) + t_up.astype(F32) + t_down.astype(F32))
    output = output.astype(BF)
    late = jnp.sum(late, axis=0)
    gain_sums = late[-2 * HEAD :].reshape(2, HEAD)
    owned = late[: -2 * HEAD].reshape(experts + 2, rows_dev)
    key_value_grad = exchange(key_value_grad, "z")
    key_value_grad = key_value_grad.transpose(1, 0, 2).astype(F32)
    key_weight_grad = key_value_grad[:, :, :HEAD].reshape(rows_dev, -1)
    value_weight_grad = key_value_grad[:, :, HEAD:].reshape(rows_dev, -1)
    (input_grad,) = norm_back(layer_input, attn_gain_all, resid_grad, (normed_sum,))
    return (
        output,
        input_grad,
        owned[experts + 1],
        query_weight_grad,
        key_weight_grad,
        value_weight_grad,
        gain_sums[0],
        gain_sums[1],
        out_weight_grad,
        owned[experts],
        owned[:experts].T,
        gate_weight_grad[None],
        up_weight_grad[None],
        down_weight_grad[None],
    )


def solution(mesh):
    dps, sequence = mesh.devices.shape
    inner = Mesh(mesh.devices.reshape(dps, STEPS, sequence // STEPS), ALL)
    rows = P(ALL, None)
    placed = (
        rows,
        P(ALL),
        P("dp", ("z", "core")),
        rows,
        rows,
        P(),
        P(),
        rows,
        P(ALL),
        rows,
        P(ALL, None, None),
        P(ALL, None, None),
        P(ALL, None, None),
        rows,
        P("dp", None),
        rows,
    )
    return jax.shard_map(
        body,
        mesh=inner,
        in_specs=placed,
        out_specs=(
            rows,
            rows,
            P(ALL),
            P("dp", ("z", "core")),
            rows,
            rows,
            P(),
            P(),
            rows,
            P(ALL),
            rows,
            P(ALL, None, None),
            P(ALL, None, None),
            P(ALL, None, None),
        ),
        check_vma=False,
    )
```

```python
from functools import partial
import math

import jax
import jax.numpy as jnp
from jax import lax
from jax.experimental import pallas as pl
from jax.experimental.pallas import tpu as pltpu
from jax.sharding import Mesh, PartitionSpec as P

HQ = 32
KEY_VALUE_HEADS = 4
TOP = 8
PROMPT = 1024
NCONT = 4
HEAD = 128

EPS = 1e-06
THETA = 1000000.0
LOG2E = 1.4426950408889634
BF = jnp.bfloat16
F32 = jnp.float32

STEPS = 4
ORDER = ((0, 1, 2, 3), (1, 0, 2, 3), (2, 3, 1, 0), (3, 2, 1, 0))
PLANE = ("dp", "core")
ALL = ("dp", "z", "core")


def angle_tables(where_at, head_width):
    ranks = jnp.arange(head_width // 2, dtype=F32) * (2.0 / head_width)
    inverse = jnp.exp(-ranks * math.log(THETA))
    angles = where_at.astype(F32)[:, None] * inverse[None, :]
    cosine, sine = jnp.cos(angles), jnp.sin(angles)
    return (
        jnp.concatenate([cosine, cosine], axis=-1),
        jnp.concatenate([-sine, sine], axis=-1),
    )


def group_layout(segment):
    length = segment.shape[0]
    one_hot = (segment[:, None] == jnp.arange(NCONT, dtype=jnp.int32)[None, :]).astype(jnp.int32)
    counted = jnp.sum(one_hot, axis=0)
    before = jnp.arange(NCONT)[:, None] > jnp.arange(NCONT)[None, :]
    starts = jnp.sum(jnp.where(before, counted[None, :], 0), axis=1)
    begins = jnp.sum(one_hot * starts[None, :], axis=1)
    within = jnp.arange(length, dtype=jnp.int32) - begins
    where_at = jnp.concatenate([jnp.arange(PROMPT, dtype=jnp.int32), PROMPT + within])
    opens = jnp.concatenate([jnp.full((PROMPT,), PROMPT, jnp.int32), PROMPT + begins])
    return (where_at, opens)


def contract_rows(left, right):
    return lax.dot_general(left, right, (((0,), (0,)), ((), ())), preferred_element_type=F32)


def times_transposed(left, right):
    return lax.dot_general(left, right, (((1,), (1,)), ((), ())), preferred_element_type=F32)


def hold(*values):
    return lax.optimization_barrier(values)


def spread_first(block):
    return (
        lax.ppermute(block, "z", [(0, 1), (1, 2), (2, 3)]),
        lax.ppermute(block, "z", [(1, 0), (2, 1), (3, 2)]),
    )


def spread_second(up, down):
    return (
        lax.ppermute(up, "z", [(1, 2), (2, 3)]),
        lax.ppermute(down, "z", [(2, 1), (1, 0)]),
    )


def spread_third(up2, down2, z):
    return lax.ppermute(jnp.where(z == 2, up2, down2), "z", [(2, 3), (1, 0)])


FIRST = (1, 0, 1, 0)
SECOND = (3, 1, 0, 2)
THIRD = (2, 1, 0, 2)


def sum_first(third):
    return lax.ppermute(third, "z", [(0, 1), (3, 2)])


def sum_second(middle):
    return (
        lax.ppermute(middle, "z", [(0, 1), (1, 2)]),
        lax.ppermute(middle, "z", [(3, 2), (2, 1)]),
    )


def sum_third(up, down):
    return (
        lax.ppermute(up, "z", [(0, 1), (1, 2), (2, 3)]),
        lax.ppermute(down, "z", [(3, 2), (2, 1), (1, 0)]),
    )


def over_dps(value, dp):
    dps = value.shape[0]
    total = lax.dynamic_index_in_dim(value, dp, 0, keepdims=False).astype(F32)
    for k in range(1, dps):
        piece = lax.dynamic_index_in_dim(value, dp ^ k, 0, keepdims=False)
        total = total + lax.ppermute(piece, "dp", [(i, i ^ k) for i in range(dps)]).astype(F32)
    return total


def exchange(value, axis):
    size, me = value.shape[0], lax.axis_index(axis)
    own = lax.dynamic_index_in_dim(value, me, 0, keepdims=False)
    whole = lax.dynamic_update_index_in_dim(jnp.zeros_like(value), own, me, 0)
    for k in range(1, size):
        piece = lax.dynamic_index_in_dim(value, me ^ k, 0, keepdims=False)
        got = lax.ppermute(piece, axis, [(i, i ^ k) for i in range(size)])
        whole = lax.dynamic_update_index_in_dim(whole, got, me ^ k, 0)
    return whole


def from_dps(value, dp):
    dps = lax.axis_size("dp")
    whole = jnp.zeros((dps, *value.shape), value.dtype)
    whole = lax.dynamic_update_index_in_dim(whole, value, dp, 0)
    for k in range(1, dps):
        got = lax.ppermute(value, "dp", [(i, i ^ k) for i in range(dps)])
        whole = lax.dynamic_update_index_in_dim(whole, got, dp ^ k, 0)
    return whole


def other_cores(value):
    cores = lax.axis_size("core")
    return [
        lax.ppermute(value, "core", [((i + k) % cores, i) for i in range(cores)])
        for k in range(1, cores)
    ]


def cores_in_order(value, c):
    cores = lax.axis_size("core")
    pieces = [value, *other_cores(value)]
    ordered = []
    for n in range(cores):
        piece = pieces[0]
        for k in range(1, cores):
            piece = jnp.where((n - c) % cores == k, pieces[k], piece)
        ordered.append(piece)
    return ordered


def sum_over_cores(pieces):
    cores = lax.axis_size("core")
    total = pieces[0].astype(F32)
    for k in range(1, cores):
        got = lax.ppermute(pieces[k], "core", [(i, (i + k) % cores) for i in range(cores)])
        total = total + got.astype(F32)
    return total


CHEAP = pl.CostEstimate(flops=1, bytes_accessed=1, transcendentals=0)
DEAR = pl.CostEstimate(flops=10**11, bytes_accessed=1, transcendentals=0)


def run(kernel, name, grid, operands, in_specs, outs, out_specs, scalars=None, scratch=(), free=(), dear=False):
    prefetch = () if scalars is None else (scalars,)
    operands = [
        v if i in free else pltpu.with_memory_space_constraint(v, pltpu.HBM)
        for i, v in enumerate(operands)
    ]
    got = pl.pallas_call(
        kernel,
        grid_spec=pltpu.PrefetchScalarGridSpec(
            num_scalar_prefetch=len(prefetch),
            grid=grid,
            in_specs=in_specs,
            out_specs=out_specs,
            scratch_shapes=scratch,
        ),
        out_shape=[pltpu.HBM(shape, kind) for shape, kind in outs],
        compiler_params=pltpu.CompilerParams(vmem_limit_bytes=52 * 1024 * 1024),
        cost_estimate=DEAR if dear else CHEAP,
        name=name,
    )(*prefetch, *operands)
    return got


def full(*shape):
    return pl.BlockSpec(shape, lambda *_: (0,) * len(shape))


def _matmul_kernel(a_ref, b_ref, o_ref, *, dims):
    part = lax.dot_general(a_ref[...], b_ref[...], (dims, ((), ())), preferred_element_type=F32)
    o_ref[...] = part.astype(o_ref.dtype)


def matmul(a, b, kind, steps, by, out=BF, dear=False):
    dims = {"nn": ((1,), (0,)), "nt": ((1,), (1,)), "tn": ((0,), (0,))}[kind]
    rows = a.shape[1 - dims[0][0]]
    columns = b.shape[1 - dims[1][0]]
    a_spec, b_spec = full(*a.shape), full(*b.shape)
    if by == "rows":
        size = rows // steps
        if kind == "tn":
            a_spec = pl.BlockSpec((a.shape[0], size), lambda i: (0, i))
        else:
            a_spec = pl.BlockSpec((size, a.shape[1]), lambda i: (i, 0))
        o_spec = pl.BlockSpec((size, columns), lambda i: (i, 0))
    else:
        size = columns // steps
        if kind == "nt":
            b_spec = pl.BlockSpec((size, b.shape[1]), lambda i: (i, 0))
        else:
            b_spec = pl.BlockSpec((b.shape[0], size), lambda i: (0, i))
        o_spec = pl.BlockSpec((rows, size), lambda i: (0, i))
    return run(
        partial(_matmul_kernel, dims=dims),
        "matmul_" + kind,
        (steps,),
        (a, b),
        [a_spec, b_spec],
        [((rows, columns), out)],
        [o_spec],
        dear=dear,
    )[0]


def _dispatch_kernel(s_ref, pick_ref, *refs, sources):
    z, rows = s_ref[0], refs[0][...]
    for n in range(1, len(refs) - 1):
        here = False
        for at, source in enumerate(sources):
            if source == n:
                here = here | (z == at)
        rows = jnp.where(here, refs[n][...], rows)
    refs[-1][...] = jnp.dot(pick_ref[...], rows, preferred_element_type=F32).astype(BF)


def dispatch(scalars, pick, blocks, sources):
    slots, tokens = pick.shape
    width = blocks[0].shape[1]
    tile = pl.BlockSpec((tokens, 1024), lambda j, s: (0, j))
    return run(
        partial(_dispatch_kernel, sources=sources),
        "dispatch",
        (width // 1024,),
        (pick, *blocks),
        [full(slots, tokens)] + [tile] * len(blocks),
        [((slots, width), BF)],
        [pl.BlockSpec((slots, 1024), lambda j, s: (0, j))],
        scalars=scalars,
        free=(1, 2, 3, 4),
    )[0]


def _part_kernel(s_ref, a_ref, b_ref, *refs, step):
    z = s_ref[0]
    part = jnp.dot(a_ref[...], b_ref[...], preferred_element_type=F32)
    if step == 0:
        refs[0][...] = part.astype(BF)
    elif step == 1:
        third, got, part_ref, middle_ref = refs
        part_ref[...] = part.astype(BF)
        middle = jnp.where((z == 0) | (z == 3), part, third[...].astype(F32))
        middle_ref[...] = (middle + got[...].astype(F32)).astype(BF)
    else:
        second, up, down, up_ref, down_ref = refs
        other = second[...].astype(F32)
        up_ref[...] = (jnp.where(z == 1, other, part) + up[...].astype(F32)).astype(BF)
        down_ref[...] = (jnp.where(z == 2, other, part) + down[...].astype(F32)).astype(BF)


def line_part(scalars, a, b, tokens, step=0, more=()):
    width = b.shape[1]
    tile = pl.BlockSpec((tokens, 1024), lambda j, s: (0, j))
    return run(
        partial(_part_kernel, step=step),
        "line_part",
        (width // 1024,),
        (a, b, *more),
        [
            pl.BlockSpec((tokens, a.shape[1]), lambda j, s: (s[1], 0)),
            pl.BlockSpec((b.shape[0], 1024), lambda j, s: (0, j)),
        ]
        + [tile] * len(more),
        [((tokens, width), BF)] * (1 if step == 0 else 2),
        [tile] * (1 if step == 0 else 2),
        scalars=scalars,
        free=(1, 2, 3, 4),
    )


def _norm_kernel(x_ref, gain_ref, *refs):
    terms, (resid_ref, low_ref) = refs[:-2], refs[-2:]
    value = x_ref[...].astype(F32)
    for term in terms:
        value = value + term[...].astype(F32)
    resid_ref[...] = value
    factor = lax.rsqrt(jnp.mean(value * value, axis=-1, keepdims=True) + EPS)
    low_ref[...] = (value * factor * gain_ref[...]).astype(BF)


def add_and_norm(x, gain, terms):
    tokens, width = x.shape
    step = min(tokens, 128)
    tile = pl.BlockSpec((step, width), lambda i: (i, 0))
    return run(
        _norm_kernel,
        "add_and_norm",
        (tokens // step,),
        (x, gain, *terms),
        [tile, full(1, width)] + [tile] * len(terms),
        [((tokens, width), F32), ((tokens, width), BF)],
        [tile, tile],
    )


def _norm_back_kernel(v_ref, gain_ref, above_ref, *refs, logits):
    if logits:
        logit_ref, router_ref, *terms, total_ref, low_ref, gain_grad_ref = refs
    else:
        *terms, total_ref = refs
    grad = sum([term[...].astype(F32) for term in terms])
    if logits:
        grad = grad + times_transposed(logit_ref[...], router_ref[...])
    value = v_ref[...].astype(F32)
    factor = lax.rsqrt(jnp.mean(value * value, axis=-1, keepdims=True) + EPS)
    unit = value * factor
    if logits:

        @pl.when(pl.program_id(0) == 0)
        def _():
            gain_grad_ref[...] = jnp.zeros_like(gain_grad_ref)

        gain_grad_ref[...] += jnp.sum(grad * unit, axis=0, keepdims=True)
    grad = grad * gain_ref[...]
    shift = jnp.mean(grad * unit, axis=-1, keepdims=True)
    total = above_ref[...].astype(F32) + factor * (grad - unit * shift)
    total_ref[...] = total
    if logits:
        low_ref[...] = total.astype(BF)


def norm_back(value, gain, above, terms, logit_grad=None, router=None):
    tokens, width = value.shape
    step = min(tokens, 128)
    tile = pl.BlockSpec((step, width), lambda i: (i, 0))
    operands, specs = [value, gain, above], [tile, full(1, width), tile]
    outs, out_specs = [((tokens, width), F32)], [tile]
    if logit_grad is not None:
        lanes = logit_grad.shape[1]
        operands += [logit_grad, router]
        specs += [pl.BlockSpec((step, lanes), lambda i: (i, 0)), full(width, lanes)]
        outs += [((tokens, width), BF), ((1, width), F32)]
        out_specs += [tile, full(1, width)]
    return run(
        partial(_norm_back_kernel, logits=logit_grad is not None),
        "norm_back",
        (tokens // step,),
        (*operands, *terms),
        specs + [tile] * len(terms),
        outs,
        out_specs,
    )


def _pack_kernel(key_ref, value_ref, small_ref, out_ref):
    for at in range(STEPS):
        cols = slice(at * HEAD, (at + 1) * HEAD)
        out_ref[at, :, :HEAD] = key_ref[:, cols]
        out_ref[at, :, HEAD : 2 * HEAD] = value_ref[:, cols]
        out_ref[at, :, 2 * HEAD :] = small_ref[...]


def pack(key, value, small):
    rows = small.shape[0]
    lanes = 2 * HEAD + small.shape[1]
    return run(
        _pack_kernel,
        "pack",
        (1,),
        (key, value, small),
        [full(*key.shape), full(*value.shape), full(*small.shape)],
        [((STEPS, rows, lanes), BF)],
        [full(STEPS, rows, lanes)],
    )[0]


def _gain_kernel(grad_ref, value_ref, gain_ref, out_ref):
    @pl.when(pl.program_id(0) == 0)
    def _():
        out_ref[...] = jnp.zeros_like(out_ref)

    product = grad_ref[...].astype(F32) * value_ref[...].astype(F32)
    out_ref[...] += jnp.sum(product, axis=0, keepdims=True)

    @pl.when(pl.program_id(0) == pl.num_programs(0) - 1)
    def _():
        out_ref[...] = out_ref[...] / gain_ref[...]


def gain_sum(grad, value, gain):
    tokens, width = grad.shape
    tile = pl.BlockSpec((tokens // STEPS, width), lambda i: (i, 0))
    return run(
        _gain_kernel,
        "gain_sum",
        (STEPS,),
        (grad, value, gain),
        [tile, tile, full(1, width)],
        [((1, width), F32)],
        [full(1, width)],
    )[0]


def _lane_mean(value):
    ones = jnp.full((HEAD, HEAD), 1.0 / HEAD, BF)
    return jnp.dot(value.astype(BF), ones, preferred_element_type=F32)


def _project_kernel(
    x_ref, gain_ref, w_ref, cos_ref, sin_ref, qg_ref, kg_ref, n_ref, raw_ref, q_ref, kv_ref
):
    x = x_ref[...].astype(F32)
    factor = lax.rsqrt(jnp.mean(x * x, axis=-1, keepdims=True) + EPS)
    normed = (x * factor * gain_ref[...]).astype(BF)
    n_ref[...] = normed
    raw_ref[...] = jnp.dot(normed, w_ref[...], preferred_element_type=F32)
    cosine, sine = cos_ref[...], sin_ref[...]
    heads = q_ref.shape[1] // HEAD
    for h in range(heads + 1):
        cols = slice(h * HEAD, (h + 1) * HEAD)
        value = raw_ref[:, cols]
        factor = lax.rsqrt(_lane_mean(value * value) + EPS)
        value = value * factor * (qg_ref[...] if h < heads else kg_ref[...])
        value = (value * cosine + pltpu.roll(value, HEAD // 2, 1) * sine).astype(BF)
        if h < heads:
            q_ref[:, cols] = value
        else:
            kv_ref[:, :HEAD] = value
    kv_ref[:, HEAD:] = raw_ref[:, (heads + 1) * HEAD :].astype(BF)


def project(x, gain, w_in, cosine, sine, query_gain, key_gain, rows):
    tokens, width = x.shape
    columns = w_in.shape[1]

    def tile(size):
        return pl.BlockSpec((rows, size), lambda i: (i, 0))

    return run(
        _project_kernel,
        "project",
        (tokens // rows,),
        (x, gain, w_in, cosine, sine, query_gain, key_gain),
        [tile(width), full(1, width), full(width, columns), tile(HEAD), tile(HEAD)]
        + [full(1, HEAD)] * 2,
        [
            ((tokens, width), BF),
            ((tokens, columns), F32),
            ((tokens, columns - 2 * HEAD), BF),
            ((tokens, 2 * HEAD), BF),
        ],
        [tile(width), tile(columns), tile(columns - 2 * HEAD), tile(2 * HEAD)],
        dear=True,
    )


def _project_back_kernel(
    raw_ref, near_ref, last_ref, dkv_ref, w_ref, cos_ref, sin_ref, qg_ref, kg_ref,
    ng_ref, rg_ref, dqg_ref, dkg_ref,
):
    @pl.when(pl.program_id(0) == 0)
    def _():
        dqg_ref[...] = jnp.zeros_like(dqg_ref)
        dkg_ref[...] = jnp.zeros_like(dkg_ref)

    cosine, sine = cos_ref[...], sin_ref[...]
    heads = near_ref.shape[1] // HEAD
    at_last = pl.program_id(0) == STEPS - 1
    for h in range(heads + 1):
        cols = slice(h * HEAD, (h + 1) * HEAD)
        value = raw_ref[:, cols]
        factor = lax.rsqrt(_lane_mean(value * value) + EPS)
        unit = value * factor
        if h < heads:
            grad = jnp.where(at_last, last_ref[:, cols], near_ref[:, cols]).astype(F32) * (1.0 / math.sqrt(HEAD))
        else:
            grad = dkv_ref[:, :HEAD]
        grad = grad * cosine + pltpu.roll(grad * sine, HEAD // 2, 1)
        gain_grad = jnp.sum(grad * unit, axis=0, keepdims=True)
        if h < heads:
            dqg_ref[...] += gain_grad
            grad = grad * qg_ref[...]
        else:
            dkg_ref[...] += gain_grad
            grad = grad * kg_ref[...]
        shift = _lane_mean(grad * unit)
        rg_ref[:, cols] = (factor * (grad - unit * shift)).astype(BF)
    rg_ref[:, (heads + 1) * HEAD :] = dkv_ref[:, HEAD:].astype(BF)
    ng_ref[...] = times_transposed(rg_ref[...], w_ref[...]).astype(BF)


def project_back(raw, near, last, key_value_grads, w_in, cosine, sine, query_gain, key_gain, rows):
    tokens, columns = raw.shape
    width = w_in.shape[0]

    def tile(size):
        return pl.BlockSpec((rows, size), lambda i: (i, 0))

    return run(
        _project_back_kernel,
        "project_back",
        (tokens // rows,),
        (raw, near, last, key_value_grads, w_in, cosine, sine, query_gain, key_gain),
        [
            tile(columns),
            pl.BlockSpec((rows, columns - 2 * HEAD), lambda i: (jnp.minimum(i, STEPS - 2), 0)),
            full(rows, columns - 2 * HEAD),
            tile(2 * HEAD),
            full(width, columns),
            tile(HEAD),
            tile(HEAD),
            full(1, HEAD),
            full(1, HEAD),
        ],
        [((tokens, width), BF), ((tokens, columns), BF), ((1, HEAD), F32), ((1, HEAD), F32)],
        [tile(width), tile(columns), full(1, HEAD), full(1, HEAD)],
        dear=True,
    )


def _mask_bias(at_ref, opens_ref, bias_ref, low, high):
    rows = at_ref.shape[0]
    key_at = low + lax.broadcasted_iota(jnp.int32, (rows, high - low), 1)
    query_at = at_ref[...]
    allowed = (key_at <= query_at) & ((key_at < PROMPT) | (key_at >= opens_ref[...]))
    bias = jnp.where(allowed, 0.0, -1e30).astype(F32)
    bias_ref[:rows, low:high] = bias
    bias_ref[rows:, low:high] = bias


def _spans(number, chunk):
    return (number + 1) * chunk, min(number * chunk, PROMPT)


def _place_keys(table, pieces, k_ref, v_ref, rows):
    for k, piece in enumerate(pieces):
        for i in range(STEPS):
            place = pl.ds(pl.multiple_of(table[k * STEPS + i], rows), rows)
            k_ref[place, :HEAD] = piece[i * rows : (i + 1) * rows, :HEAD]
            v_ref[place, :HEAD] = piece[i * rows : (i + 1) * rows, HEAD:]


def _two_heads(ref, pair):
    first = pl.multiple_of(pair * 2 * HEAD, 2 * HEAD)
    return jnp.concatenate([ref[:, pl.ds(first, HEAD)], ref[:, pl.ds(first + HEAD, HEAD)]])


def _store_heads(ref, pair, value):
    first = pl.multiple_of(pair * 2 * HEAD, 2 * HEAD)
    rows = ref.shape[0]
    ref[:, pl.ds(first, HEAD)] = value[:rows].astype(ref.dtype)
    ref[:, pl.ds(first + HEAD, HEAD)] = value[rows:].astype(ref.dtype)


def _attend_kernel(table, *refs, cores, chunk, rows):
    pieces, refs = refs[:cores], refs[cores:]
    q_ref, at_ref, opens_ref, o_ref, l_ref, bias_ref, k_ref, v_ref = refs

    @pl.when(pl.program_id(0) == 0)
    def _():
        _place_keys(table, pieces, k_ref, v_ref, rows)
        v_ref[:, HEAD:] = jnp.ones((v_ref.shape[0], HEAD), BF)

    number = pl.program_id(0)
    for n in range(STEPS):

        @pl.when(number == n)
        def _(n=n):
            keys, masked = _spans(n, chunk)
            _mask_bias(at_ref, opens_ref, bias_ref, masked, keys)

            def pair_of_heads(pair, carry):
                query = _two_heads(q_ref, pair)
                out = None
                for low in range(0, keys, chunk):
                    s = times_transposed(query, k_ref[low : low + chunk, :])
                    if low >= masked:
                        s = s + bias_ref[:, low : low + chunk]
                    o = jnp.dot(
                        jnp.exp2(s).astype(BF),
                        v_ref[low : low + chunk, :],
                        preferred_element_type=F32,
                    )
                    out = o if out is None else out + o
                total = out[:, HEAD:]
                _store_heads(o_ref, pair, out[:, :HEAD] / total)
                log_total = jnp.log2(total)
                l_ref[2 * pair] = log_total[:rows]
                l_ref[2 * pair + 1] = log_total[rows:]
                return carry

            lax.fori_loop(0, q_ref.shape[1] // (2 * HEAD), pair_of_heads, 0, unroll=2)


def attend(table, queries, pieces, query_at, opens, rows):
    tokens, width = queries.shape
    heads, cores = width // HEAD, len(pieces)
    group = cores * tokens
    chunk = group // STEPS
    column = pl.BlockSpec((rows, 1), lambda i, o: (i, 0))
    tile = pl.BlockSpec((rows, width), lambda i, o: (i, 0))
    return run(
        partial(_attend_kernel, cores=cores, chunk=chunk, rows=rows),
        "attend",
        (STEPS,),
        (*pieces, queries, query_at, opens),
        [full(tokens, 2 * HEAD)] * cores + [tile, column, column],
        [((tokens, width), BF), ((heads, tokens, HEAD), F32)],
        [tile, pl.BlockSpec((heads, rows, HEAD), lambda i, o: (0, i, 0))],
        scalars=table,
        dear=True,
        scratch=[
            pltpu.VMEM((2 * rows, group), F32),
            pltpu.VMEM((group, HEAD), BF),
            pltpu.VMEM((group, 2 * HEAD), BF),
        ],
    )


def _beside(value, column):
    high = column.astype(BF)
    low = (column - high.astype(F32)).astype(BF)
    lane = lax.broadcasted_iota(jnp.int32, value.shape, 1)
    zero = jnp.zeros(value.shape, BF)
    extra = jnp.where(lane == 0, -high, jnp.where(lane == 1, -low, zero))
    return jnp.concatenate([value, extra], axis=1)


def _attend_back_kernel(table, *refs, cores, chunk, rows, first, count):
    pieces, refs = refs[:cores], refs[cores:]
    q_ref, do_ref, o_ref, l_ref, at_ref, opens_ref, dq_ref = refs[:7]
    sums, refs = refs[7 : 7 + cores], refs[7 + cores :]
    bias_ref, k_ref, v_ref, dk_ref, dv_ref = refs

    @pl.when(pl.program_id(0) == 0)
    def _():
        _place_keys(table, pieces, k_ref, v_ref, rows)
        ones = jnp.ones((k_ref.shape[0], HEAD), BF)
        k_ref[:, HEAD:] = ones
        v_ref[:, HEAD:] = ones
        dk_ref[...] = jnp.zeros_like(dk_ref)
        dv_ref[...] = jnp.zeros_like(dv_ref)

    number = first + pl.program_id(0)
    for n in range(first, first + count):

        @pl.when(number == n)
        def _(n=n):
            keys, masked = _spans(n, chunk)
            _mask_bias(at_ref, opens_ref, bias_ref, masked, keys)

            def pair_of_heads(pair, carry):
                query, grad = _two_heads(q_ref, pair), _two_heads(do_ref, pair)
                out = _two_heads(o_ref, pair)
                centre = jnp.sum(grad.astype(F32) * out.astype(F32), axis=-1, keepdims=True)
                log_total = jnp.concatenate([l_ref[2 * pair], l_ref[2 * pair + 1]])
                query_wide = _beside(query, log_total)
                grad_wide = _beside(grad, jnp.broadcast_to(centre, grad.shape))
                dq = None
                for low in range(0, keys, chunk):
                    span = slice(low, low + chunk)
                    s = times_transposed(query_wide, k_ref[span, :])
                    if low >= masked:
                        s = s + bias_ref[:, span]
                    p = jnp.exp2(s)
                    ds = (p * times_transposed(grad_wide, v_ref[span, :])).astype(BF)
                    dv_ref[span, :] += contract_rows(p.astype(BF), grad)
                    dk_ref[span, :] += contract_rows(ds, query)
                    part = jnp.dot(ds, k_ref[span, :HEAD], preferred_element_type=F32)
                    dq = part if dq is None else dq + part
                _store_heads(dq_ref, pair, dq)
                return carry

            lax.fori_loop(0, q_ref.shape[1] // (2 * HEAD), pair_of_heads, 0)

    @pl.when(number == first + count - 1)
    def _():
        for k, piece in enumerate(sums):
            for i in range(STEPS):
                place = pl.ds(pl.multiple_of(table[k * STEPS + i], rows), rows)
                piece[i * rows : (i + 1) * rows, :HEAD] = dk_ref[place, :] * (1.0 / LOG2E)
                piece[i * rows : (i + 1) * rows, HEAD:] = dv_ref[place, :]


def attend_back(table, queries, grads, mixed, log_totals, pieces, query_at, opens, rows, first, count):
    tokens, width = queries.shape
    heads, cores = width // HEAD, len(pieces)
    group = cores * tokens
    chunk = group // STEPS
    piece = full(tokens, 2 * HEAD)
    column = pl.BlockSpec((rows, 1), lambda i, o: (i + first, 0))
    tile = pl.BlockSpec((rows, width), lambda i, o: (i + first, 0))
    return run(
        partial(_attend_back_kernel, cores=cores, chunk=chunk, rows=rows, first=first, count=count),
        "attend_back",
        (count,),
        (*pieces, queries, grads, mixed, log_totals, query_at, opens),
        [piece] * cores
        + [tile, tile, tile, pl.BlockSpec((heads, rows, HEAD), lambda i, o: (0, i + first, 0))]
        + [column, column],
        [((count * rows, width), BF)] + [((tokens, 2 * HEAD), F32)] * cores,
        [pl.BlockSpec((rows, width), lambda i, o: (i, 0))] + [piece] * cores,
        scalars=table,
        dear=True,
        scratch=[
            pltpu.VMEM((2 * rows, group), F32),
            pltpu.VMEM((group, 2 * HEAD), BF),
            pltpu.VMEM((group, 2 * HEAD), BF),
            pltpu.VMEM((group, HEAD), F32),
            pltpu.VMEM((group, HEAD), F32),
        ],
    )


def _expert_kernel(
    x_ref, pulled_ref, chosen_ref, own_ref, router_ref, gate_ref, up_ref,
    dx_ref, dg_ref, du_ref, h_ref, c_ref,
):
    rows = x_ref[...]
    logits = jnp.dot(rows, router_ref[...], preferred_element_type=F32)
    chosen = chosen_ref[...].astype(F32)
    logits = jnp.where(chosen > 0.0, logits, -1e30)
    raised = jnp.exp(logits - jnp.max(logits, axis=-1, keepdims=True)) * chosen
    weight = jnp.sum(raised * own_ref[...], axis=-1, keepdims=True)
    weight = weight / jnp.maximum(jnp.sum(raised, axis=-1, keepdims=True), 1e-30)
    gate = jnp.dot(rows, gate_ref[...], preferred_element_type=F32)
    up = jnp.dot(rows, up_ref[...], preferred_element_type=F32)
    sigma = jax.nn.sigmoid(gate)
    swish = gate * sigma
    hidden = swish * up
    pulled = pulled_ref[...].astype(F32)
    c_ref[...] = jnp.sum(hidden * pulled, axis=-1, keepdims=True)
    h_ref[...] = (weight * hidden).astype(BF)
    pulled = weight * pulled
    gate_grad = (pulled * up * sigma * (1.0 + gate * (1.0 - sigma))).astype(BF)
    up_grad = (pulled * swish).astype(BF)
    dg_ref[...] = gate_grad
    du_ref[...] = up_grad
    dx = times_transposed(gate_grad, gate_ref[...]) + times_transposed(up_grad, up_ref[...])
    dx_ref[...] = dx.astype(BF)


def expert(rows, pulled, chosen, own, router, gate, up):
    count, width = rows.shape
    hidden = gate.shape[1]
    lanes = chosen.shape[1]
    step = min(count, 256)
    across = pl.BlockSpec((step, width), lambda i: (i, 0))
    thin = pl.BlockSpec((step, hidden), lambda i: (i, 0))
    column = pl.BlockSpec((step, 1), lambda i: (i, 0))
    return run(
        _expert_kernel,
        "expert",
        (count // step,),
        (rows, pulled, chosen, own, router, gate, up),
        [across, thin, pl.BlockSpec((step, lanes), lambda i: (i, 0)), full(1, lanes)]
        + [full(width, lanes), full(width, hidden), full(width, hidden)],
        [((count, width), BF)] + [((count, hidden), BF)] * 3 + [((count, 1), F32)],
        [across, thin, thin, thin, column],
        free=(0,),
        dear=True,
    )


def _rows_kernel(*refs):
    count = (len(refs) - 1) // 2
    total = None
    for left, right in zip(refs[:count], refs[count:-1]):
        part = contract_rows(left[...], right[...])
        total = part if total is None else total + part
    refs[-1][...] = total


def contract_chunks(lefts, rights):
    count, tall = lefts[0].shape
    wide = rights[0].shape[1]
    step = min(tall, 256)
    return run(
        _rows_kernel,
        "contract_chunks",
        (tall // step,),
        (*lefts, *rights),
        [pl.BlockSpec((count, step), lambda i: (0, i))] * len(lefts)
        + [full(count, wide)] * len(rights),
        [((tall, wide), F32)],
        [pl.BlockSpec((step, wide), lambda i: (i, 0))],
    )[0]


def body(
    layer_input,
    attn_gain,
    w_query,
    key_matrix,
    value_matrix,
    query_gain,
    key_gain,
    w_out,
    moe_gain,
    router,
    expert_gate,
    expert_up,
    expert_down,
    expert_ids,
    cont_segment,
    out_grad,
):
    tokens, width = layer_input.shape
    dps, _, cores = sizes = [lax.axis_size(a) for a in ALL]
    devices = math.prod(sizes)
    dp, z, c = [lax.axis_index(a) for a in ALL]
    experts = router.shape[1]
    capacity = tokens * TOP // experts
    plane = dps * cores
    slots = plane * capacity
    order = jnp.array(ORDER, jnp.int32)[z]
    where_block = jnp.array([[o.index(b) for b in range(STEPS)] for o in ORDER], jnp.int32)[z]
    own_heads = HQ // (STEPS * cores)
    heads = HQ // STEPS
    head_cols = heads * HEAD
    own_cols = own_heads * HEAD

    rows_dev = router.shape[0]
    id_cols = tokens * TOP // rows_dev
    router_pad = -(experts + 2 + id_cols) % 128
    small = jnp.concatenate(
        [
            router,
            attn_gain[:, None],
            moe_gain[:, None],
            expert_ids.astype(BF).reshape(rows_dev, id_cols),
            jnp.zeros((rows_dev, router_pad), BF),
        ],
        axis=1,
    )
    packed = pack(key_matrix, value_matrix, small)
    arrived = lax.all_gather(layer_input, "z", axis=0, tiled=True)
    query_own = from_dps(w_query, dp).reshape(width, own_cols)
    packed = exchange(packed, "z")
    packed, w_out, order, where_block = hold(packed, w_out, order, where_block)
    w_back = lax.all_to_all(w_out, "dp", split_axis=0, concat_axis=0, tiled=True)

    at_slot = jnp.arange(capacity, dtype=jnp.int32)
    earlier = (jnp.arange(tokens)[:, None] > jnp.arange(tokens)[None, :]).astype(BF)

    def plan(ids):
        chosen = jnp.any(ids[:, :, None] == jnp.arange(experts, dtype=jnp.int32), axis=1)
        ranks = jnp.dot(earlier, chosen.astype(BF), preferred_element_type=F32).astype(jnp.int32)
        ranks = jnp.where(chosen & (ranks < capacity), ranks, -1)
        in_plane = lax.dynamic_index_in_dim(
            ranks.reshape(tokens, dps, STEPS, cores), z, 2, keepdims=False
        ).reshape(tokens, plane)
        pick = (in_plane[:, :, None] == at_slot).reshape(tokens, slots).astype(BF)
        back = (in_plane.T[:, None, :] == at_slot[:, None]).reshape(slots, tokens).astype(BF)
        return chosen, ranks, pick, back

    def to_plane(rows):
        return lax.all_to_all(rows, PLANE, split_axis=0, concat_axis=0, tiled=True)

    zs = jnp.stack([z, jnp.int32(0)])
    own_chosen, own_ranks, own_pick, own_back = plan(expert_ids)
    own_slots = own_ranks[:, :, None] == at_slot
    first_id = 2 * HEAD + experts + 2
    ids = packed[:, :, first_id : first_id + id_cols].astype(jnp.int32)
    ids = ids.reshape(STEPS, tokens, TOP)
    ids = [lax.dynamic_index_in_dim(ids, order[i], 0, keepdims=False) for i in range(STEPS)]
    packed = jnp.stack(cores_in_order(packed, c), axis=1).reshape(w_query.shape[0], -1)
    packed = from_dps(packed, dp).reshape(width, -1)
    w_in = cores_in_order(query_own, c)
    *w_in, packed, ids, w_back = hold(*w_in, packed, ids, w_back)
    w_back = lax.all_to_all(w_back, "z", split_axis=0, concat_axis=0, tiled=True)
    w_back = lax.all_gather(w_back, PLANE, axis=0, tiled=True)
    rest = packed[:, 2 * HEAD :]
    lanes = rest.shape[1]
    router_all = rest[:, :experts]
    attn_gain_all = rest[:, experts].astype(F32)[None, :]
    moe_gain_all = rest[:, experts + 1].astype(F32)[None, :]
    w_in = jnp.concatenate([*w_in, packed[:, : 2 * HEAD]], axis=1)
    plans = [(own_chosen, own_ranks, own_pick, own_back)] + [plan(i) for i in ids[1:]]
    pick = [p[2] for p in plans]
    back = [p[3] for p in plans]
    slot_chosen = jnp.stack(
        [
            jnp.dot(back[i], jnp.pad(p[0].astype(BF), ((0, 0), (0, lanes - experts))))
            for i, p in enumerate(plans)
        ]
    ).reshape(STEPS, plane, capacity, lanes)
    slot_chosen = slot_chosen.transpose(1, 0, 2, 3)
    own_expert = dp * (STEPS * cores) + z * cores + c
    own_expert = (jnp.arange(lanes)[None, :] == own_expert).astype(F32)

    where_at, opens = group_layout(cont_segment[0])
    group = where_at.shape[0]

    def own_rows(table):
        mine = lax.dynamic_index_in_dim(table.reshape(STEPS, cores, tokens), c, 1, keepdims=False)
        return mine.reshape(-1)

    cosine, sine = angle_tables(own_rows(where_at), HEAD)
    query_at = own_rows(jnp.arange(group, dtype=jnp.int32))[:, None]
    opens = own_rows(opens)[:, None]
    numbers = jnp.arange(STEPS, dtype=jnp.int32)
    table = jnp.concatenate([(numbers * cores + (c + k) % cores) * tokens for k in range(cores)])
    query_gain_f = query_gain.astype(F32)[None, :]
    key_gain_f = key_gain.astype(F32)[None, :]
    scale = LOG2E / math.sqrt(HEAD)
    query_gain_s = query_gain_f * scale
    gate_w, up_w, down_w = expert_gate[0], expert_up[0], expert_down[0]
    at_block = [jnp.stack([z, order[i]]) for i in range(STEPS)]

    (
        upstream_block, w_in, pick, back, slot_chosen, cosine, sine, query_at, opens, table,
        query_gain_s, key_gain_f, at_block, own_expert, attn_gain_all, moe_gain_all, rest,
    ) = hold(
        out_grad, w_in, pick, back, slot_chosen, cosine, sine, query_at, opens, table,
        query_gain_s, key_gain_f, at_block, own_expert, attn_gain_all, moe_gain_all, rest,
    )
    g_up, g_down = spread_first(upstream_block)
    g0 = to_plane(dispatch(zs, back[0], [upstream_block], (0, 0, 0, 0)))
    normed, raw, queries, key_value_rows = project(
        arrived, attn_gain_all, w_in, cosine, sine, query_gain_s, key_gain_f, tokens
    )
    pieces = [key_value_rows, *other_cores(key_value_rows)]
    queries, g_up, g_down, *pieces = hold(queries, g_up, g_down, *pieces)
    g_up2, g_down2 = spread_second(g_up, g_down)
    g1 = to_plane(dispatch(zs, back[1], [g_up, g_down], FIRST))
    mixed, log_totals = attend(table, queries, pieces, query_at, opens, tokens)
    mixed, g_up2, g_down2 = hold(mixed, g_up2, g_down2)
    g_last = spread_third(g_up2, g_down2, z)
    w_back = w_back.reshape(dps, cores, STEPS, dps // STEPS, -1, width).transpose(3, 2, 1, 0, 4, 5)
    w_back = w_back.reshape(head_cols, width)
    attended = matmul(mixed, w_back, "nn", 4, "columns")
    attended, g_last, g0, g1, g_up2, g_down2 = hold(attended, g_last, g0, g1, g_up2, g_down2)
    attended = lax.psum_scatter(attended, "z", scatter_dimension=0, tiled=True)
    g2 = to_plane(dispatch(zs, back[2], [g_up, g_down, g_up2, g_down2], SECOND))
    pulled0 = matmul(g0, down_w, "nt", 2, "rows", F32)
    g2, g_last, pulled0 = hold(g2, g_last, pulled0)
    g3 = to_plane(dispatch(zs, back[3], [g_up2, g_down2, g_last], THIRD))
    pulled1 = matmul(g1, down_w, "nt", 2, "rows", F32)
    pulled2 = matmul(g2, down_w, "nt", 2, "rows", F32)
    g3, pulled1, pulled2, slot_chosen = hold(g3, pulled1, pulled2, slot_chosen)
    slot_chosen = to_plane(slot_chosen)
    slot_chosen = slot_chosen.transpose(1, 0, 2, 3).reshape(STEPS, slots, lanes)
    slot_chosen = [slot_chosen[i] for i in range(STEPS)]
    pulled3 = matmul(g3, down_w, "nt", 2, "rows", F32)
    attended, pulled3, slot_chosen = hold(attended, pulled3, slot_chosen)
    upstream_slots = [g0, g1, g2, g3]
    resid, moe_low = add_and_norm(layer_input, moe_gain_all, (attended,))

    def through(i, rows, pulled):
        return expert(rows, pulled, slot_chosen[i], own_expert, rest, gate_w, up_w)

    m_up, m_down = spread_first(moe_low)
    r0 = to_plane(dispatch(zs, back[0], [moe_low], (0, 0, 0, 0)))
    m_up, m_down = hold(m_up, m_down)
    m_up2, m_down2 = spread_second(m_up, m_down)
    r1 = dispatch(zs, back[1], [m_up, m_down], FIRST)
    r1, r0 = hold(r1, r0)
    r1 = to_plane(r1)
    e0 = through(0, r0, pulled0)
    m_up2, m_down2, e0 = hold(m_up2, m_down2, e0)
    m_last = spread_third(m_up2, m_down2, z)
    r2 = dispatch(zs, back[2], [m_up, m_down, m_up2, m_down2], SECOND)
    r2, r1 = hold(r2, r1)
    r2 = to_plane(r2)
    e1 = through(1, r1, pulled1)
    m_last, e1 = hold(m_last, e1)
    r3 = dispatch(zs, back[3], [m_up2, m_down2, m_last], THIRD)
    r3, r2 = hold(r3, r2)
    r3 = to_plane(r3)
    e2 = through(2, r2, pulled2)
    r3, e2 = hold(r3, e2)
    e3 = through(3, r3, pulled3)
    rows = [r0, r1, r2, r3]
    slot_grads, gate_grads, up_grads, hiddens, centres = [list(v) for v in zip(e0, e1, e2, e3)]
    d0, d1, d2, d3 = slot_grads
    b3 = to_plane(d3)
    moe_row, d2, centres, hiddens = hold(moe_low, d2, centres, hiddens)
    logits = jnp.dot(moe_row, router_all, preferred_element_type=F32)
    logits = jnp.where(own_chosen, logits, -jnp.inf)
    raised = jnp.exp(logits - jnp.max(logits, axis=-1, keepdims=True))
    gates = raised / jnp.sum(raised, axis=-1, keepdims=True)
    stacked = jnp.stack([v.reshape(dps, cores, capacity) for v in centres])
    centre_back = jnp.stack(
        [
            lax.dynamic_index_in_dim(stacked, where_block[b], 0, keepdims=False)
            for b in range(STEPS)
        ],
        axis=1,
    ).reshape(experts, capacity)
    h0, h1, h2, h3 = hiddens

    def produced(value):
        return matmul(value, down_w, "nn", 2, "columns", dear=True)

    p3 = produced(h3)
    b3, d2, p3, centre_back, gates, h0, h1, h2 = hold(
        b3, d2, p3, centre_back, gates, h0, h1, h2
    )
    b2 = to_plane(d2)
    (c3,) = line_part(zs, pick[3], b3, tokens)
    c3, h2 = hold(c3, h2)
    got = sum_first(c3)
    p2 = produced(h2)
    b2, d1, h1, p2 = hold(b2, d1, h1, p2)
    b1 = to_plane(d1)
    p1 = produced(h1)
    got, b2, p1 = hold(got, b2, p1)
    c2, middle = line_part(zs, pick[2], b2, tokens, 1, (c3, got))
    s_up, s_down = sum_second(middle)
    b1, d0, h0 = hold(b1, d0, h0)
    b0 = to_plane(d0)
    p0 = produced(h0)
    s_up, s_down, b1, p0 = hold(s_up, s_down, b1, p0)
    s_up, s_down = line_part(zs, pick[1], b1, tokens, 2, (c2, s_up, s_down))
    s_up, s_down = sum_third(s_up, s_down)
    b0, centre_back = hold(b0, centre_back)
    centre_back = lax.all_to_all(centre_back, ALL, split_axis=0, concat_axis=0, tiled=True)
    (c0,) = line_part(zs, pick[0], b0, tokens)
    weight_grad = jnp.sum(jnp.where(own_slots, centre_back[None], 0.0), axis=2)
    logit_grad = (
        gates * (weight_grad - jnp.sum(gates * weight_grad, axis=-1, keepdims=True))
    ).astype(BF)
    logit_wide = jnp.pad(logit_grad, ((0, 0), (0, lanes - experts)))
    s_up, s_down, c0, logit_wide = hold(s_up, s_down, c0, logit_wide)
    resid_grad, resid_low, moe_gain_grad = norm_back(
        resid, moe_gain_all, out_grad, (c0, s_up, s_down), logit_wide, rest
    )

    def by_core(value, axis):
        size = value.shape[axis] // cores
        return [
            lax.dynamic_slice_in_dim(value, (c + k) % cores * size, size, axis)
            for k in range(cores)
        ]

    resid_low, p3, logit_grad, hiddens, rows = hold(resid_low, p3, logit_grad, hiddens, rows)
    resid_all = lax.all_gather(resid_low, "z", axis=0, tiled=True)
    o3 = to_plane(p3)
    down_weight_grad = contract_chunks(hiddens, upstream_slots)
    router_grad = contract_rows(moe_low, logit_grad)
    o3, p2, rows, down_weight_grad, router_grad = hold(
        o3, p2, rows, down_weight_grad, router_grad
    )
    o2 = to_plane(p2)
    (o3,) = line_part(zs, pick[3], o3, tokens)
    up_weight_grad = contract_chunks(rows, up_grads)
    o2, p1, rows, up_weight_grad = hold(o2, p1, rows, up_weight_grad)
    o1 = to_plane(p1)
    gate_weight_grad = contract_chunks(rows, gate_grads)
    resid_all, o3, o2, gate_weight_grad = hold(resid_all, o3, o2, gate_weight_grad)
    t_got = sum_first(o3)
    mixed_grad = matmul(resid_all, w_back, "nt", 4, "rows", dear=True)
    mixed_grad, resid_all = hold(mixed_grad, resid_all)
    out_weight_grad = matmul(mixed, resid_all, "tn", 4, "columns")
    out_weight_grad = out_weight_grad.reshape(dps // STEPS, STEPS, cores, dps, -1, width)
    out_weight_grad = out_weight_grad.transpose(3, 2, 1, 0, 4, 5).reshape(head_cols, width)
    out_weight_grad, mixed_grad, t_got, o2, o3 = hold(out_weight_grad, mixed_grad, t_got, o2, o3)
    out_weight_grad = lax.psum_scatter(out_weight_grad, PLANE, scatter_dimension=0, tiled=True)
    o2, middle = line_part(zs, pick[2], o2, tokens, 1, (o3, t_got))
    middle, o2, mixed_grad = hold(middle, o2, mixed_grad)
    t_up, t_down = sum_second(middle)
    back = partial(attend_back, table, queries, mixed_grad, mixed, log_totals, pieces, query_at)
    near_grads, *near_sums = back(opens, tokens, 0, STEPS - 1)
    near_grads, t_up, t_down, o1, o2, mixed_grad = hold(
        near_grads, t_up, t_down, o1, o2, mixed_grad
    )
    t_up, t_down = line_part(zs, pick[1], o1, tokens, 2, (o2, t_up, t_down))
    t_up, t_down, mixed_grad = hold(t_up, t_down, mixed_grad)
    t_up, t_down = sum_third(t_up, t_down)
    last_grads, *last_sums = attend_back(
        table, queries, mixed_grad, mixed, log_totals, pieces, query_at, opens, tokens, STEPS - 1, 1
    )
    last_grads, out_weight_grad, *last_sums = hold(last_grads, out_weight_grad, *last_sums)
    own_sums, *other_sums = [a + b for a, b in zip(near_sums, last_sums)]
    sums = sum_over_cores([own_sums, *[v.astype(BF) for v in other_sums]])
    sums, t_up, t_down = hold(sums, t_up, t_down)
    normed_grad, raw_grad, query_gain_grad, key_gain_grad = project_back(
        raw, near_grads, last_grads, sums, w_in, cosine, sine, query_gain_f, key_gain_f, tokens
    )
    normed_grad, raw_grad, out_weight_grad, p0 = hold(normed_grad, raw_grad, out_weight_grad, p0)
    normed_sum = lax.psum_scatter(normed_grad, "z", scatter_dimension=0, tiled=True)
    o0 = to_plane(p0)
    in_grad = matmul(normed, raw_grad, "tn", 4, "rows")
    in_grad, o0 = hold(in_grad, o0)
    out_weight_grad = exchange(out_weight_grad.reshape(STEPS, -1, width), "z")
    query_share = sum_over_cores(by_core(in_grad[:, :head_cols], 1)).astype(BF)
    key_value_grad = in_grad[:, head_cols:].reshape(dps, STEPS, cores, rows_dev, 2 * HEAD)
    key_value_grad = sum_over_cores(
        [part[:, :, 0] for part in by_core(key_value_grad, 2)]
    ).astype(BF)
    attn_gain_grad = gain_sum(normed_grad, normed, attn_gain_all)

    def to_owners(value):
        columns = value.shape[0]
        split = value.reshape(columns, devices, rows_dev).transpose(1, 0, 2)
        return split.reshape(devices, columns * rows_dev)

    gain_row = jnp.concatenate([query_gain_grad, key_gain_grad], axis=1)
    late = jnp.concatenate(
        [
            to_owners(jnp.concatenate([router_grad.T, moe_gain_grad, attn_gain_grad])),
            jnp.broadcast_to(gain_row, (devices, 2 * HEAD)),
        ],
        axis=1,
    )
    query_share, key_value_grad, late, out_weight_grad, o0 = hold(
        query_share, key_value_grad, late, out_weight_grad, o0
    )
    late = lax.all_to_all(late, ALL, split_axis=0, concat_axis=0, tiled=True)
    query_weight_grad = over_dps(query_share.reshape(dps, -1, own_cols), dp)
    key_value_grad = over_dps(key_value_grad, dp).astype(BF)
    out_weight_grad = exchange(out_weight_grad.reshape(dps, -1, width), "dp")
    out_weight_grad = out_weight_grad.reshape(-1, width).astype(F32)
    (o0,) = line_part(zs, pick[0], o0, tokens)
    output = resid + (o0.astype(F32) + t_up.astype(F32) + t_down.astype(F32))
    output = output.astype(BF)
    late = jnp.sum(late, axis=0)
    gain_sums = late[-2 * HEAD :].reshape(2, HEAD)
    owned = late[: -2 * HEAD].reshape(experts + 2, rows_dev)
    key_value_grad = exchange(key_value_grad, "z")
    key_value_grad = key_value_grad.transpose(1, 0, 2).astype(F32)
    key_weight_grad = key_value_grad[:, :, :HEAD].reshape(rows_dev, -1)
    value_weight_grad = key_value_grad[:, :, HEAD:].reshape(rows_dev, -1)
    (input_grad,) = norm_back(layer_input, attn_gain_all, resid_grad, (normed_sum,))
    return (
        output,
        input_grad,
        owned[experts + 1],
        query_weight_grad,
        key_weight_grad,
        value_weight_grad,
        gain_sums[0],
        gain_sums[1],
        out_weight_grad,
        owned[experts],
        owned[:experts].T,
        gate_weight_grad[None],
        up_weight_grad[None],
        down_weight_grad[None],
    )


def solution(mesh):
    dps, sequence = mesh.devices.shape
    inner = Mesh(mesh.devices.reshape(dps, STEPS, sequence // STEPS), ALL)
    rows = P(ALL, None)
    placed = (
        rows,
        P(ALL),
        P("dp", ("z", "core")),
        rows,
        rows,
        P(),
        P(),
        rows,
        P(ALL),
        rows,
        P(ALL, None, None),
        P(ALL, None, None),
        P(ALL, None, None),
        rows,
        P("dp", None),
        rows,
    )
    return jax.shard_map(
        body,
        mesh=inner,
        in_specs=placed,
        out_specs=(
            rows,
            rows,
            P(ALL),
            P("dp", ("z", "core")),
            rows,
            rows,
            P(),
            P(),
            rows,
            P(ALL),
            rows,
            P(ALL, None, None),
            P(ALL, None, None),
            P(ALL, None, None),
        ),
        check_vma=False,
    )
```
